32 devices in a mesh: dp: 2 (over x), ctx: 4 (over y, core), exp: 4 (over z).
Axes of the slice: x: 2, y: 2, z: 4, core: 2. Of those that a mesh axis runs over, the one named last changes fastest.
Arguments:
- hidden_in: float32 [8, 1024, 1536], P(('dp', 'exp'), 'ctx'), may hold values from -6 to 6
- lengths: int32 [8, 3], P(('dp', 'exp')), may hold values from 1 to 512, 1024 in all within a row
- order: int32 [8, 1024], P(('dp', 'exp')), may hold values from 0 to 1023, each once within a row
- routes: int32 [8, 1024, 4], P(('dp', 'exp'), 'ctx'), may hold values from 0 to 7, all different within a row; in each aligned block of 256 rows (0 to 255, 256 to 511, ..., all dimensions but the last counted through in order) at most 192 rows name the same one
- cotangent: float32 [8, 1024, 1536], P(('dp', 'exp'), 'ctx'), may hold values from -6 to 6
- attn_gain: bfloat16 [1536], P(('dp', 'ctx', 'exp')), may hold values from 0.5 to 1.5
- qkv_weight: bfloat16 [1536, 2048], P(('dp', 'ctx', 'exp')), may hold values from -0.15625 to 0.15625
- out_weight: bfloat16 [1536, 1536], P(None, ('dp', 'ctx', 'exp')), may hold values from -0.875 to 0.875
- ffn_gain: bfloat16 [1536], P(('dp', 'ctx', 'exp')), may hold values from 0.5 to 1.5
- router_weight: bfloat16 [1536, 8], P(('dp', 'ctx', 'exp')), may hold values from -0.078125 to 0.078125
- gate_up_weight: bfloat16 [8, 1536, 1536], P('exp', ('dp', 'ctx')), may hold values from -0.15625 to 0.15625
- down_weight: bfloat16 [8, 768, 1536], P('exp', ('dp', 'ctx')), may hold values from -0.21875 to 0.21875
Outputs:
- output: float32 [8, 1024, 1536], P(('dp', 'exp'), 'ctx')
- grad_input: float32 [8, 1024, 1536], P(('dp', 'exp'), 'ctx')
- grad_attn_gain: float32 [1536], P(('dp', 'ctx', 'exp'))
- grad_qkv: float32 [1536, 2048], P(('dp', 'ctx', 'exp'))
- grad_out_proj: float32 [1536, 1536], P(None, ('dp', 'ctx', 'exp'))
- grad_ffn_gain: float32 [1536], P(('dp', 'ctx', 'exp'))
- grad_router: float32 [1536, 8], P(('dp', 'ctx', 'exp'))
- grad_gate_up: float32 [8, 1536, 1536], P('exp', ('dp', 'ctx'))
- grad_down: float32 [8, 768, 1536], P('exp', ('dp', 'ctx'))
The draws below stay inside these ranges and needn't reach their ends.
Inputs may be any that keep to these rules, and one draw needn't show every extreme that they name: Each row holds the lengths of 3 documents that fill the group's 1024 positions; the longest is exactly 512. `order`: each row is a permutation of the group's packed positions. `routes`: each token names 4 different experts; among the 256 tokens of one device (aligned blocks of rows in the order of the first two dimensions) no expert is named more than 192 times, a bound that some block reaches.
All inputs are finite; a program needn't handle non-finite values.
Results may differ from the reference program's by a relative error of at most 0.029.
Values may be sent and summed in bfloat16 or wider, within the bound.
No kernel may reach another device: no remote copies, remote signals or barrier semaphores. Data moves between devices by JAX's collectives and lax.ppermute only.
A program may use at most 192 MiB of HBM per device.

```python
import math
import jax
import jax.numpy as jnp
import numpy as np
from jax import lax

D = 1536
QUERY_HEADS = 12
KEY_VALUE_HEADS = 2
HEAD_SIZE = 128
FFE = 768
TOP = 4
NSEQ = 3
TOK_DEV = 256
EXPERTS = 8
QW = 1536
QKV = 2048
GTOK = 1024
SEQB = 8
SEQ_MAX = 512
CAP = 192


def level_of(stream_key, extent, cuts, low, top_value):
    def one(position, blocks):
        heights = jax.random.uniform(jax.random.fold_in(jax.random.fold_in(stream_key, 6), position), (blocks,), jnp.float32, low / len(cuts), top_value / len(cuts))
        return jnp.repeat(jnp.exp(heights), extent[position] // blocks).reshape((-1,) + (1,) * (len(extent) - position - 1))

    level = one(*cuts[0])
    for cut in cuts[1:]:
        level = level * one(*cut)
    return level


def length_profile(count, total, bound, lean):
    portions = [(1 << 20) // math.isqrt(standing ** lean) + 1 for standing in range(2, count + 1)]
    rest, holding = total - bound - (count - 1), [1] * (count - 1)
    while rest > 0:
        candidates = [i for i in range(count - 1) if holding[i] < bound]
        mass, remaining = sum([portions[i] for i in candidates]), rest
        for i in candidates:
            more = min(bound - holding[i], max(1, remaining * portions[i] // mass), rest)
            holding[i] = holding[i] + more
            rest = rest - more
    return np.array([bound] + holding)


def ragged(key, number_of, total, reach, skew):
    if number_of == 2:
        one = jax.random.randint(key, (), max(1, total - reach), min(reach, total - 1) + 1)
        return jnp.stack([one, total - one])
    sizes = jnp.asarray(length_profile(number_of, total, reach, skew), jnp.int32)
    twos = (number_of - 1) // 2
    donor, sink = sizes[1:1 + 2 * twos:2], sizes[2:2 + 2 * twos:2]
    margin = jnp.minimum(donor - 1, reach - sink)
    passed = jax.random.randint(jax.random.fold_in(key, 1), (twos,), 0, 1 << 20) % (margin + 1)
    sizes = sizes.at[1:1 + 2 * twos:2].set(donor - passed).at[2:2 + 2 * twos:2].set(sink + passed)
    return sizes[jax.random.permutation(jax.random.fold_in(key, 2), number_of)]


def assign_block(own_key, own, number, rows, count, top, reach, lean):
    sequence = jax.random.permutation(own_key, count)
    crowded, usual = shares(count, rows * top, reach, lean, True), shares(count, rows * top, reach, lean, False)
    places = jnp.arange(count)

    def named(sizes, turn):
        used = int((sizes > 0).sum())
        fixed = max(1, used // 4)
        moved = fixed + (places - fixed + turn * (used - fixed)) % max(1, count - fixed)
        return jnp.zeros((count,), jnp.int32).at[sequence[jnp.where(places < fixed, places, moved)]].set(jnp.asarray(sizes, jnp.int32))

    sizes = jnp.where(number % 4 == 0, named(crowded, number // 4), named(usual, number - number // 4 - 1))
    mixed = jax.random.permutation(jax.random.fold_in(own, 3), count)
    donor, sink = mixed[0:count // 2 * 2:2], mixed[1:count // 2 * 2:2]
    slack = jnp.minimum(sizes[donor] - 1, reach - sizes[sink]) // 2
    slack = jnp.where((donor == sequence[0]) | (sink == sequence[0]) | (sizes[sink] == 0), 0, jnp.maximum(slack, 0))
    moved = jax.random.randint(jax.random.fold_in(own, 4), (count // 2,), 0, 1 << 20) % (slack + 1)
    sizes = sizes.at[donor].add(-moved).at[sink].add(moved)
    items = jnp.searchsorted(jnp.cumsum(sizes), jnp.arange(rows * top), side="right").astype(jnp.int32)
    table = items.reshape(top, rows).T
    table = table[jax.random.permutation(jax.random.fold_in(own, 1), rows)]
    turn = jax.random.randint(jax.random.fold_in(own, 2), (rows, 1), 0, top)
    return jnp.take_along_axis(table, (jnp.arange(top)[None, :] + turn) % top, axis=1)


def shares(number_of, total, bound, slope, full):
    portions = [(1 << 20) // math.isqrt(rank ** slope) + 1 for rank in range(1, number_of + 1)]
    largest = bound if full else min(bound, max(-(-total // number_of), total * portions[0] // sum(portions)))
    least = 1 if total - largest >= number_of - 1 else 0
    holding, spare = [largest] + [least] * (number_of - 1), total - largest - least * (number_of - 1)
    while spare > 0:
        candidates = [i for i in range(1, number_of) if holding[i] < largest] or [i for i in range(1, number_of) if holding[i] < bound]
        pool, left = sum([portions[i] for i in candidates]), spare
        for i in candidates:
            more = min(bound - holding[i], max(1, left * portions[i] // pool), spare)
            holding[i] = holding[i] + more
            spare = spare - more
    return np.array(holding)


def gaussian(own_key, dims, scale, reach, shards=(), kind=jnp.bfloat16):
    array = jax.random.normal(own_key, dims, jnp.float32) * scale
    if len(shards) > 0:
        array = level_of(own_key, dims, shards, -0.22, 0.18) * array
    return jnp.clip(array, min=-reach, max=reach).astype(kind)


def setup_inputs(seed: int = 0) -> dict:
    streams_of = jax.random.split(jax.random.key(seed), 13)
    hidden_in = gaussian(streams_of[0], (SEQB, GTOK, D), 1.0, 6.0, ((0, 8), (1, 4)), jnp.float32)
    lengths = jax.vmap(lambda own: ragged(own, NSEQ, GTOK, SEQ_MAX, 2))(jax.random.split(streams_of[1], SEQB)).reshape((SEQB, NSEQ)).astype(jnp.int32)
    order = jax.vmap(lambda own: jax.random.permutation(own, GTOK))(jax.random.split(streams_of[2], SEQB)).reshape((SEQB, GTOK)).astype(jnp.int32)
    routes_keys = jax.random.split(jax.random.fold_in(streams_of[3], 1), SEQB * GTOK // TOK_DEV)
    routes_turns = jax.random.permutation(jax.random.fold_in(streams_of[3], 3), SEQB * GTOK // TOK_DEV)
    routes = jax.vmap(lambda own, number: assign_block(jax.random.fold_in(streams_of[3], 2), own, number, TOK_DEV, EXPERTS, TOP, CAP, 1))(routes_keys, routes_turns).reshape((SEQB, GTOK, TOP))
    cotangent = gaussian(streams_of[4], (SEQB, GTOK, D), 1.0, 6.0, ((0, 8), (1, 4)), jnp.float32)
    attn_gain = jnp.clip(1.0 + 0.1 * jax.random.normal(streams_of[5], (D,), jnp.float32), 0.5, 1.5).astype(jnp.bfloat16)
    qkv_weight = gaussian(streams_of[6], (D, QKV), D ** -0.5, 0.15625, ((0, 32),))
    out_weight = gaussian(streams_of[7], (QW, D), (QW // 32) ** -0.5, 0.875, ((1, 32),))
    ffn_gain = jnp.clip(1.0 + 0.1 * jax.random.normal(streams_of[8], (D,), jnp.float32), 0.5, 1.5).astype(jnp.bfloat16)
    router_weight = gaussian(streams_of[9], (D, EXPERTS), (4 * D) ** -0.5, 0.078125, ((0, 32),))
    gate_up_weight = gaussian(streams_of[10], (EXPERTS, D, 2 * FFE), D ** -0.5, 0.15625, ((0, 4), (1, 8)))
    down_weight = gaussian(streams_of[11], (EXPERTS, FFE, D), FFE ** -0.5, 0.21875, ((0, 4), (1, 8)))
    return dict(hidden_in=hidden_in, lengths=lengths, order=order, routes=routes, cotangent=cotangent, attn_gain=attn_gain, qkv_weight=qkv_weight, out_weight=out_weight, ffn_gain=ffn_gain, router_weight=router_weight, gate_up_weight=gate_up_weight, down_weight=down_weight)


EPS = 1e-06
BASE = 1000000.0
HIGH = lax.Precision.HIGHEST

@jax.custom_vjp
def lower_bound(v):
    return lax.optimization_barrier(v.astype(jnp.bfloat16)).astype(jnp.float32)

@jax.custom_vjp
def low_back(v):
    return v

def low_keep(v):
    return (lower_bound(v), None)

def low_pass(kept, grad):
    return (grad,)

def back_keep(v):
    return (v, None)

def back_low(kept, grad):
    return (lower_bound(grad),)
lower_bound.defvjp(low_keep, low_pass)
low_back.defvjp(back_keep, back_low)

def norm_rows(v, gain):
    return v * lax.rsqrt(lax.optimization_barrier(jnp.mean(v * v, axis=-1, keepdims=True)) + EPS) * gain

def apply_rotation(t, slot_position, sign):
    half = t.shape[-1] // 2
    freq = jnp.exp(jnp.arange(half, dtype=jnp.float32) * (-2.0 * math.log(BASE) / t.shape[-1]))
    angle = slot_position.astype(jnp.float32)[:, None] * freq[None, :]
    cosine = jnp.cos(angle)[:, None, :]
    sine = sign * jnp.sin(angle)[:, None, :]
    first = t[..., :half]
    second = t[..., half:]
    return jnp.concatenate([first * cosine - second * sine, second * cosine + first * sine], axis=-1)

def place_docs(packed, lengths):
    ends = jnp.cumsum(lengths).astype(jnp.int32)
    before = packed[:, None] >= ends[None, :]
    docs = lax.optimization_barrier(jnp.sum(before.astype(jnp.int32), axis=1)).astype(jnp.int32)
    starts = lax.optimization_barrier(jnp.max(jnp.where(before, ends[None, :], 0), axis=1)).astype(jnp.int32)
    return (docs, packed - starts)

def attend_group(query_rows, key_rows, value_rows, packed, docs):
    overall_row_count = query_rows.shape[0]
    block = min(512, overall_row_count)
    scale = query_rows.shape[-1] ** (-0.5)

    def one_block(index):
        start = index * block
        qpart = lax.dynamic_slice_in_dim(query_rows, start, block, 0)
        qpos = lax.dynamic_slice_in_dim(packed, start, block, 0)
        qdoc = lax.dynamic_slice_in_dim(docs, start, block, 0)
        scores = low_back(jnp.einsum('qhgd,khd->hgqk', qpart, key_rows, precision=HIGH) * scale)
        allowed = (qdoc[:, None] == docs[None, :]) & (packed[None, :] <= qpos[:, None])
        scores = jnp.where(allowed, scores, -1e+30)
        upper_bound = lax.optimization_barrier(jnp.max(scores, axis=-1, keepdims=True))
        weights = jnp.exp(scores - upper_bound)
        probs = weights / lax.optimization_barrier(jnp.sum(weights, axis=-1, keepdims=True))
        out = jnp.einsum('hgqk,khd->qhgd', lower_bound(probs), value_rows, precision=HIGH)
        return out.reshape(block, -1)
    parts = lax.map(jax.checkpoint(one_block), jnp.arange(overall_row_count // block, dtype=jnp.int32))
    return parts.reshape(overall_row_count, -1)

def forward(hidden_in, attn_gain, qkv_weight, out_weight, ffn_gain, router_weight, gate_up_weight, down_weight, lengths, order, routes):
    query_groups, overall_row_count, width = hidden_in.shape
    query_width = QUERY_HEADS * HEAD_SIZE
    key_value_width = KEY_VALUE_HEADS * HEAD_SIZE
    normed = lower_bound(norm_rows(hidden_in, attn_gain))
    projected_output = low_back(jnp.einsum('srd,de->sre', normed, qkv_weight, precision=HIGH))

    def one_group(pieces):
        projection_weight, lens, packed = pieces
        docs, slot_position = place_docs(packed, lens)
        query_rows = lower_bound(apply_rotation(projection_weight[:, :query_width].reshape(overall_row_count, QUERY_HEADS, HEAD_SIZE), slot_position, 1.0)).reshape(overall_row_count, KEY_VALUE_HEADS, QUERY_HEADS // KEY_VALUE_HEADS, HEAD_SIZE)
        key_rows = lower_bound(apply_rotation(projection_weight[:, query_width:query_width + key_value_width].reshape(overall_row_count, KEY_VALUE_HEADS, HEAD_SIZE), slot_position, 1.0))
        value_rows = lower_bound(projection_weight[:, query_width + key_value_width:].reshape(overall_row_count, KEY_VALUE_HEADS, HEAD_SIZE))
        return attend_group(query_rows, key_rows, value_rows, packed, docs)
    attended = lax.map(one_group, (projected_output, lengths, order))
    mixed = lower_bound(low_back(attended))
    branch = low_back(jnp.einsum('sre,ed->srd', mixed, out_weight, precision=HIGH))
    middle = hidden_in + branch
    inner = lower_bound(norm_rows(middle, ffn_gain))
    logits = low_back(jnp.einsum('srd,de->sre', inner, router_weight, precision=HIGH))
    probs = jax.nn.softmax(logits, axis=-1)
    picked = (routes[..., None] == jnp.arange(EXPERTS)[None, None, None, :]).astype(jnp.float32)
    chosen = lax.optimization_barrier(jnp.sum(picked * probs[:, :, None, :], axis=-1))
    gates = chosen / lax.optimization_barrier(jnp.sum(chosen, axis=-1, keepdims=True))
    combine = lax.optimization_barrier(jnp.sum(picked * gates[..., None], axis=2))

    def one_expert(total, pieces):
        gate_up, down, column = pieces
        entry = low_back(inner)
        both = low_back(jnp.einsum('srd,df->srf', entry, gate_up, precision=HIGH))
        act = lower_bound(low_back(jax.nn.gelu(both[..., :FFE]) * both[..., FFE:]))
        result = lower_bound(low_back(jnp.einsum('srf,fd->srd', act, down, precision=HIGH)))
        return (total + column[..., None] * result, None)
    moe, _ = lax.scan(jax.checkpoint(one_expert), jnp.zeros_like(middle), (gate_up_weight, down_weight, jnp.moveaxis(combine, -1, 0)))
    return middle + moe

def reference(hidden_in, lengths, order, routes, cotangent, attn_gain, qkv_weight, out_weight, ffn_gain, router_weight, gate_up_weight, down_weight):

    def run(x_in, gain_one, w_qkv, w_out, gain_two, w_router, w_gate_up, w_down):
        return forward(x_in, gain_one, w_qkv, w_out, gain_two, w_router, w_gate_up, w_down, lengths, order, routes)
    output, pullback = jax.vjp(run, hidden_in, attn_gain.astype(jnp.float32), qkv_weight.astype(jnp.float32), out_weight.astype(jnp.float32), ffn_gain.astype(jnp.float32), router_weight.astype(jnp.float32), gate_up_weight.astype(jnp.float32), down_weight.astype(jnp.float32))
    grads = pullback(cotangent)
    return (output, grads[0], grads[1], grads[2], grads[3], grads[4], grads[5], grads[6], grads[7])
```

```python
import math

import jax
import jax.numpy as jnp
from jax import lax
from jax.experimental import pallas as pl
from jax.experimental.pallas import tpu as pltpu
from jax.sharding import PartitionSpec as P

QUERY_HEADS = 12
KEY_VALUE_HEADS = 2
HEAD_SIZE = 128
TOP = 4
CORES = 2
LANES = 128


EPS = 1e-06
BASE = 1000000.0
BF16 = jnp.bfloat16
F32 = jnp.float32


def norm_rows(v, gain):
    return v * lax.rsqrt(jnp.mean(v * v, axis=-1, keepdims=True) + EPS) * gain


def rotation_angles(slot_position):
    half = HEAD_SIZE // 2
    freq = jnp.exp(jnp.arange(half, dtype=F32) * (-2.0 * math.log(BASE) / HEAD_SIZE))
    angle = slot_position.astype(F32)[:, None] * freq[None, :]
    return jnp.cos(angle)[:, None, :], jnp.sin(angle)[:, None, :]


def apply_rotation(t, cosine, sine):
    half = HEAD_SIZE // 2
    first = t[..., :half]
    second = t[..., half:]
    return jnp.concatenate(
        [first * cosine - second * sine, second * cosine + first * sine], axis=-1
    )


def place_docs(packed, lengths):
    ends = jnp.cumsum(lengths)
    before = packed[:, None] >= ends[None, :]
    docs = jnp.sum(before.astype(jnp.int32), axis=1)
    starts = jnp.max(jnp.where(before, ends[None, :], 0), axis=1)
    return (docs, packed - starts)


def act_fn(both):
    half = both.shape[-1] // 2
    return jax.nn.gelu(both[..., :half]) * both[..., half:]


def dot(a, b):
    return jnp.dot(a, b, preferred_element_type=F32)


def dot_turned(a, b):
    return lax.dot_general(a, b, (((1,), (1,)), ((), ())), preferred_element_type=F32)


def dot_rows(a, b):
    return lax.dot_general(a, b, (((0,), (0,)), ((), ())), preferred_element_type=F32)


def after(value, *others):
    return lax.optimization_barrier((value, others))[0]


def axis_len(axis):
    if axis == "y":
        return lax.axis_size("ctx") // CORES
    return lax.axis_size(axis)


def axis_place(axis):
    if axis == "y":
        return lax.axis_index("ctx") // CORES
    return lax.axis_index(axis)


def shifted(value, axis, step):
    name, stride = ("ctx", CORES) if axis == "y" else (axis, 1)
    n = lax.axis_size(name)
    return lax.ppermute(value, name, [(i, (i + step * stride) % n) for i in range(n)])


def core_swap(value):
    n = lax.axis_size("ctx")
    return lax.ppermute(value, "ctx", [(i, i ^ 1) for i in range(n)])


def both_cores(value):
    return jnp.concatenate([value, core_swap(value)], axis=0)


def core_sum(value):
    half = value.shape[0] // 2
    other = core_swap(value[half:].astype(BF16))
    return value[:half].astype(F32) + other.astype(F32)


def in_core_order(mine, other):
    core = lax.axis_index("ctx") % CORES
    return jnp.where(core == 0, jnp.stack([mine, other]), jnp.stack([other, mine]))


def plane_gather(first, second, *before_far):
    lists = []
    for value, order in ((first, ("dp", "y")), (second, ("y", "dp"))):
        n1, n2 = axis_len(order[0]), axis_len(order[1])
        near = jnp.stack([value] + [shifted(value, order[0], s) for s in range(1, n1)])
        if before_far:
            near = after(near, *before_far)
        lists.append([near] + [shifted(near, order[1], t) for t in range(1, n2)])
    return lists


def place_blocks(first, second, parts):
    nx, ny = axis_len("dp"), axis_len("y")

    def kernel(place_ref, *refs):
        first_refs, second_refs = refs[:ny], refs[ny : ny + nx]
        outs = refs[ny + nx :]
        at = pl.program_id(0)
        x_step = lax.rem(place_ref[0] - at // ny + nx, nx)
        y_step = lax.rem(place_ref[1] - at % ny + ny, ny)
        first_columns = first_refs[0].shape[2]
        for taken, step, index, left in (
            (first_refs, y_step, x_step, 0),
            (second_refs, x_step, y_step, first_columns),
        ):
            columns_here = taken[0].shape[2]
            for k, block in enumerate(taken):

                @pl.when(step == k)
                def _(block=block):
                    for (row, n_rows, column, columns), out in zip(parts, outs):
                        low, high = max(column, left), min(column + columns, left + columns_here)
                        if low < high:
                            out[:, low - column : high - column] = block[
                                index, row : row + n_rows, low - left : high - left
                            ]

    whole = [
        pl.BlockSpec(v.shape, lambda i, place_ref: (0, 0, 0)) for v in (*first, *second)
    ]
    return pl.pallas_call(
        kernel,
        grid_spec=pltpu.PrefetchScalarGridSpec(
            num_scalar_prefetch=1,
            grid=(nx * ny,),
            in_specs=whole,
            out_specs=[
                pl.BlockSpec((n_rows, columns), lambda i, place_ref: (i, 0))
                for _, n_rows, _, columns in parts
            ],
        ),
        out_shape=[
            jax.ShapeDtypeStruct((nx * ny * n_rows, columns), first[0].dtype)
            for _, n_rows, _, columns in parts
        ],
        compiler_params=pltpu.CompilerParams(vmem_limit_bytes=48 * 1024 * 1024),
        name="place_blocks",
    )(jnp.stack([axis_place("dp"), axis_place("y")]).astype(jnp.int32), *first, *second)


def xor_shift(value, step):
    n = lax.axis_size("exp")
    return lax.ppermute(value, "exp", [(i, i ^ step) for i in range(n)])


def line_gather(value, n):
    blocks = [value]
    for step in range(1, n):
        if step % 2 == 1:
            blocks.append(xor_shift(blocks[step - 1], 1))
        else:
            blocks.append(xor_shift(value, step))
    return blocks


def line_scatter(blocks):
    total = blocks[0].astype(F32) + xor_shift(blocks[1].astype(BF16), 1).astype(F32)
    for step in range(2, len(blocks), 2):
        handed = xor_shift(blocks[step + 1].astype(BF16), 1).astype(F32)
        pair = (blocks[step].astype(F32) + handed).astype(BF16)
        total = total + xor_shift(pair, step).astype(F32)
    return total


def take_block(parts, dim, place):
    return jnp.concatenate(
        [lax.dynamic_index_in_dim(part, place, dim, keepdims=False) for part in parts], axis=-2
    )


def axis_scatter(parts, axis, dim):
    n, place = axis_len(axis), axis_place(axis)
    total = take_block(parts, dim, place).astype(F32)
    for step in range(1, n):
        sent = take_block(parts, dim, lax.rem(place + step, n))
        total = total + shifted(sent, axis, step).astype(F32)
    return total


def plane_scatter(first, second):
    first = axis_scatter(first, "dp", 0).astype(BF16)
    second = axis_scatter(second, "y", 1).astype(BF16)
    return axis_scatter([first], "y", 0), axis_scatter([second], "dp", 0)


def on_device(
    hidden_in,
    lengths,
    order,
    routes,
    cotangent,
    attn_gain,
    qkv_weight,
    out_weight,
    ffn_gain,
    router_weight,
    gate_up_weight,
    down_weight,
):
    hidden = hidden_in[0]
    grad_out = cotangent[0]
    rows, width = hidden.shape
    n_experts = router_weight.shape[1]
    nx, ny, nz = axis_len("dp"), axis_len("y"), axis_len("exp")
    core = lax.axis_index("ctx") % CORES
    other_core = 1 - core
    shard = qkv_weight.shape[0]
    chip_rows = CORES * rows
    query_width = QUERY_HEADS * HEAD_SIZE
    heads = QUERY_HEADS // KEY_VALUE_HEADS
    own_query = heads * HEAD_SIZE
    own_width = own_query + 2 * HEAD_SIZE
    hidden_units = gate_up_weight.shape[2] // 2
    scale = HEAD_SIZE ** (-0.5)

    def head_columns(which):
        query = lax.dynamic_slice_in_dim(qkv_weight, which * own_query, own_query, 1)
        key = lax.dynamic_slice_in_dim(qkv_weight, query_width + which * HEAD_SIZE, HEAD_SIZE, 1)
        value = lax.dynamic_slice_in_dim(
            qkv_weight, query_width + (KEY_VALUE_HEADS + which) * HEAD_SIZE, HEAD_SIZE, 1
        )
        return [query, key, value]

    extra = jnp.concatenate([attn_gain[:, None], ffn_gain[:, None], router_weight], axis=1)
    extra = jnp.pad(extra, ((0, 0), (0, LANES - extra.shape[1])))
    split = 4 * HEAD_SIZE

    def gather_z(mine, theirs):
        pair = in_core_order(mine, core_swap(theirs)).reshape(CORES * shard, -1)
        blocks = line_gather(pair, nz)
        place = lax.axis_index("exp")
        whole = jnp.zeros((CORES, nz, shard, pair.shape[1]), BF16)
        for step, block in enumerate(blocks):
            at = jnp.bitwise_xor(place, step)
            whole = lax.dynamic_update_slice_in_dim(
                whole, block.reshape(CORES, 1, shard, -1), at, 1
            )
        return whole.reshape(CORES * nz * shard, -1)

    qkv_z = gather_z(
        jnp.concatenate(head_columns(core) + [extra], axis=1),
        jnp.concatenate(head_columns(other_core) + [extra], axis=1),
    )
    block_rows = CORES * nz * shard
    w_all, extra_all = place_blocks(
        *plane_gather(qkv_z[:, :split], qkv_z[:, split:]),
        ((0, block_rows, 0, own_width), (0, block_rows, own_width, LANES)),
    )
    gain_one = extra_all[:, 0].astype(F32)
    gain_two = extra_all[:, 1].astype(F32)
    router_all = extra_all[:, 2 : 2 + n_experts]

    out_rows = out_weight.T
    out_z = gather_z(
        after(lax.dynamic_slice_in_dim(out_rows, core * own_query, own_query, 1), qkv_z),
        lax.dynamic_slice_in_dim(out_rows, other_core * own_query, own_query, 1),
    )
    half_query = own_query // 2
    (out_turned,) = place_blocks(
        *plane_gather(*after((out_z[:, :half_query], out_z[:, half_query:]), w_all)),
        ((0, block_rows, 0, own_query),),
    )

    def expert_rows(which):
        return (
            lax.dynamic_index_in_dim(gate_up_weight, which, 0, keepdims=False),
            lax.dynamic_index_in_dim(down_weight, which, 0, keepdims=False),
        )

    gu_mine, down_mine = expert_rows(core)
    gu_shard, down_shard = gu_mine.shape[0], down_mine.shape[0]
    received = core_swap(jnp.concatenate(expert_rows(other_core), axis=0))
    gu_pair = in_core_order(gu_mine, received[:gu_shard]).reshape(CORES * gu_shard, -1)
    down_pair = in_core_order(down_mine, received[gu_shard:]).reshape(CORES * down_shard, -1)
    expert_block = jnp.concatenate([gu_pair, down_pair], axis=0)
    half_width = width // 2
    gate_up_all, down_all = place_blocks(
        *plane_gather(
            expert_block[:, :hidden_units], expert_block[:, hidden_units:], out_turned
        ),
        (
            (0, CORES * gu_shard, 0, 2 * hidden_units),
            (CORES * gu_shard, CORES * down_shard, 0, width),
        ),
    )

    expert_ids = jnp.arange(n_experts, dtype=jnp.int32)
    used = jnp.any(routes[0][:, :, None] == expert_ids[None, None, :], axis=1)
    marks = jnp.pad(used.astype(BF16), ((0, 0), (0, LANES - n_experts)))
    cot_rows = after(jnp.concatenate([grad_out.astype(BF16), marks], axis=1), out_z)
    group = 4 if nz % 4 == 0 else nz
    cot_near = line_gather(cot_rows, group) if group == nz else None

    mean_root = lax.rsqrt(jnp.mean(hidden * hidden, axis=-1, keepdims=True) + EPS)
    normed = (both_cores((hidden * mean_root).astype(BF16)).astype(F32) * gain_one).astype(BF16)
    packed_all, all_lengths = after((order[0], lengths[0]), qkv_z)
    docs_all, place_all = place_docs(packed_all, all_lengths)

    def own_first(values):
        y_place, y_rows = axis_place("y"), chip_rows
        parts = []
        for t in range(ny):
            at = lax.rem(y_place - t + ny, ny) * y_rows
            for which in (core, other_core):
                parts.append(lax.dynamic_slice_in_dim(values, at + which * rows, rows, 0))
        return jnp.concatenate(parts, axis=0)

    packed_keys, docs_keys, place_keys = (own_first(v) for v in (packed_all, docs_all, place_all))
    packed, docs, slot_position = (v[:chip_rows] for v in (packed_keys, docs_keys, place_keys))
    cosine, sine = rotation_angles(slot_position)
    projected = dot(normed, w_all)
    query_out = projected[:, :own_query]
    query_rows = apply_rotation(
        query_out.reshape(chip_rows, heads, HEAD_SIZE), cosine, sine
    ).astype(BF16)
    key_rows = apply_rotation(
        projected[:, own_query : own_query + HEAD_SIZE].reshape(
            chip_rows, 1, HEAD_SIZE
        ),
        cosine,
        sine,
    ).astype(BF16).reshape(chip_rows, HEAD_SIZE)
    value_rows = projected[:, own_query + HEAD_SIZE :].astype(BF16)
    key_value = jnp.concatenate([key_rows, value_rows], axis=1)
    key_value = jnp.concatenate(
        [key_value] + [shifted(key_value, "y", t) for t in range(1, ny)], axis=0
    )
    keys, values = key_value[:, :HEAD_SIZE], key_value[:, HEAD_SIZE:]
    allowed = (docs[:, None] == docs_keys[None, :]) & (packed_keys[None, :] <= packed[:, None])

    def masked_scores():
        scores = jnp.einsum("qhd,kd->hqk", query_rows, keys, preferred_element_type=F32) * scale
        return jnp.where(allowed, scores, -1e30)

    scores = masked_scores()
    top_score = jnp.max(scores, axis=-1)
    weights = jnp.exp(scores - top_score[..., None])
    total = jnp.sum(weights, axis=-1)
    accum = jnp.einsum("hqk,kd->hqd", weights.astype(BF16), values, preferred_element_type=F32)
    lse = top_score + jnp.log(total)
    attended = accum / total[..., None]
    mixed = jnp.transpose(attended, (1, 0, 2)).reshape(chip_rows, own_query).astype(BF16)
    middle = hidden + core_sum(dot_turned(mixed, out_turned))
    inner = norm_rows(middle, gain_two).astype(BF16)

    def dense_gates(chunk, named):
        logits = dot(chunk, router_all)
        return jax.nn.softmax(jnp.where(named, logits, -jnp.inf), axis=-1)

    gates = dense_gates(inner, used)
    own_expert = lax.axis_index("exp") * CORES + core
    is_own = (expert_ids == own_expert).astype(F32)

    def expert_group(inner_near, cot_near):
        cots = [both_cores(c) for c in cot_near]
        chunks = [both_cores(c) for c in inner_near]
        backs, gated, grads = [], [], []
        for chunk, cot_chunk in zip(chunks, cots):
            if backs:
                chunk = after(chunk, partial)
            cot, named = cot_chunk[:, :width], cot_chunk[:, width : width + n_experts] > 0
            gate = jnp.sum(dense_gates(chunk, named) * is_own, axis=-1, keepdims=True)
            act, act_pull = jax.vjp(act_fn, dot(chunk, gate_up_all))
            grad_act = dot_turned(cot, down_all)
            share = jnp.sum(act * grad_act, axis=-1, keepdims=True)
            grad_both = act_pull(grad_act * gate)[0].astype(BF16)
            gated.append((act * gate).astype(BF16))
            grads.append(grad_both)
            partial = dot_turned(grad_both, gate_up_all)
            shares = jnp.pad(share * is_own, ((0, 0), (0, LANES // 2 - n_experts)))
            high = lax.reduce_precision(shares, 8, 7)
            partial = jnp.concatenate([partial, high, shares - high], axis=1).astype(BF16)
            backs.append(core_sum(partial))
        gated_all, grads_all, chunks_all = after(
            (jnp.concatenate(gated, 0), jnp.concatenate(grads, 0), jnp.concatenate(chunks, 0)),
            backs,
        )
        cot_all = jnp.concatenate([c[:, :width] for c in cots], axis=0)
        weight_grads = (
            dot_rows(chunks_all, grads_all[:, :hidden_units]),
            dot_rows(chunks_all, grads_all[:, hidden_units:]),
            dot_rows(gated_all, cot_all),
        )
        partial_out = dot(gated_all, down_all).astype(BF16).reshape(-1, CORES, rows, width)
        outs = partial_out[:, 0].astype(F32) + core_swap(partial_out[:, 1]).astype(F32)
        return line_scatter(backs), outs, weight_grads

    if group == nz:
        grad_back, outs, weight_grads = expert_group(line_gather(inner, nz), cot_near)
    else:

        def visit(_, state):
            inner_here, cot_here, back, out, sums = state
            more_back, outs, more = expert_group(
                line_gather(inner_here, group), line_gather(cot_here, group)
            )
            out = out + line_scatter([outs[i] for i in range(group)])
            sums = tuple(a + b for a, b in zip(sums, more))
            moved = (shifted(v, "exp", nz - group) for v in (inner_here, cot_here, back + more_back, out))
            return (*moved, sums)

        sums = (
            jnp.zeros((width, hidden_units), F32),
            jnp.zeros((width, hidden_units), F32),
            jnp.zeros((hidden_units, width), F32),
        )
        start = (jnp.zeros((rows, width + LANES), F32), jnp.zeros((rows, width), F32), sums)
        _, _, grad_back, moe, weight_grads = lax.fori_loop(
            0, nz // group, visit, (inner, cot_rows, *start)
        )
        outs = None
    grad_gate_weight, grad_up_weight, grad_down_weight = (w.astype(BF16) for w in weight_grads)

    gu_block, down_block = CORES * gu_shard, CORES * down_shard
    first_sum, second_sum = plane_scatter(
        [
            grad_gate_weight.reshape(nx, ny, gu_block, hidden_units),
            grad_down_weight[:, :half_width].reshape(nx, ny, down_block, half_width),
        ],
        [
            grad_up_weight.reshape(nx, ny, gu_block, hidden_units),
            grad_down_weight[:, half_width:].reshape(nx, ny, down_block, half_width),
        ],
    )
    gu_sum = jnp.concatenate([first_sum[:gu_block], second_sum[:gu_block]], axis=1)
    down_sum = jnp.concatenate([first_sum[gu_block:], second_sum[gu_block:]], axis=1)
    gu_sum = gu_sum.reshape(CORES, gu_shard, 2 * hidden_units)
    down_sum = down_sum.reshape(CORES, down_shard, width)

    def of_core(value, which):
        return lax.dynamic_index_in_dim(value, which, 0, keepdims=False)

    received = core_swap(
        jnp.concatenate([of_core(gu_sum, other_core), of_core(down_sum, other_core)], 0).astype(BF16)
    ).astype(F32)
    grad_gate_up = in_core_order(of_core(gu_sum, core), received[:gu_shard])
    grad_down = in_core_order(of_core(down_sum, core), received[gu_shard:])

    shares = (
        grad_back[:, width : width + n_experts]
        + grad_back[:, width + LANES // 2 : width + LANES // 2 + n_experts]
    )
    mean_share = jnp.sum(gates * shares, axis=1, keepdims=True)
    grad_logits = (gates * (shares - mean_share)).astype(BF16)
    grad_router = dot_rows(inner, grad_logits)
    grad_inner = grad_back[:, :width] + dot_turned(grad_logits, router_all)
    _, second_pull = jax.vjp(norm_rows, middle, gain_two)
    grad_middle_norm, grad_ffn_gain = second_pull(grad_inner)
    grad_middle = grad_out + grad_middle_norm
    grad_branch = both_cores(grad_middle.astype(BF16))
    if outs is not None:
        outs = after(outs, grad_branch)
        moe = line_scatter([outs[i] for i in range(nz)])
    grad_out_turned = dot_rows(grad_branch, mixed).astype(BF16)
    blended_gradient = dot(after(grad_branch, grad_out_turned), out_turned).astype(BF16)
    head_gradient = jnp.transpose(
        blended_gradient.reshape(chip_rows, heads, HEAD_SIZE), (1, 0, 2)
    )
    offset = jnp.sum(head_gradient.astype(F32) * attended, axis=-1)
    probs = jnp.exp(masked_scores() - lse[..., None])
    grad_probs = jnp.einsum("hqd,kd->hqk", head_gradient, values, preferred_element_type=F32)
    grad_scores = (probs * (grad_probs - offset[..., None])).astype(BF16)
    grad_query = jnp.einsum("hqk,kd->qhd", grad_scores, keys, preferred_element_type=F32) * scale
    grad_key = (
        jnp.einsum("hqk,qhd->kd", grad_scores, query_rows, preferred_element_type=F32) * scale
    )
    grad_value = jnp.einsum(
        "hqk,hqd->kd", probs.astype(BF16), head_gradient, preferred_element_type=F32
    )
    grad_kv = jnp.concatenate([grad_key, grad_value], axis=1)
    grad_kv_own = grad_kv[:chip_rows]
    for t in range(1, ny):
        part = grad_kv[t * chip_rows : (t + 1) * chip_rows].astype(BF16)
        grad_kv_own = grad_kv_own + shifted(part, "y", ny - t).astype(F32)
    grad_query = apply_rotation(grad_query, cosine, -sine).reshape(chip_rows, own_query)
    grad_key = apply_rotation(
        grad_kv_own[:, :HEAD_SIZE].reshape(chip_rows, 1, HEAD_SIZE), cosine, -sine
    ).reshape(chip_rows, HEAD_SIZE)
    grad_projected = jnp.concatenate(
        [grad_query, grad_key, grad_kv_own[:, HEAD_SIZE:]], axis=1
    ).astype(BF16)
    output = middle + after(moe, grad_projected)
    grad_first, grad_rest = grad_projected[:, :split], grad_projected[:, split:]
    grad_normed = core_sum(dot_turned(grad_projected, w_all))
    _, first_pull = jax.vjp(norm_rows, hidden, gain_one)
    grad_hidden_norm, grad_attn_gain = first_pull(grad_normed)
    grad_input = grad_middle + grad_hidden_norm

    def scatter_sum(first, second):
        first, second = plane_scatter(
            [first.reshape(nx, ny, block_rows, -1)], [second.reshape(nx, ny, block_rows, -1)]
        )
        summed = jnp.concatenate([first, second], axis=1).reshape(CORES, nz, shard, -1)
        place = lax.axis_index("exp")
        return line_scatter(
            [
                lax.dynamic_index_in_dim(summed, jnp.bitwise_xor(place, step), 1, keepdims=False)
                for step in range(nz)
            ]
        )

    out_sum = scatter_sum(grad_out_turned[:, :half_query], grad_out_turned[:, half_query:])
    out_other = core_swap(of_core(out_sum, other_core).astype(BF16)).astype(F32)
    out_sum = in_core_order(of_core(out_sum, core), out_other)
    grad_out_proj = out_sum.swapaxes(0, 1).reshape(shard, query_width).T

    extra_grad = jnp.concatenate([grad_attn_gain[:, None], grad_ffn_gain[:, None], grad_router], 1)
    extra_grad = jnp.pad(extra_grad, ((0, 0), (0, LANES - extra_grad.shape[1]))).astype(BF16)
    qkv_sum = scatter_sum(
        dot_rows(normed, grad_first).astype(BF16),
        jnp.concatenate([dot_rows(normed, grad_rest).astype(BF16), extra_grad], axis=1),
    )
    qkv_other = core_swap(of_core(qkv_sum, other_core).astype(BF16)).astype(F32)
    qkv_mine = of_core(qkv_sum, core)
    extra_sum = qkv_mine[:, own_width:] + qkv_other[:, own_width:]
    pair = in_core_order(qkv_mine[:, :own_width], qkv_other[:, :own_width])
    key_at, value_at = own_query, own_query + HEAD_SIZE
    grad_qkv = jnp.concatenate(
        [
            pair[:, :, :key_at].swapaxes(0, 1).reshape(shard, -1),
            pair[:, :, key_at:value_at].swapaxes(0, 1).reshape(shard, -1),
            pair[:, :, value_at:].swapaxes(0, 1).reshape(shard, -1),
        ],
        axis=1,
    )
    return (
        output[None],
        grad_input[None],
        extra_sum[:, 0],
        grad_qkv,
        grad_out_proj,
        extra_sum[:, 1],
        extra_sum[:, 2 : 2 + n_experts],
        grad_gate_up,
        grad_down,
    )


def solution(mesh):
    return jax.shard_map(
        on_device,
        mesh=mesh,
        in_specs=(
            P(("dp", "exp"), "ctx", None),
            P(("dp", "exp"), None),
            P(("dp", "exp"), None),
            P(("dp", "exp"), "ctx", None),
            P(("dp", "exp"), "ctx", None),
            P(("dp", "ctx", "exp")),
            P(("dp", "ctx", "exp"), None),
            P(None, ("dp", "ctx", "exp")),
            P(("dp", "ctx", "exp")),
            P(("dp", "ctx", "exp"), None),
            P("exp", ("dp", "ctx"), None),
            P("exp", ("dp", "ctx"), None),
        ),
        out_specs=(
            P(("dp", "exp"), "ctx", None),
            P(("dp", "exp"), "ctx", None),
            P(("dp", "ctx", "exp")),
            P(("dp", "ctx", "exp"), None),
            P(None, ("dp", "ctx", "exp")),
            P(("dp", "ctx", "exp")),
            P(("dp", "ctx", "exp"), None),
            P("exp", ("dp", "ctx"), None),
            P("exp", ("dp", "ctx"), None),
        ),
        check_vma=False,
    )
```

```python
import math

import jax
import jax.numpy as jnp
from jax import lax
from jax.experimental import pallas as pl
from jax.experimental.pallas import tpu as pltpu
from jax.sharding import PartitionSpec as P

QUERY_HEADS = 12
KEY_VALUE_HEADS = 2
HEAD_SIZE = 128
TOP = 4
CORES = 2
LANES = 128
ROUTER_LANE = 2


EPS = 1e-06
BASE = 1000000.0
BF16 = jnp.bfloat16
F32 = jnp.float32


def norm_rows(v, gain):
    return v * lax.rsqrt(jnp.mean(v * v, axis=-1, keepdims=True) + EPS) * gain


def norm_back(v, gain, grad):
    root = lax.rsqrt(jnp.mean(v * v, axis=-1, keepdims=True) + EPS)
    unit = v * root
    scaled = grad * gain
    along = jnp.mean(scaled * unit, axis=-1, keepdims=True)
    return root * (scaled - unit * along), (grad * unit).astype(BF16)


def rotation_tables(slot_position):
    half = HEAD_SIZE // 2
    freq = jnp.exp(jnp.arange(half, dtype=F32) * (-2.0 * math.log(BASE) / HEAD_SIZE))
    angle = slot_position.astype(F32)[:, None] * freq[None, :]
    cosine, sine = jnp.cos(angle), jnp.sin(angle)
    return jnp.concatenate([cosine, cosine], axis=1), jnp.concatenate([-sine, sine], axis=1)


def rotate(t, cosine, sine):
    half = HEAD_SIZE // 2
    return t * cosine + jnp.concatenate([t[:, half:], t[:, :half]], axis=1) * sine


def doc_starts(packed, lengths):
    ends = jnp.cumsum(lengths)
    return jnp.max(jnp.where(packed[:, None] >= ends[None, :], ends[None, :], 0), axis=1)


def dot(a, b):
    return jnp.dot(a, b, preferred_element_type=F32)


def dot_turned(a, b):
    return lax.dot_general(a, b, (((1,), (1,)), ((), ())), preferred_element_type=F32)


def dot_rows(a, b):
    return lax.dot_general(a, b, (((0,), (0,)), ((), ())), preferred_element_type=F32)


def after(value, *others):
    values, tree = jax.tree.flatten(value)
    others = jax.tree.leaves(others)

    def kernel(*refs):
        pass

    anywhere = pl.BlockSpec(memory_space=pl.ANY)
    tied = pl.pallas_call(
        kernel,
        out_shape=[jax.ShapeDtypeStruct(v.shape, v.dtype) for v in values],
        in_specs=[anywhere] * (len(values) + len(others)),
        out_specs=[anywhere] * len(values),
        input_output_aliases={i: i for i in range(len(values))},
        cost_estimate=pl.CostEstimate(flops=1, bytes_accessed=1, transcendentals=0),
        name="after",
    )(*values, *others)
    return jax.tree.unflatten(tree, tied)


def axis_len(axis):
    if axis == "y":
        return lax.axis_size("ctx") // CORES
    return lax.axis_size(axis)


def axis_place(axis):
    if axis == "y":
        return lax.axis_index("ctx") // CORES
    return lax.axis_index(axis)


def shifted(value, axis, step):
    name, stride = ("ctx", CORES) if axis == "y" else (axis, 1)
    n = lax.axis_size(name)
    return lax.ppermute(value, name, [(i, (i + step * stride) % n) for i in range(n)])


def core_swap(value):
    n = lax.axis_size("ctx")
    return lax.ppermute(value, "ctx", [(i, i ^ 1) for i in range(n)])


def both_cores(value):
    return jnp.concatenate([value, core_swap(value)], axis=0)


def core_sum(value):
    half = value.shape[0] // 2
    other = core_swap(value[half:].astype(BF16))
    return value[:half].astype(F32) + other.astype(F32)


def in_core_order(mine, other):
    core = lax.axis_index("ctx") % CORES
    return jnp.where(core == 0, jnp.stack([mine, other]), jnp.stack([other, mine]))


def plane_first(first, second):
    nx, ny = axis_len("dp"), axis_len("y")
    return (
        {(s, 0): shifted(first, "dp", s) for s in range(1, nx)},
        {(0, t): shifted(second, "y", t) for t in range(1, ny)},
    )


def plane_second(first, second):
    nx, ny = axis_len("dp"), axis_len("y")
    return (
        {(0, t): shifted(first, "y", t) for t in range(1, ny)},
        {(s, 0): shifted(second, "dp", s) for s in range(1, nx)},
    )


def plane_third(came):
    nx, ny = axis_len("dp"), axis_len("y")
    return (
        {(s, t): shifted(came[0][s, 0], "y", t) for s in range(1, nx) for t in range(1, ny)},
        {(s, t): shifted(came[1][0, t], "dp", s) for s in range(1, nx) for t in range(1, ny)},
    )


def place_blocks(halves, came, parts):
    nx, ny = axis_len("dp"), axis_len("y")
    steps = [(s, t) for s in range(nx) for t in range(ny)]
    blocks = []
    for k, half in enumerate(halves):
        known = {(0, 0): half}
        for pair in came:
            known.update(pair[k])
        blocks.append([known[step] for step in steps])

    def kernel(place_ref, *refs):
        first_refs, second_refs = refs[: len(steps)], refs[len(steps) : 2 * len(steps)]
        outs = refs[2 * len(steps) :]
        at = pl.program_id(0)
        x_step = lax.rem(place_ref[0] - at // ny + nx, nx)
        y_step = lax.rem(place_ref[1] - at % ny + ny, ny)
        left = first_refs[0].shape[1]
        for step, first, second in zip(steps, first_refs, second_refs):

            @pl.when((x_step == step[0]) & (y_step == step[1]))
            def _(first=first, second=second):
                for (row, n_rows, column, columns), out in zip(parts, outs):
                    for block, low, high in (
                        (first, 0, left),
                        (second, left, left + second.shape[1]),
                    ):
                        begin, end = max(column, low), min(column + columns, high)
                        if begin < end:
                            out[:, begin - column : end - column] = block[
                                row : row + n_rows, begin - low : end - low
                            ]

    whole = [pl.BlockSpec(v.shape, lambda i, place_ref: (0, 0)) for v in (*blocks[0], *blocks[1])]
    return pl.pallas_call(
        kernel,
        grid_spec=pltpu.PrefetchScalarGridSpec(
            num_scalar_prefetch=1,
            grid=(nx * ny,),
            in_specs=whole,
            out_specs=[
                pl.BlockSpec((n_rows, columns), lambda i, place_ref: (i, 0))
                for _, n_rows, _, columns in parts
            ],
        ),
        out_shape=[
            jax.ShapeDtypeStruct((nx * ny * n_rows, columns), BF16)
            for _, n_rows, _, columns in parts
        ],
        compiler_params=pltpu.CompilerParams(vmem_limit_bytes=48 * 1024 * 1024),
        cost_estimate=pl.CostEstimate(flops=1, bytes_accessed=1, transcendentals=0),
        name="place_blocks",
    )(jnp.stack([axis_place("dp"), axis_place("y")]).astype(jnp.int32), *blocks[0], *blocks[1])


def xor_shift(value, step):
    n = lax.axis_size("exp")
    return lax.ppermute(value, "exp", [(i, i ^ step) for i in range(n)])


def line_gather(value, n, *waits):
    blocks = [value]
    for step in range(1, n):
        if step % 2 == 1:
            handed = blocks[step - 1]
            if waits and step > 1:
                handed = blocks[step - 1] = after(handed, *waits)
            blocks.append(xor_shift(handed, 1))
        else:
            blocks.append(xor_shift(value, step))
    return blocks


def line_pairs(blocks, handed):
    return [
        (blocks[step].astype(F32) + other.astype(F32)).astype(BF16)
        for step, other in zip(range(2, len(blocks), 2), handed)
    ]


def line_far(blocks, near, pairs):
    total = blocks[0].astype(F32) + near.astype(F32)
    for step, pair in zip(range(2, len(blocks), 2), pairs):
        total = total + xor_shift(pair, step).astype(F32)
    return total


def line_scatter(blocks):
    odd = xor_shift(jnp.stack(blocks[1::2]), 1)
    pairs = line_pairs(blocks, odd[1:])
    return line_far(blocks, odd[0], pairs), pairs


PLANE_AXES = (("dp", "y"), ("y", "dp"))


def plane_places():
    return jnp.stack([axis_place("dp"), axis_place("y")]).astype(jnp.int32)


def plane_blocks(parts, axes):
    half = []
    for near in range(axis_len(axes[0])):
        blocks = []
        for far in range(axis_len(axes[1])):
            s, t = (near, far) if axes[0] == "dp" else (far, near)
            x = lax.rem(axis_place("dp") + s, axis_len("dp"))
            y = lax.rem(axis_place("y") + t, axis_len("y"))
            taken = [
                lax.dynamic_slice(part, (x, y, 0, 0), (1, 1, *part.shape[2:])).reshape(
                    part.shape[2:]
                )
                for part in parts
            ]
            blocks.append(jnp.concatenate(taken, axis=0))
        half.append(blocks)
    return half


def plane_moved(halves):
    return [
        [shifted(blocks, axes[0], near) for near, blocks in enumerate(half) if near > 0]
        for half, axes in zip(halves, PLANE_AXES)
    ]


def plane_moved_part(halves, handed_on):
    return [
        [
            [shifted(block, axes[0], near) for block in (blocks[1:] if handed_on else blocks[:1])]
            for near, blocks in enumerate(half)
            if near > 0
        ]
        for half, axes in zip(halves, PLANE_AXES)
    ]


def plane_joined(stay, handed_on):
    return [[a + b for a, b in zip(*half)] for half in zip(stay, handed_on)]


def half_sum(half, received, far):
    total = half[0][far].astype(F32)
    for blocks in received:
        total = total + blocks[far].astype(F32)
    return total


def plane_hand_on(halves, received):
    return [
        [half_sum(half, came, far).astype(BF16) for far in range(1, len(half[0]))]
        for half, came in zip(halves, received)
    ]


def plane_handed(handed):
    return [
        [shifted(block, axes[1], far) for far, block in enumerate(blocks, 1)]
        for blocks, axes in zip(handed, PLANE_AXES)
    ]


def plane_sum(halves, received, handed):
    sums = []
    for half, came, last in zip(halves, received, handed):
        total = half_sum(half, came, 0)
        for block in last:
            total = total + block.astype(F32)
        sums.append(total)
    return sums


def half_shapes(shapes):
    counts = [(axis_len(axes[0]), axis_len(axes[1])) for axes in PLANE_AXES]
    return [(far, *shape) for (near, far), shape in zip(counts, shapes) for _ in range(near)]


def two_halves(arrays):
    n = axis_len("dp")
    return [list(arrays[:n]), list(arrays[n:])]


def store_blocks(place_ref, at, outs, first, second):
    nx, ny = axis_len("dp"), axis_len("y")
    x_step, y_step = step_to(place_ref, at)
    for s in range(nx):

        @pl.when(x_step == s)
        def _(s=s):
            first(outs[s].at[y_step])

    for t in range(ny):

        @pl.when(y_step == t)
        def _(t=t):
            second(outs[nx + t].at[x_step])


def blocks_a_step(block_rows):
    n = 1
    while n * block_rows % LANES != 0:
        n += 1
    return n


def step_to(place_ref, at):
    nx, ny = axis_len("dp"), axis_len("y")
    return lax.rem(at // ny - place_ref[0] + nx, nx), lax.rem(at % ny - place_ref[1] + ny, ny)


SMALL = pl.CostEstimate(flops=1, bytes_accessed=1, transcendentals=0)
LOG2_E = 1.4426950408889634
GELU_ROOT = math.sqrt(2.0 / math.pi)
GELU_CUBE = 0.044715
ROW_TILE = 256


def kernel_params(n_axes=1):
    return pltpu.CompilerParams(
        dimension_semantics=("arbitrary",) * n_axes, vmem_limit_bytes=56 * 1024 * 1024
    )


def contract(a, b, a_dim, b_dim):
    return lax.dot_general(a, b, (((a_dim,), (b_dim,)), ((), ())), preferred_element_type=F32)


def turned(t, cosine, sine):
    return t * cosine + pltpu.roll(t, HEAD_SIZE // 2, 1) * sine


def fill_keys(parts, keys_ref, values_ref):
    for i, part in enumerate(parts):
        n = part.shape[0]
        keys_ref[i * n : (i + 1) * n, :] = part[:, :HEAD_SIZE]
        values_ref[i * n : (i + 1) * n, :] = part[:, HEAD_SIZE:]


def fill_bias(key_place_ref, bounds_ref, bias_ref):
    place = key_place_ref[...]
    allowed = (place >= bounds_ref[0:1, :]) & (place <= bounds_ref[1:2, :])
    bias_ref[...] = jnp.where(allowed, 0.0, -1e30)


def unit_rows(rows, *waits):
    def kernel(rows_ref, *refs):
        value = rows_ref[...]
        root = lax.rsqrt(jnp.mean(value * value, axis=-1, keepdims=True) + EPS)
        refs[-1][...] = (value * root).astype(BF16)

    return pl.pallas_call(
        kernel,
        in_specs=[pl.BlockSpec(memory_space=pltpu.VMEM)]
        + [pl.BlockSpec(memory_space=pl.ANY)] * len(waits),
        out_specs=pl.BlockSpec(memory_space=pltpu.VMEM),
        out_shape=jax.ShapeDtypeStruct(rows.shape, BF16),
        compiler_params=pltpu.CompilerParams(vmem_limit_bytes=32 * 1024 * 1024),
        cost_estimate=SMALL,
        name="unit_rows",
    )(rows, *waits)


def attention_forward(projected, key_value, cosine, sine, key_place, bounds, heads, *waits):
    rows = projected.shape[0]
    n_keys = key_place.shape[0]
    n_parts = len(key_value)
    factor = HEAD_SIZE ** (-0.5) * LOG2_E

    def kernel(projected_ref, cos_ref, sin_ref, place_ref, bounds_ref, *refs):
        parts = refs[:n_parts]
        query_ref, mixed_ref, lse_ref, keys_ref, values_ref, bias_ref = refs[n_parts + len(waits) :]
        head = pl.program_id(0)

        @pl.when(head == 0)
        def _():
            fill_keys(parts, keys_ref, values_ref)
            fill_bias(place_ref, bounds_ref, bias_ref)

        for start in range(0, rows, ROW_TILE):
            tile = slice(start, start + ROW_TILE)
            query = turned(projected_ref[tile, :], cos_ref[tile, :], sin_ref[tile, :]).astype(BF16)
            query_ref[tile, :] = query
            scores = contract(keys_ref[...], query, 1, 1) * factor + bias_ref[:, tile]
            top = jnp.max(scores, axis=0, keepdims=True)
            weights = jnp.exp2(scores - top)
            total = jnp.sum(weights, axis=0, keepdims=True)
            probs = (weights * (1.0 / total)).astype(BF16)
            mixed_ref[tile, :] = contract(probs, values_ref[...], 0, 0).astype(BF16)
            lse_ref[pl.ds(head, 1), tile] = top + jnp.log2(total)

    def fixed(shape):
        return pl.BlockSpec(shape, lambda h: (0,) * len(shape))

    by_head = pl.BlockSpec((rows, HEAD_SIZE), lambda h: (0, h))
    return pl.pallas_call(
        kernel,
        grid=(heads,),
        in_specs=[
            by_head,
            fixed(cosine.shape),
            fixed(sine.shape),
            fixed(key_place.shape),
            fixed(bounds.shape),
        ]
        + [fixed(p.shape) for p in key_value]
        + [pl.BlockSpec(memory_space=pl.ANY)] * len(waits),
        out_specs=[by_head, by_head, fixed((8, rows))],
        out_shape=[
            jax.ShapeDtypeStruct((rows, heads * HEAD_SIZE), BF16),
            jax.ShapeDtypeStruct((rows, heads * HEAD_SIZE), BF16),
            jax.ShapeDtypeStruct((8, rows), F32),
        ],
        scratch_shapes=[
            pltpu.VMEM((n_keys, HEAD_SIZE), BF16),
            pltpu.VMEM((n_keys, HEAD_SIZE), BF16),
            pltpu.VMEM((n_keys, rows), F32),
        ],
        compiler_params=kernel_params(),
        cost_estimate=SMALL,
        name="attention_forward",
    )(projected, cosine, sine, key_place, bounds, *key_value, *waits)


def attention_backward(
    query, head_gradient, lse, key_value, cosine, sine, key_place, bounds, heads
):
    rows = query.shape[0]
    n_keys = key_place.shape[0]
    n_parts = len(key_value)
    scale = HEAD_SIZE ** (-0.5)
    factor = scale * LOG2_E

    def kernel(query_ref, grad_ref, lse_ref, cos_ref, sin_ref, place_ref, bounds_ref, *refs):
        parts = refs[:n_parts]
        out_ref = refs[n_parts]
        part_outs = refs[n_parts + 1 : 2 * n_parts + 1]
        keys_ref, values_ref, bias_ref, grad_keys_ref, grad_values_ref = refs[2 * n_parts + 1 :]
        head = pl.program_id(0)

        @pl.when(head == 0)
        def _():
            fill_keys(parts, keys_ref, values_ref)
            fill_bias(place_ref, bounds_ref, bias_ref)
            grad_keys_ref[...] = jnp.zeros_like(grad_keys_ref)
            grad_values_ref[...] = jnp.zeros_like(grad_values_ref)

        for start in range(0, rows, ROW_TILE):
            tile = slice(start, start + ROW_TILE)
            query, grad = query_ref[tile, :], grad_ref[tile, :]
            scores = contract(keys_ref[...], query, 1, 1) * factor + bias_ref[:, tile]
            probs = jnp.exp2(scores - lse_ref[pl.ds(head, 1), tile])
            weighted = probs * contract(values_ref[...], grad, 1, 1)
            offset = jnp.sum(weighted, axis=0, keepdims=True)
            grad_scores = (weighted - probs * offset).astype(BF16)
            grad_keys_ref[...] += contract(grad_scores, query, 1, 0)
            grad_values_ref[...] += contract(probs.astype(BF16), grad, 1, 0)
            grad_query = contract(grad_scores, keys_ref[...], 0, 0) * scale
            out_ref[tile, :] = turned(grad_query, cos_ref[tile, :], -sin_ref[tile, :]).astype(BF16)

        @pl.when(head == heads - 1)
        def _():
            for i, out in enumerate(part_outs):
                n = out.shape[0]
                out[:, :HEAD_SIZE] = (grad_keys_ref[i * n : (i + 1) * n, :] * scale).astype(out.dtype)
                out[:, HEAD_SIZE:] = grad_values_ref[i * n : (i + 1) * n, :].astype(out.dtype)

    def fixed(shape):
        return pl.BlockSpec(shape, lambda h: (0,) * len(shape))

    by_head = pl.BlockSpec((rows, HEAD_SIZE), lambda h: (0, h))
    return pl.pallas_call(
        kernel,
        grid=(heads,),
        in_specs=[
            by_head,
            by_head,
            fixed(lse.shape),
            fixed(cosine.shape),
            fixed(sine.shape),
            fixed(key_place.shape),
            fixed(bounds.shape),
        ]
        + [fixed(p.shape) for p in key_value],
        out_specs=[by_head] + [fixed(p.shape) for p in key_value],
        out_shape=[jax.ShapeDtypeStruct((rows, heads * HEAD_SIZE), BF16)]
        + [
            jax.ShapeDtypeStruct(p.shape, F32 if i == 0 else BF16)
            for i, p in enumerate(key_value)
        ],
        scratch_shapes=[
            pltpu.VMEM((n_keys, HEAD_SIZE), BF16),
            pltpu.VMEM((n_keys, HEAD_SIZE), BF16),
            pltpu.VMEM((n_keys, rows), F32),
            pltpu.VMEM((n_keys, HEAD_SIZE), F32),
            pltpu.VMEM((n_keys, HEAD_SIZE), F32),
        ],
        compiler_params=kernel_params(),
        cost_estimate=SMALL,
        name="attention_backward",
    )(query, head_gradient, lse, cosine, sine, key_place, bounds, *key_value)


def expert_step(expert, chunk, cot, gate_up, down, router, index, n_steps, buffers):
    rows, width = chunk[0].shape
    units = down.shape[0]
    tile = min(256, units)
    steps = units // tile
    n_chunk = len(chunk)
    half_lanes = LANES // 2

    def kernel(expert_ref, *refs):
        chunk_refs, cot_refs = refs[:n_chunk], refs[n_chunk : 2 * n_chunk]
        gate_ref, up_ref, down_ref, router_ref = refs[2 * n_chunk : 2 * n_chunk + 4]
        refs = refs[2 * n_chunk + 4 + len(buffers) :]
        part_refs = refs[:n_chunk]
        rows_ref, cot_ref, gated_ref, grad_gate_ref, grad_up_ref = refs[n_chunk : n_chunk + 5]
        total_ref, weight_ref, share_ref = refs[n_chunk + 5 :]
        step = pl.program_id(0)
        lane = lax.broadcasted_iota(jnp.int32, (rows, LANES), 1)
        places = [slice(i * rows, (i + 1) * rows) for i in range(n_chunk)]

        @pl.when(step == 0)
        def _():
            for i, at in enumerate(places):
                rows_ref[at, :] = chunk_refs[i][...]
                cot_ref[at, :] = cot_refs[i][0, :, :width]
                logits = jnp.dot(chunk_refs[i][...], router_ref[...], preferred_element_type=F32)
                named = cot_refs[i][0, :, width:].astype(F32) > 0
                logits = jnp.where(named, logits, -jnp.inf)
                top = jnp.max(logits, axis=1, keepdims=True)
                weights = jnp.exp(logits - top)
                total = jnp.sum(weights, axis=1, keepdims=True)
                own = jnp.sum(
                    jnp.where(lane == expert_ref[0] + ROUTER_LANE, weights, 0.0), axis=1, keepdims=True
                )
                weight_ref[at, :] = jnp.broadcast_to(own / total, (rows, LANES))
                share_ref[at, :] = jnp.zeros((rows, LANES), F32)
                total_ref[at, :] = jnp.zeros((rows, width), F32)

        for i, at in enumerate(places):
            row = chunk_refs[i][...]
            weight = weight_ref[at, 0:1]
            gate = jnp.dot(row, gate_ref[...], preferred_element_type=F32)
            up = jnp.dot(row, up_ref[...], preferred_element_type=F32)
            grad_act = contract(cot_refs[i][0, :, :width], down_ref[...], 1, 1)
            square = gate * gate
            curve = jnp.tanh(GELU_ROOT * gate * (1.0 + GELU_CUBE * square))
            lifted = 0.5 + 0.5 * curve
            gelu = gate * lifted
            slope = lifted + (0.5 * GELU_ROOT) * gate * (1.0 - curve * curve) * (
                1.0 + (3.0 * GELU_CUBE) * square
            )
            act = gelu * up
            share_ref[at, :] += jnp.broadcast_to(
                jnp.sum(act * grad_act, axis=1, keepdims=True), (rows, LANES)
            )
            gated_ref[at, :] = (act * weight).astype(BF16)
            grad_act = grad_act * weight
            grad_up = (grad_act * gelu).astype(BF16)
            grad_gate = (grad_act * up * slope).astype(BF16)
            grad_gate_ref[at, :] = grad_gate
            grad_up_ref[at, :] = grad_up
            total_ref[at, :] += contract(grad_gate, gate_ref[...], 1, 1) + contract(
                grad_up, up_ref[...], 1, 1
            )

        @pl.when(step == steps - 1)
        def _():
            for i, at in enumerate(places):
                part_refs[i][:, :width] = total_ref[at, :].astype(BF16)
                share = share_ref[at, :]
                high = share.astype(BF16).astype(F32)
                part_refs[i][:, width:] = jnp.where(
                    lane == expert_ref[0],
                    high,
                    jnp.where(lane == expert_ref[0] + half_lanes, share - high, 0.0),
                ).astype(BF16)

    def fixed(shape):
        return pl.BlockSpec(shape, lambda j, scalars: (0,) * len(shape))

    n_rows = n_chunk * rows
    whole_rows = pl.BlockSpec((n_rows, width), lambda j, scalars: (index, 0))
    unit_tile = pl.BlockSpec((n_rows, tile), lambda j, scalars: (index, j))
    first_buffer = 1 + 2 * n_chunk + 4
    grid_spec = pltpu.PrefetchScalarGridSpec(
        num_scalar_prefetch=1,
        grid=(steps,),
        in_specs=[fixed(v.shape) for v in chunk]
        + [
            pl.BlockSpec((1, rows, width + LANES), lambda j, scalars: (scalars[1], 0, 0))
            for _ in cot
        ]
        + [
            pl.BlockSpec((width, tile), lambda j, scalars: (0, j)),
            pl.BlockSpec((width, tile), lambda j, scalars: (0, j + steps)),
            pl.BlockSpec((tile, width), lambda j, scalars: (j, 0)),
            fixed(router.shape),
        ]
        + [pl.BlockSpec(memory_space=pl.ANY)] * len(buffers),
        out_specs=[fixed((rows, width + LANES))] * n_chunk + [whole_rows] * 2 + [unit_tile] * 3,
        scratch_shapes=[
            pltpu.VMEM((n_rows, width), F32),
            pltpu.VMEM((n_rows, LANES), F32),
            pltpu.VMEM((n_rows, LANES), F32),
        ],
    )
    outs = pl.pallas_call(
        kernel,
        grid_spec=grid_spec,
        out_shape=[jax.ShapeDtypeStruct((rows, width + LANES), BF16)] * n_chunk
        + [jax.ShapeDtypeStruct((n_steps * n_rows, width), BF16)] * 2
        + [jax.ShapeDtypeStruct((n_steps * n_rows, units), BF16)] * 3,
        input_output_aliases={first_buffer + i: n_chunk + i for i in range(len(buffers))},
        compiler_params=kernel_params(),
        cost_estimate=SMALL,
        name="expert_step",
    )(expert, *chunk, *cot, gate_up, gate_up, down, router, *buffers)
    return outs[:n_chunk], outs[n_chunk:]


def gate_up_grads(rows, grad_gate, grad_up):
    n_rows, width = rows.shape
    units = grad_gate.shape[1]
    chunk, tile = n_rows // 4, 256

    def kernel(rows_ref, gate_ref, up_ref, gate_out, up_out, gate_sum, up_sum):
        step = pl.program_id(0)

        @pl.when(step == 0)
        def _():
            gate_sum[...] = jnp.zeros_like(gate_sum)
            up_sum[...] = jnp.zeros_like(up_sum)

        for right, total in ((gate_ref, gate_sum), (up_ref, up_sum)):
            for at in range(0, units, tile):
                total[:, at : at + tile] += contract(rows_ref[...], right[:, at : at + tile], 0, 0)

        @pl.when(step == 3)
        def _():
            gate_out[...] = gate_sum[...].astype(BF16)
            up_out[...] = up_sum[...].astype(BF16)

    def by_chunk(columns):
        return pl.BlockSpec((chunk, columns), lambda j: (j, 0))

    whole = pl.BlockSpec((width, units), lambda j: (0, 0))
    return pl.pallas_call(
        kernel,
        grid=(4,),
        in_specs=[by_chunk(width), by_chunk(units), by_chunk(units)],
        out_specs=[whole, whole],
        out_shape=[jax.ShapeDtypeStruct((width, units), BF16)] * 2,
        scratch_shapes=[pltpu.VMEM((width, units), F32)] * 2,
        compiler_params=kernel_params(),
        cost_estimate=SMALL,
        name="gate_up_grads",
    )(rows, grad_gate, grad_up)


def expert_weight_grads(gate_grad, up_grad, cot, gated):
    n_rows, width = cot.shape
    units = gated.shape[1]
    half = width // 2
    nx, ny = axis_len("dp"), axis_len("y")
    n_blocks = nx * ny
    gu_rows, down_rows = width // n_blocks, units // n_blocks
    n_out = 2 * n_blocks
    block_shape = (gu_rows + down_rows, half)
    chunk, tile = n_rows // 4, 256

    def kernel(place_ref, gate_ref, up_ref, cot_ref, gated_ref, *refs):
        outs, down_sum = refs[:n_out], refs[n_out]
        step = pl.program_id(0)

        @pl.when(step == 0)
        def _():
            down_sum[...] = jnp.zeros_like(down_sum)

        for at in range(0, width, tile):
            down_sum[:, at : at + tile] += contract(gated_ref[...], cot_ref[:, at : at + tile], 0, 0)

        def store(out, grad_ref, at, columns):
            out[:gu_rows, :] = grad_ref[at * gu_rows : (at + 1) * gu_rows, :]
            down = down_sum[at * down_rows : (at + 1) * down_rows, columns]
            out[gu_rows:, :] = down.astype(BF16)

        @pl.when(step == 3)
        def _():
            for at in range(n_blocks):
                x_step, y_step = step_to(place_ref, at)
                for s in range(nx):
                    for t in range(ny):

                        @pl.when((x_step == s) & (y_step == t))
                        def _(at=at, s=s, t=t):
                            store(outs[s * ny + t], gate_ref, at, slice(0, half))
                            store(outs[n_blocks + t * nx + s], up_ref, at, slice(half, width))

    def by_chunk(columns):
        return pl.BlockSpec((chunk, columns), lambda j, place: (j, 0))

    whole = pl.BlockSpec((width, units), lambda j, place: (0, 0))
    outs = pl.pallas_call(
        kernel,
        grid_spec=pltpu.PrefetchScalarGridSpec(
            num_scalar_prefetch=1,
            grid=(4,),
            in_specs=[whole, whole, by_chunk(width), by_chunk(units)],
            out_specs=[pl.BlockSpec(block_shape, lambda j, place: (0, 0))] * n_out,
            scratch_shapes=[pltpu.VMEM((units, width), F32)],
        ),
        out_shape=[jax.ShapeDtypeStruct(block_shape, BF16)] * n_out,
        compiler_params=kernel_params(),
        cost_estimate=SMALL,
        name="expert_weight_grads",
    )(plane_places(), gate_grad, up_grad, cot, gated)
    return [
        [outs[s * ny : (s + 1) * ny] for s in range(nx)],
        [outs[n_blocks + t * nx : n_blocks + (t + 1) * nx] for t in range(ny)],
    ]


def expert_results(gated, down):
    n_rows, units = gated.shape
    width = down.shape[1]
    half = n_rows // 8

    def kernel(gated_ref, down_ref, own_ref, other_ref):
        for i, out in enumerate((own_ref, other_ref)):
            rows = gated_ref[i * half : (i + 1) * half, :]
            out[...] = jnp.dot(rows, down_ref[...], preferred_element_type=F32).astype(BF16)

    out = pl.BlockSpec((half, width), lambda j: (2 * (1 - j % 2) + j // 2, 0))
    return pl.pallas_call(
        kernel,
        grid=(4,),
        in_specs=[
            pl.BlockSpec((2 * half, units), lambda j: (j, 0)),
            pl.BlockSpec(down.shape, lambda j: (0, 0)),
        ],
        out_specs=[out, out],
        out_shape=[jax.ShapeDtypeStruct((4 * half, width), BF16)] * 2,
        compiler_params=kernel_params(),
        cost_estimate=SMALL,
        name="expert_results",
    )(gated, down)


def branch_backward(grads, mixed, weight):
    rows, columns = mixed.shape
    width = weight.shape[0]
    half, chip_half = columns // 2, rows // 2
    block_rows = width // (axis_len("dp") * axis_len("y"))
    shapes = half_shapes([(block_rows, half)] * 2)
    n_out = len(shapes)
    together = blocks_a_step(block_rows)
    tile = together * block_rows
    n_tiles = width // tile

    def kernel(place_ref, own_ref, other_ref, mixed_ref, weight_ref, *refs):
        out_ref, outs, total_ref = refs[0], refs[1 : 1 + n_out], refs[1 + n_out]
        at = pl.program_id(0)
        both = jnp.concatenate([own_ref[...], other_ref[...]], axis=0)
        part = jnp.dot(both, weight_ref[...], preferred_element_type=F32)

        @pl.when(at == 0)
        def _():
            total_ref[...] = part

        @pl.when(at > 0)
        def _():
            total_ref[...] += part

        product = contract(both, mixed_ref[...], 0, 0).astype(BF16)
        for i in range(together):
            block = product[i * block_rows : (i + 1) * block_rows]

            def first(out, block=block):
                out[...] = block[:, :half]

            def second(out, block=block):
                out[...] = block[:, half:]

            store_blocks(place_ref, at * together + i, outs, first, second)

        @pl.when(at == n_tiles - 1)
        def _():
            out_ref[...] = total_ref[...].astype(BF16)

    def fixed(shape):
        return pl.BlockSpec(shape, lambda j, place: (0,) * len(shape))

    by_columns = pl.BlockSpec((chip_half, tile), lambda j, place: (0, j))
    outs = pl.pallas_call(
        kernel,
        grid_spec=pltpu.PrefetchScalarGridSpec(
            num_scalar_prefetch=1,
            grid=(n_tiles,),
            in_specs=[
                by_columns,
                by_columns,
                fixed(mixed.shape),
                pl.BlockSpec((tile, columns), lambda j, place: (j, 0)),
            ],
            out_specs=[fixed(mixed.shape)] + [fixed(shape) for shape in shapes],
            scratch_shapes=[pltpu.VMEM((rows, columns), F32)],
        ),
        out_shape=[jax.ShapeDtypeStruct((rows, columns), BF16)]
        + [jax.ShapeDtypeStruct(shape, BF16) for shape in shapes],
        compiler_params=kernel_params(),
        cost_estimate=SMALL,
        name="branch_backward",
    )(plane_places(), *grads, mixed, weight)
    return outs[0], two_halves(outs[1:])


def projection_backward(
    normed, units, weight, grad_query, grad_key_value, split, extra_rows, extra_columns
):
    rows, width = normed.shape
    own_query = grad_query.shape[1]
    columns = own_query + grad_key_value.shape[1]
    half = rows // 2
    block_rows = width // (axis_len("dp") * axis_len("y"))
    shapes = half_shapes([(block_rows, split), (block_rows, columns - split + LANES)])
    together = blocks_a_step(block_rows)
    tile = together * block_rows

    def kernel(
        place_ref, normed_ref, unit_ref, other_unit_ref, weight_ref, query_ref, key_value_ref, *refs
    ):
        extra_refs, column_ref = refs[: len(extra_rows)], refs[len(extra_rows)]
        own_ref, other_ref = refs[len(extra_rows) + 1 : len(extra_rows) + 3]
        outs = refs[len(extra_rows) + 3 :]
        at = pl.program_id(0)
        part = contract(query_ref[...], weight_ref[:, :own_query], 1, 1) + contract(
            key_value_ref[...], weight_ref[:, own_query:], 1, 1
        )
        own_ref[...] = part[:half]
        other_ref[...] = part[half:].astype(BF16)
        both_units = jnp.concatenate([unit_ref[...], other_unit_ref[...]], axis=0)
        terms = (part * both_units.astype(F32)).astype(BF16)
        first = (lax.broadcasted_iota(jnp.int32, (rows, LANES), 1) == 0).astype(F32).astype(BF16)
        extra = contract(terms, first, 0, 0)
        row = 0
        for extra_ref in extra_refs:
            n = extra_ref.shape[0]
            extra += contract(extra_ref[...], column_ref[row : row + n, :], 0, 0)
            row += n
        by_query = contract(normed_ref[...], query_ref[...], 0, 0).astype(BF16)
        by_key_value = contract(normed_ref[...], key_value_ref[...], 0, 0).astype(BF16)
        extra = extra.astype(BF16)
        for i in range(together):
            these = slice(i * block_rows, (i + 1) * block_rows)

            def first(out, these=these):
                out[...] = by_query[these, :split]

            def second(out, these=these):
                out[:, : own_query - split] = by_query[these, split:]
                out[:, own_query - split : columns - split] = by_key_value[these]
                out[:, columns - split :] = extra[these]

            store_blocks(place_ref, at * together + i, outs, first, second)

    def fixed(shape):
        return pl.BlockSpec(shape, lambda j, place: (0,) * len(shape))

    def by_columns(n):
        return pl.BlockSpec((n, tile), lambda j, place: (0, j))

    outs = pl.pallas_call(
        kernel,
        grid_spec=pltpu.PrefetchScalarGridSpec(
            num_scalar_prefetch=1,
            grid=(width // tile,),
            in_specs=[
                by_columns(rows),
                by_columns(half),
                by_columns(half),
                pl.BlockSpec((tile, columns), lambda j, place: (j, 0)),
                fixed(grad_query.shape),
                fixed(grad_key_value.shape),
            ]
            + [by_columns(r.shape[0]) for r in extra_rows]
            + [fixed(extra_columns.shape)],
            out_specs=[by_columns(half), by_columns(half)] + [fixed(shape) for shape in shapes],
        ),
        out_shape=[
            jax.ShapeDtypeStruct((half, width), F32),
            jax.ShapeDtypeStruct((half, width), BF16),
        ]
        + [jax.ShapeDtypeStruct(shape, BF16) for shape in shapes],
        compiler_params=kernel_params(),
        cost_estimate=SMALL,
        name="projection_backward",
    )(
        plane_places(),
        normed,
        *units,
        weight,
        grad_query,
        grad_key_value,
        *extra_rows,
        extra_columns,
    )
    return (
        outs[0],
        outs[1],
        two_halves(outs[2:]),
    )


def middle_backward(backs, gates, middle, gain, router, grad_out):
    rows, width = middle.shape
    half_lanes = LANES // 2
    arrays = jax.tree.leaves(backs)
    n_backs = len(arrays)
    sizes = [len(jax.tree.leaves(back)) for back in backs]

    def kernel(*refs):
        gate_ref, middle_ref, gain_ref, router_ref, out_ref = refs[n_backs : n_backs + 5]
        grad_ref, rounded_ref, terms_ref, logits_ref = refs[n_backs + 5 :]
        came, at = 0.0, 0
        for n in sizes:
            pieces = [r[...].astype(F32) for r in refs[at : at + n]]
            came = came + (jnp.concatenate(pieces, axis=0) if n > 1 else pieces[0])
            at += n
        shares = came[:, width:]
        lane = lax.broadcasted_iota(jnp.int32, (rows, LANES), 1)
        shares = shares + pltpu.roll(shares, half_lanes, 1)
        shares = jnp.where(lane < half_lanes, shares, 0.0)
        shares = pltpu.roll(shares, ROUTER_LANE, 1)
        gate = gate_ref[...]
        mean = jnp.sum(gate * shares, axis=1, keepdims=True)
        logits = (gate * (shares - mean)).astype(BF16)
        logits_ref[...] = logits
        grad = came[:, :width] + contract(logits, router_ref[...], 1, 1)
        value = middle_ref[...]
        root = lax.rsqrt(jnp.mean(value * value, axis=-1, keepdims=True) + EPS)
        unit = value * root
        scaled = grad * gain_ref[...]
        along_unit = jnp.mean(scaled * unit, axis=-1, keepdims=True)
        total = out_ref[...] + root * (scaled - unit * along_unit)
        grad_ref[...] = total
        rounded_ref[...] = total.astype(BF16)
        terms_ref[...] = (grad * unit).astype(BF16)

    vmem = pl.BlockSpec(memory_space=pltpu.VMEM)
    return pl.pallas_call(
        kernel,
        in_specs=[vmem] * (n_backs + 5),
        out_specs=[vmem] * 4,
        out_shape=[
            jax.ShapeDtypeStruct((rows, width), F32),
            jax.ShapeDtypeStruct((rows, width), BF16),
            jax.ShapeDtypeStruct((rows, width), BF16),
            jax.ShapeDtypeStruct((rows, LANES), BF16),
        ],
        compiler_params=pltpu.CompilerParams(vmem_limit_bytes=48 * 1024 * 1024),
        cost_estimate=SMALL,
        name="middle_backward",
    )(*arrays, gates, middle, gain, router, grad_out)


def on_device(
    hidden_in,
    lengths,
    order,
    routes,
    cotangent,
    attn_gain,
    qkv_weight,
    out_weight,
    ffn_gain,
    router_weight,
    gate_up_weight,
    down_weight,
):
    hidden = hidden_in[0]
    grad_out = cotangent[0]
    rows, width = hidden.shape
    n_experts = router_weight.shape[1]
    nx, ny, nz = axis_len("dp"), axis_len("y"), axis_len("exp")
    core = lax.axis_index("ctx") % CORES
    other_core = 1 - core
    shard = qkv_weight.shape[0]
    chip_rows = CORES * rows
    query_width = QUERY_HEADS * HEAD_SIZE
    heads = QUERY_HEADS // KEY_VALUE_HEADS
    own_query = heads * HEAD_SIZE
    own_width = own_query + 2 * HEAD_SIZE
    hidden_units = gate_up_weight.shape[2] // 2
    scale = HEAD_SIZE ** (-0.5)

    extra = jnp.concatenate([attn_gain[:, None], ffn_gain[:, None], router_weight], axis=1)
    extra = jnp.pad(extra, ((0, 0), (0, LANES - extra.shape[1])))
    split = 5 * HEAD_SIZE

    def gather_z(pair, *waits):
        blocks = line_gather(pair.reshape(CORES * shard, -1), nz, *waits)
        place = lax.axis_index("exp")
        whole = jnp.zeros((CORES, nz, shard, pair.shape[2]), BF16)
        for step, block in enumerate(blocks):
            at = jnp.bitwise_xor(place, step)
            whole = lax.dynamic_update_slice_in_dim(
                whole, block.reshape(CORES, 1, shard, -1), at, 1
            )
        return whole.reshape(CORES * nz * shard, -1)

    weights = jnp.concatenate([qkv_weight, extra, out_weight.T], axis=1)
    weights = in_core_order(weights, core_swap(weights))
    key_at = query_width + core * HEAD_SIZE
    value_at = key_at + KEY_VALUE_HEADS * HEAD_SIZE
    extra_at = qkv_weight.shape[1]
    out_at = extra_at + LANES + core * own_query
    weights = jnp.concatenate(
        [
            lax.dynamic_slice_in_dim(weights, core * own_query, own_query, 2),
            lax.dynamic_slice_in_dim(weights, key_at, HEAD_SIZE, 2),
            lax.dynamic_slice_in_dim(weights, value_at, HEAD_SIZE, 2),
            weights[:, :, extra_at : extra_at + LANES],
            lax.dynamic_slice_in_dim(weights, out_at, own_query, 2),
        ],
        axis=2,
    )
    def expert_rows(which):
        return (
            lax.dynamic_index_in_dim(gate_up_weight, which, 0, keepdims=False),
            lax.dynamic_index_in_dim(down_weight, which, 0, keepdims=False),
        )

    gu_mine, down_mine = expert_rows(core)
    gu_shard, down_shard = gu_mine.shape[0], down_mine.shape[0]
    received = core_swap(after(jnp.concatenate(expert_rows(other_core), axis=0), weights))
    gu_pair = in_core_order(gu_mine, received[:gu_shard]).reshape(CORES * gu_shard, -1)
    down_pair = in_core_order(down_mine, received[gu_shard:]).reshape(CORES * down_shard, -1)
    half_width = width // 2
    expert_halves = (
        jnp.concatenate([gu_pair[:, :hidden_units], down_pair[:, :half_width]], axis=0),
        jnp.concatenate([gu_pair[:, hidden_units:], down_pair[:, half_width:]], axis=0),
    )
    expert_first = plane_first(*expert_halves)

    weights_z = after(gather_z(weights), expert_first)
    block_rows = CORES * nz * shard
    half_query = own_query // 2
    group = 4 if nz % 4 == 0 else nz
    phased = group == nz
    qkv_z, out_z = weights_z[:, : own_width + LANES], weights_z[:, own_width + LANES :]
    qkv_halves = (qkv_z[:, :split], qkv_z[:, split:])
    out_halves = (out_z[:, :half_query], out_z[:, half_query:])

    expert_ids = jnp.arange(n_experts, dtype=jnp.int32)
    used = jnp.any(routes[0][:, :, None] == expert_ids[None, None, :], axis=1)
    marks = jnp.pad(
        used.astype(BF16), ((0, 0), (ROUTER_LANE, LANES - ROUTER_LANE - n_experts))
    )
    cot_rows = jnp.concatenate([grad_out.astype(BF16), marks], axis=1)
    cot_all = lax.all_gather(after(cot_rows, weights_z), "exp", axis=0, tiled=False)

    units = unit_rows(hidden, weights_z)
    units_other = core_swap(units)
    qkv_first, qkv_second = plane_first(*qkv_halves), plane_second(*qkv_halves)
    qkv_first, qkv_second, out_halves = after((qkv_first, qkv_second, out_halves), units_other)
    qkv_third = plane_third(qkv_first)
    w_all, extra_all = place_blocks(
        qkv_halves,
        (qkv_first, qkv_second, qkv_third),
        ((0, block_rows, 0, own_width), (0, block_rows, own_width, LANES)),
    )
    out_halves = after(out_halves, w_all)
    out_first, out_second = plane_first(*out_halves), plane_second(*out_halves)
    gain_one = extra_all[:, 0].astype(F32)
    gain_two = extra_all[:, 1].astype(F32)
    lanes = jnp.arange(LANES)
    is_router = (lanes >= ROUTER_LANE) & (lanes < ROUTER_LANE + n_experts)
    router_all = jnp.where(is_router[None, :], extra_all, 0)

    normed = jnp.concatenate([units, units_other], axis=0)
    normed = (normed.astype(F32) * gain_one).astype(BF16)
    packed_all, all_lengths = after((order[0], lengths[0]), weights_z)
    starts_all = doc_starts(packed_all, all_lengths)

    def own_first(values):
        y_place, y_rows = axis_place("y"), chip_rows
        parts = []
        for t in range(ny):
            at = lax.rem(y_place - t + ny, ny) * y_rows
            for which in (core, other_core):
                parts.append(lax.dynamic_slice_in_dim(values, at + which * rows, rows, 0))
        return jnp.concatenate(parts, axis=0)

    packed_keys, starts = own_first(packed_all), own_first(starts_all)[:chip_rows]
    packed = packed_keys[:chip_rows]
    cosine, sine = rotation_tables(packed - starts)
    bounds = jnp.concatenate(
        [starts[None, :], packed[None, :], jnp.zeros((6, chip_rows), jnp.int32)], axis=0
    )
    key_place = packed_keys[:, None]
    projected = dot(normed, w_all)
    key_value = jnp.concatenate(
        [
            rotate(projected[:, own_query : own_query + HEAD_SIZE], cosine, sine),
            projected[:, own_query + HEAD_SIZE : own_width],
        ],
        axis=1,
    ).astype(BF16)
    key_value = [key_value] + [shifted(key_value, "y", t) for t in range(1, ny)]
    out_first, expert_halves, projected, cot_all = after(
        (out_first, expert_halves, projected, cot_all), key_value, out_second
    )
    out_third = plane_third(out_first)
    cot_other = core_swap(cot_all)
    expert_second = plane_second(*expert_halves)
    query_rows, mixed, lse = attention_forward(
        projected, key_value, cosine, sine, key_place, bounds, heads
    )
    mixed, expert_first = after((mixed, expert_first), out_third, cot_other)
    expert_third = plane_third(after(expert_first, expert_second))
    (out_turned,) = place_blocks(
        out_halves, (out_first, out_second, out_third), ((0, block_rows, 0, own_query),)
    )
    middle = hidden + core_sum(dot_turned(mixed, out_turned))
    inner = norm_rows(middle, gain_two).astype(BF16)
    gate_up_all, down_all = place_blocks(
        expert_halves,
        (expert_first, expert_second, expert_third),
        (
            (0, CORES * gu_shard, 0, 2 * hidden_units),
            (CORES * gu_shard, CORES * down_shard, 0, width),
        ),
    )

    logits = jnp.where(marks > 0, dot(inner, extra_all), -jnp.inf)
    gates = jax.nn.softmax(logits, axis=-1)
    place_z = lax.axis_index("exp")
    own_expert = place_z * CORES + core

    def expert_group(inner_rows, from_place):
        buffers = []

        def run(index, chunk):
            scalars = jnp.stack([own_expert, jnp.bitwise_xor(from_place, index)])
            (mine, other), filled = expert_step(
                scalars.astype(jnp.int32),
                chunk,
                [cot_all, cot_other],
                gate_up_all,
                down_all,
                extra_all,
                index,
                4,
                buffers,
            )
            buffers[:] = filled
            return mine, other

        def joined(mine, other):
            return (mine.astype(F32) + other.astype(F32)).astype(BF16)

        rows_1, rows_2 = xor_shift(inner_rows, 1), xor_shift(inner_rows, 2)
        mine_0, other_0 = run(0, [inner_rows, core_swap(inner_rows)])

        rows_1, rows_2 = after((rows_1, rows_2), other_0)
        rows_3 = xor_shift(rows_2, 1)
        swapped = [core_swap(rows_1), core_swap(rows_2)]
        rows_1, other_1_rows, other_2_rows = after((rows_1, *swapped))
        other_0 = core_swap(other_0)
        mine_1, other_1 = run(1, [rows_1, other_1_rows])

        rows_2, rows_3, other_1 = after((rows_2, rows_3, other_1), other_0)
        other_3_rows = core_swap(rows_3)
        other_1 = core_swap(other_1)
        mine_2, other_2 = run(2, [rows_2, other_2_rows])

        rows_3, other_2, mine_1 = after((rows_3, other_2, mine_1), other_3_rows, other_1)
        other_2 = core_swap(other_2)
        back_1 = joined(mine_1, other_1)
        near = xor_shift(back_1, 1)
        rows_3 = after(rows_3, back_1)
        mine_3, other_3 = run(3, [rows_3, other_3_rows])

        mine_3, other_3 = after((mine_3, other_3), other_2, near)
        back_3 = joined(mine_3, core_swap(other_3))
        handed = xor_shift(back_3, 1)
        all_rows, all_cots, gated_all, grad_gates, grad_ups = after(buffers, back_3)
        if phased:
            grad_gate, grad_up = gate_up_grads(all_rows, grad_gates, grad_ups)
            grad_gate, grad_up, handed = after((grad_gate, grad_up, handed))
        mine_0, mine_2 = after((mine_0, mine_2), back_3)
        back_2 = joined(mine_2, other_2)
        (pair,) = line_pairs([None, None, back_2, None], [handed])
        if phased:
            grad_gate, gated_all, pair = after((grad_gate, gated_all, pair), gates)
        pieces = [pair[: rows // 2], pair[rows // 2 :]]
        moved, received = xor_shift(pieces[0], 2), []
        if phased:
            weight_grads = expert_weight_grads(grad_gate, grad_up, all_cots, gated_all)
            weight_grads, gated_all, moved, pieces = after((weight_grads, gated_all, moved, pieces))
            received = plane_moved_part(weight_grads, True)
        else:
            weight_grads = (
                dot_rows(all_rows, grad_gates),
                dot_rows(all_rows, grad_ups),
                dot_rows(gated_all, all_cots),
            )
        moved_more = xor_shift(pieces[1], 2)
        back_0 = joined(mine_0, other_0)
        outs, outs_other = expert_results(gated_all, down_all)
        outs, outs_other, moved_more, received, weight_grads = after(
            (outs, outs_other, moved_more, received, weight_grads), back_0
        )
        if phased:
            received = plane_joined(plane_moved_part(weight_grads, False), received)
        outs_other = core_swap(outs_other)
        outs = [
            (outs[half].astype(F32) + outs_other[half].astype(F32)).astype(BF16)
            for half in (slice(0, 2 * rows), slice(2 * rows, 4 * rows))
        ]
        return (back_0, near, (moved, moved_more)), outs, weight_grads, received

    if phased:
        backs, outs, expert_grads, expert_received = expert_group(inner, place_z)
    else:

        def visit(turn, state):
            inner_here, back, out, sums = state
            more_back, outs, more, _ = expert_group(
                inner_here, lax.rem(place_z + turn * group, nz)
            )
            back = back + more_back[0].astype(F32) + more_back[1].astype(F32)
            back = back + jnp.concatenate(more_back[2], axis=0).astype(F32)
            odd, even = (o.reshape(2, rows, width) for o in outs)
            out = out + line_scatter([even[0], odd[0], even[1], odd[1]])[0]
            sums = tuple(a + b for a, b in zip(sums, more))
            return (*(shifted(v, "exp", nz - group) for v in (inner_here, back, out)), sums)

        sums = (
            jnp.zeros((width, hidden_units), F32),
            jnp.zeros((width, hidden_units), F32),
            jnp.zeros((hidden_units, width), F32),
        )
        start = (jnp.zeros((rows, width + LANES), F32), jnp.zeros((rows, width), F32), sums)
        _, back, moe, sums = lax.fori_loop(0, nz // group, visit, (inner, *start))
        backs = (back,)
        gate, up, down = (w.astype(BF16) for w in sums)
        gate, up = (w.reshape(nx, ny, CORES * gu_shard, hidden_units) for w in (gate, up))
        down = down.reshape(nx, ny, CORES * down_shard, width)
        expert_grads = [
            plane_blocks([gate, down[..., :half_width]], PLANE_AXES[0]),
            plane_blocks([up, down[..., half_width:]], PLANE_AXES[1]),
        ]
        expert_received = plane_joined(
            plane_moved_part(expert_grads, False), plane_moved_part(expert_grads, True)
        )
    gu_block = CORES * gu_shard

    if phased:
        results_near, results_handed = (
            xor_shift(outs[0][low : low + rows], 1) for low in (0, rows)
        )

    grad_middle, grad_branch, ffn_terms, grad_logits = middle_backward(
        backs, gates, middle, gain_two[None, :], router_all, grad_out
    )
    grad_branch = [grad_branch, core_swap(grad_branch)]
    blended_gradient, out_grads = branch_backward(grad_branch, mixed, out_turned)
    if phased:
        blended_gradient, results_handed = after((blended_gradient, results_handed))
        pair = (outs[1][rows:].astype(F32) + results_handed.astype(F32)).astype(BF16)
        cuts = [0, rows // 128 * 48, rows // 128 * 80, rows]
        pieces = [pair[low:high] for low, high in zip(cuts, cuts[1:])]
        blended_gradient, pieces = after((blended_gradient, pieces))
        moe_far = [xor_shift(pieces[0], 2)]
    blended_gradient, out_grads, expert_received = after(
        (blended_gradient, out_grads, expert_received)
    )
    out_received = plane_moved(out_grads)
    grad_query, grad_kv_own, *grad_kv_parts = attention_backward(
        query_rows, blended_gradient, lse, key_value, cosine, sine, key_place, bounds, heads
    )

    if phased:
        grad_query, grad_kv_parts, pieces, results_near = after(
            (grad_query, grad_kv_parts, pieces, results_near), moe_far
        )
        moe_far.append(xor_shift(pieces[1], 2))
    grad_kv_parts, out_received = after((grad_kv_parts, out_received))
    grad_kv_parts = [shifted(part, "y", ny - t) for t, part in enumerate(grad_kv_parts, 1)]
    out_received = after(out_received, grad_query)
    if phased:
        grad_query, pieces = after((grad_query, pieces), moe_far, grad_kv_parts)
        moe_far.append(xor_shift(pieces[2], 2))
    out_handed = plane_handed(plane_hand_on(out_grads, out_received))

    for part in grad_kv_parts:
        grad_kv_own = grad_kv_own + part.astype(F32)
    grad_key_value = jnp.concatenate(
        [rotate(grad_kv_own[:, :HEAD_SIZE], cosine, -sine), grad_kv_own[:, HEAD_SIZE:]], axis=1
    ).astype(BF16)
    is_ffn = (lax.broadcasted_iota(jnp.int32, (rows, LANES), 1) == 1).astype(BF16)
    grad_normed, grad_normed_other, qkv_grads = projection_backward(
        normed,
        [units, units_other],
        w_all,
        grad_query,
        grad_key_value,
        split,
        [ffn_terms, inner],
        jnp.concatenate([is_ffn, grad_logits], axis=0),
    )
    if phased:
        qkv_grads, moe_far = after((qkv_grads, moe_far))
        moe = outs[1][:rows].astype(F32) + results_near.astype(F32)
        moe = moe + jnp.concatenate(moe_far, axis=0).astype(F32)
    qkv_grads, out_handed = after((qkv_grads, out_handed))

    def line_sum(first, second):
        summed = jnp.concatenate([first, second], axis=1).astype(BF16)
        summed = summed.reshape(CORES, nz, shard, -1)
        place = lax.axis_index("exp")
        return line_scatter(
            [
                lax.dynamic_index_in_dim(summed, jnp.bitwise_xor(place, step), 1, keepdims=False)
                for step in range(nz)
            ]
        )

    def of_core(value, which):
        return lax.dynamic_index_in_dim(value, which, 0, keepdims=False)

    qkv_received = plane_moved(qkv_grads)
    out_received, out_handed = after((out_received, out_handed), qkv_grads)
    out_sum, out_pairs = line_sum(*plane_sum(out_grads, out_received, out_handed))
    qkv_hand_on = plane_hand_on(qkv_grads, qkv_received)
    qkv_handed = plane_handed(qkv_hand_on)
    expert_hand_on = plane_hand_on(expert_grads, after(expert_received, qkv_grads))
    grad_normed_other, moe = after((grad_normed_other, moe), qkv_hand_on)
    grad_normed = grad_normed + core_swap(grad_normed_other).astype(F32)
    grad_hidden_norm, _ = norm_back(hidden, gain_one, grad_normed)
    grad_input = grad_middle + grad_hidden_norm
    output = middle + moe
    expert_handed = plane_handed(after(expert_hand_on, qkv_hand_on))
    qkv_sum, qkv_pairs = line_sum(*plane_sum(qkv_grads, qkv_received, qkv_handed))
    out_sum = after(out_sum, qkv_pairs)
    out_other = core_swap(of_core(out_sum, other_core).astype(BF16)).astype(F32)
    out_sum = in_core_order(of_core(out_sum, core), out_other)
    grad_out_proj = out_sum.swapaxes(0, 1).reshape(shard, query_width).T

    first_sum, second_sum = plane_sum(expert_grads, expert_received, expert_handed)
    gu_sum = jnp.concatenate([first_sum[:gu_block], second_sum[:gu_block]], axis=1)
    down_sum = jnp.concatenate([first_sum[gu_block:], second_sum[gu_block:]], axis=1)
    gu_sum = gu_sum.reshape(CORES, gu_shard, 2 * hidden_units)
    down_sum = down_sum.reshape(CORES, down_shard, width)
    received = core_swap(
        jnp.concatenate([of_core(gu_sum, other_core), of_core(down_sum, other_core)], 0).astype(BF16)
    ).astype(F32)
    grad_gate_up = in_core_order(of_core(gu_sum, core), received[:gu_shard])
    grad_down = in_core_order(of_core(down_sum, core), received[gu_shard:])

    qkv_other = core_swap(of_core(qkv_sum, other_core).astype(BF16)).astype(F32)
    qkv_mine = of_core(qkv_sum, core)
    extra_sum = qkv_mine[:, own_width:] + qkv_other[:, own_width:]
    pair = in_core_order(qkv_mine[:, :own_width], qkv_other[:, :own_width])
    key_at, value_at = own_query, own_query + HEAD_SIZE
    grad_qkv = jnp.concatenate(
        [
            pair[:, :, :key_at].swapaxes(0, 1).reshape(shard, -1),
            pair[:, :, key_at:value_at].swapaxes(0, 1).reshape(shard, -1),
            pair[:, :, value_at:].swapaxes(0, 1).reshape(shard, -1),
        ],
        axis=1,
    )
    return (
        output[None],
        grad_input[None],
        extra_sum[:, 0],
        grad_qkv,
        grad_out_proj,
        extra_sum[:, 1],
        extra_sum[:, 2 : 2 + n_experts],
        grad_gate_up,
        grad_down,
    )


def solution(mesh):
    return jax.shard_map(
        on_device,
        mesh=mesh,
        in_specs=(
            P(("dp", "exp"), "ctx", None),
            P(("dp", "exp"), None),
            P(("dp", "exp"), None),
            P(("dp", "exp"), "ctx", None),
            P(("dp", "exp"), "ctx", None),
            P(("dp", "ctx", "exp")),
            P(("dp", "ctx", "exp"), None),
            P(None, ("dp", "ctx", "exp")),
            P(("dp", "ctx", "exp")),
            P(("dp", "ctx", "exp"), None),
            P("exp", ("dp", "ctx"), None),
            P("exp", ("dp", "ctx"), None),
        ),
        out_specs=(
            P(("dp", "exp"), "ctx", None),
            P(("dp", "exp"), "ctx", None),
            P(("dp", "ctx", "exp")),
            P(("dp", "ctx", "exp"), None),
            P(None, ("dp", "ctx", "exp")),
            P(("dp", "ctx", "exp")),
            P(("dp", "ctx", "exp"), None),
            P("exp", ("dp", "ctx"), None),
            P("exp", ("dp", "ctx"), None),
        ),
        check_vma=False,
    )
```

```python
import math

import jax
import jax.numpy as jnp
from jax import lax
from jax.experimental import pallas as pl
from jax.experimental.pallas import tpu as pltpu
from jax.sharding import PartitionSpec as P

QUERY_HEADS = 12
KEY_VALUE_HEADS = 2
HEAD_SIZE = 128
TOP = 4
CORES = 2
LANES = 128
ROUTER_LANE = 2


EPS = 1e-06
BASE = 1000000.0
BF16 = jnp.bfloat16
F32 = jnp.float32


def norm_rows(v, gain):
    return v * lax.rsqrt(jnp.mean(v * v, axis=-1, keepdims=True) + EPS) * gain


def norm_back(v, gain, grad):
    root = lax.rsqrt(jnp.mean(v * v, axis=-1, keepdims=True) + EPS)
    unit = v * root
    scaled = grad * gain
    along = jnp.mean(scaled * unit, axis=-1, keepdims=True)
    return root * (scaled - unit * along), (grad * unit).astype(BF16)


def rotation_tables(slot_position):
    half = HEAD_SIZE // 2
    freq = jnp.exp(jnp.arange(half, dtype=F32) * (-2.0 * math.log(BASE) / HEAD_SIZE))
    angle = slot_position.astype(F32)[:, None] * freq[None, :]
    cosine, sine = jnp.cos(angle), jnp.sin(angle)
    return jnp.concatenate([cosine, cosine], axis=1), jnp.concatenate([-sine, sine], axis=1)


def rotate(t, cosine, sine):
    half = HEAD_SIZE // 2
    return t * cosine + jnp.concatenate([t[:, half:], t[:, :half]], axis=1) * sine


def doc_starts(packed, lengths):
    ends = jnp.cumsum(lengths)
    return jnp.max(jnp.where(packed[:, None] >= ends[None, :], ends[None, :], 0), axis=1)


def dot(a, b):
    return jnp.dot(a, b, preferred_element_type=F32)


def dot_turned(a, b):
    return lax.dot_general(a, b, (((1,), (1,)), ((), ())), preferred_element_type=F32)


def dot_rows(a, b):
    return lax.dot_general(a, b, (((0,), (0,)), ((), ())), preferred_element_type=F32)


def after(value, *others):
    values, tree = jax.tree.flatten(value)
    others = jax.tree.leaves(others)

    def kernel(*refs):
        pass

    anywhere = pl.BlockSpec(memory_space=pl.ANY)
    tied = pl.pallas_call(
        kernel,
        out_shape=[jax.ShapeDtypeStruct(v.shape, v.dtype) for v in values],
        in_specs=[anywhere] * (len(values) + len(others)),
        out_specs=[anywhere] * len(values),
        input_output_aliases={i: i for i in range(len(values))},
        cost_estimate=pl.CostEstimate(flops=1, bytes_accessed=1, transcendentals=0),
        name="after",
    )(*values, *others)
    return jax.tree.unflatten(tree, tied)


def axis_len(axis):
    if axis == "y":
        return lax.axis_size("ctx") // CORES
    return lax.axis_size(axis)


def axis_place(axis):
    if axis == "y":
        return lax.axis_index("ctx") // CORES
    return lax.axis_index(axis)


def shifted(value, axis, step):
    name, stride = ("ctx", CORES) if axis == "y" else (axis, 1)
    n = lax.axis_size(name)
    return lax.ppermute(value, name, [(i, (i + step * stride) % n) for i in range(n)])


def core_swap(value):
    n = lax.axis_size("ctx")
    return lax.ppermute(value, "ctx", [(i, i ^ 1) for i in range(n)])


def both_cores(value):
    return jnp.concatenate([value, core_swap(value)], axis=0)


def core_sum(value):
    half = value.shape[0] // 2
    other = core_swap(value[half:].astype(BF16))
    return value[:half].astype(F32) + other.astype(F32)


def in_core_order(mine, other):
    core = lax.axis_index("ctx") % CORES
    return jnp.where(core == 0, jnp.stack([mine, other]), jnp.stack([other, mine]))


def plane_first(first, second):
    nx, ny = axis_len("dp"), axis_len("y")
    return (
        {(s, 0): shifted(first, "dp", s) for s in range(1, nx)},
        {(0, t): shifted(second, "y", t) for t in range(1, ny)},
    )


def plane_second(first, second):
    nx, ny = axis_len("dp"), axis_len("y")
    return (
        {(0, t): shifted(first, "y", t) for t in range(1, ny)},
        {(s, 0): shifted(second, "dp", s) for s in range(1, nx)},
    )


def plane_third(came):
    nx, ny = axis_len("dp"), axis_len("y")
    return (
        {(s, t): shifted(came[0][s, 0], "y", t) for s in range(1, nx) for t in range(1, ny)},
        {(s, t): shifted(came[1][0, t], "dp", s) for s in range(1, nx) for t in range(1, ny)},
    )


def place_blocks(halves, came, parts):
    nx, ny = axis_len("dp"), axis_len("y")
    steps = [(s, t) for s in range(nx) for t in range(ny)]
    blocks = []
    for k, half in enumerate(halves):
        known = {(0, 0): half}
        for pair in came:
            known.update(pair[k])
        blocks.append([known[step] for step in steps])

    def kernel(place_ref, *refs):
        first_refs, second_refs = refs[: len(steps)], refs[len(steps) : 2 * len(steps)]
        outs = refs[2 * len(steps) :]
        at = pl.program_id(0)
        x_step = lax.rem(place_ref[0] - at // ny + nx, nx)
        y_step = lax.rem(place_ref[1] - at % ny + ny, ny)
        left = first_refs[0].shape[1]
        for step, first, second in zip(steps, first_refs, second_refs):

            @pl.when((x_step == step[0]) & (y_step == step[1]))
            def _(first=first, second=second):
                for (row, n_rows, column, columns), out in zip(parts, outs):
                    for block, low, high in (
                        (first, 0, left),
                        (second, left, left + second.shape[1]),
                    ):
                        begin, end = max(column, low), min(column + columns, high)
                        if begin < end:
                            out[:, begin - column : end - column] = block[
                                row : row + n_rows, begin - low : end - low
                            ]

    whole = [pl.BlockSpec(v.shape, lambda i, place_ref: (0, 0)) for v in (*blocks[0], *blocks[1])]
    return pl.pallas_call(
        kernel,
        grid_spec=pltpu.PrefetchScalarGridSpec(
            num_scalar_prefetch=1,
            grid=(nx * ny,),
            in_specs=whole,
            out_specs=[
                pl.BlockSpec((n_rows, columns), lambda i, place_ref: (i, 0))
                for _, n_rows, _, columns in parts
            ],
        ),
        out_shape=[
            jax.ShapeDtypeStruct((nx * ny * n_rows, columns), BF16)
            for _, n_rows, _, columns in parts
        ],
        compiler_params=pltpu.CompilerParams(vmem_limit_bytes=48 * 1024 * 1024),
        cost_estimate=pl.CostEstimate(flops=1, bytes_accessed=1, transcendentals=0),
        name="place_blocks",
    )(jnp.stack([axis_place("dp"), axis_place("y")]).astype(jnp.int32), *blocks[0], *blocks[1])


def xor_shift(value, step):
    n = lax.axis_size("exp")
    return lax.ppermute(value, "exp", [(i, i ^ step) for i in range(n)])


def line_gather(value, n, *waits):
    blocks = [value]
    for step in range(1, n):
        if step % 2 == 1:
            handed = blocks[step - 1]
            if waits and step > 1:
                handed = blocks[step - 1] = after(handed, *waits)
            blocks.append(xor_shift(handed, 1))
        else:
            blocks.append(xor_shift(value, step))
    return blocks


def line_pairs(blocks, handed):
    return [
        (blocks[step].astype(F32) + other.astype(F32)).astype(BF16)
        for step, other in zip(range(2, len(blocks), 2), handed)
    ]


def line_far(blocks, near, pairs):
    total = blocks[0].astype(F32) + near.astype(F32)
    for step, pair in zip(range(2, len(blocks), 2), pairs):
        total = total + xor_shift(pair, step).astype(F32)
    return total


def line_scatter(blocks):
    odd = xor_shift(jnp.stack(blocks[1::2]), 1)
    pairs = line_pairs(blocks, odd[1:])
    return line_far(blocks, odd[0], pairs), pairs


PLANE_AXES = (("dp", "y"), ("y", "dp"))


def plane_places():
    return jnp.stack([axis_place("dp"), axis_place("y")]).astype(jnp.int32)


def plane_blocks(parts, axes):
    half = []
    for near in range(axis_len(axes[0])):
        blocks = []
        for far in range(axis_len(axes[1])):
            s, t = (near, far) if axes[0] == "dp" else (far, near)
            x = lax.rem(axis_place("dp") + s, axis_len("dp"))
            y = lax.rem(axis_place("y") + t, axis_len("y"))
            taken = [
                lax.dynamic_slice(part, (x, y, 0, 0), (1, 1, *part.shape[2:])).reshape(
                    part.shape[2:]
                )
                for part in parts
            ]
            blocks.append(jnp.concatenate(taken, axis=0))
        half.append(blocks)
    return half


def plane_moved(halves):
    return [
        [shifted(blocks, axes[0], near) for near, blocks in enumerate(half) if near > 0]
        for half, axes in zip(halves, PLANE_AXES)
    ]


def plane_moved_part(halves, handed_on):
    return [
        [
            [shifted(block, axes[0], near) for block in (blocks[1:] if handed_on else blocks[:1])]
            for near, blocks in enumerate(half)
            if near > 0
        ]
        for half, axes in zip(halves, PLANE_AXES)
    ]


def plane_joined(stay, handed_on):
    return [[a + b for a, b in zip(*half)] for half in zip(stay, handed_on)]


def half_sum(half, received, far):
    total = half[0][far].astype(F32)
    for blocks in received:
        total = total + blocks[far].astype(F32)
    return total


def plane_hand_on(halves, received):
    return [
        [half_sum(half, came, far).astype(BF16) for far in range(1, len(half[0]))]
        for half, came in zip(halves, received)
    ]


def plane_handed(handed):
    return [
        [shifted(block, axes[1], far) for far, block in enumerate(blocks, 1)]
        for blocks, axes in zip(handed, PLANE_AXES)
    ]


def plane_sum(halves, received, handed):
    sums = []
    for half, came, last in zip(halves, received, handed):
        total = half_sum(half, came, 0)
        for block in last:
            total = total + block.astype(F32)
        sums.append(total)
    return sums


def half_shapes(shapes):
    counts = [(axis_len(axes[0]), axis_len(axes[1])) for axes in PLANE_AXES]
    return [(far, *shape) for (near, far), shape in zip(counts, shapes) for _ in range(near)]


def two_halves(arrays):
    n = axis_len("dp")
    return [list(arrays[:n]), list(arrays[n:])]


def store_blocks(place_ref, at, outs, first, second):
    nx, ny = axis_len("dp"), axis_len("y")
    x_step, y_step = step_to(place_ref, at)
    for s in range(nx):

        @pl.when(x_step == s)
        def _(s=s):
            first(outs[s].at[y_step])

    for t in range(ny):

        @pl.when(y_step == t)
        def _(t=t):
            second(outs[nx + t].at[x_step])


def blocks_a_step(block_rows):
    n = 1
    while n * block_rows % LANES != 0:
        n += 1
    return n


def step_to(place_ref, at):
    nx, ny = axis_len("dp"), axis_len("y")
    return lax.rem(at // ny - place_ref[0] + nx, nx), lax.rem(at % ny - place_ref[1] + ny, ny)


SMALL = pl.CostEstimate(flops=1, bytes_accessed=1, transcendentals=0)
LOG2_E = 1.4426950408889634
GELU_ROOT = math.sqrt(2.0 / math.pi)
GELU_CUBE = 0.044715
ROW_TILE = 512


def kernel_params(n_axes=1):
    return pltpu.CompilerParams(
        dimension_semantics=("arbitrary",) * n_axes, vmem_limit_bytes=56 * 1024 * 1024
    )


def contract(a, b, a_dim, b_dim):
    return lax.dot_general(a, b, (((a_dim,), (b_dim,)), ((), ())), preferred_element_type=F32)


def turned(t, cosine, sine):
    return t * cosine + pltpu.roll(t, HEAD_SIZE // 2, 1) * sine


def fill_keys(parts, keys_ref, values_ref):
    for i, part in enumerate(parts):
        n = part.shape[0]
        keys_ref[i * n : (i + 1) * n, :] = part[:, :HEAD_SIZE]
        values_ref[i * n : (i + 1) * n, :] = part[:, HEAD_SIZE:]


def fill_bias(key_place_ref, bounds_ref, bias_ref):
    place = key_place_ref[...]
    allowed = (place >= bounds_ref[0:1, :]) & (place <= bounds_ref[1:2, :])
    bias_ref[...] = jnp.where(allowed, 0.0, -1e30)


def unit_rows(rows, *waits):
    def kernel(rows_ref, *refs):
        value = rows_ref[...]
        root = lax.rsqrt(jnp.mean(value * value, axis=-1, keepdims=True) + EPS)
        refs[-1][...] = (value * root).astype(BF16)

    return pl.pallas_call(
        kernel,
        in_specs=[pl.BlockSpec(memory_space=pltpu.VMEM)]
        + [pl.BlockSpec(memory_space=pl.ANY)] * len(waits),
        out_specs=pl.BlockSpec(memory_space=pltpu.VMEM),
        out_shape=jax.ShapeDtypeStruct(rows.shape, BF16),
        compiler_params=pltpu.CompilerParams(vmem_limit_bytes=32 * 1024 * 1024),
        cost_estimate=SMALL,
        name="unit_rows",
    )(rows, *waits)


def attention_forward(projected, key_value, cosine, sine, key_place, bounds, heads, *waits):
    rows = projected.shape[0]
    n_keys = key_place.shape[0]
    n_parts = len(key_value)
    factor = HEAD_SIZE ** (-0.5) * LOG2_E

    def kernel(projected_ref, cos_ref, sin_ref, place_ref, bounds_ref, *refs):
        parts = refs[:n_parts]
        query_ref, mixed_ref, lse_ref, keys_ref, values_ref, bias_ref = refs[n_parts + len(waits) :]
        head = pl.program_id(0)

        @pl.when(head == 0)
        def _():
            fill_keys(parts, keys_ref, values_ref)
            fill_bias(place_ref, bounds_ref, bias_ref)

        for start in range(0, rows, ROW_TILE):
            tile = slice(start, start + ROW_TILE)
            query = turned(projected_ref[tile, :], cos_ref[tile, :], sin_ref[tile, :]).astype(BF16)
            query_ref[tile, :] = query
            scores = contract(keys_ref[...], query, 1, 1) * factor + bias_ref[:, tile]
            top = jnp.max(scores, axis=0, keepdims=True)
            weights = jnp.exp2(scores - top)
            total = jnp.sum(weights, axis=0, keepdims=True)
            probs = (weights * (1.0 / total)).astype(BF16)
            mixed_ref[tile, :] = contract(probs, values_ref[...], 0, 0).astype(BF16)
            lse_ref[pl.ds(head, 1), tile] = top + jnp.log2(total)

    def fixed(shape):
        return pl.BlockSpec(shape, lambda h: (0,) * len(shape))

    by_head = pl.BlockSpec((rows, HEAD_SIZE), lambda h: (0, h))
    return pl.pallas_call(
        kernel,
        grid=(heads,),
        in_specs=[
            by_head,
            fixed(cosine.shape),
            fixed(sine.shape),
            fixed(key_place.shape),
            fixed(bounds.shape),
        ]
        + [fixed(p.shape) for p in key_value]
        + [pl.BlockSpec(memory_space=pl.ANY)] * len(waits),
        out_specs=[by_head, by_head, fixed((8, rows))],
        out_shape=[
            jax.ShapeDtypeStruct((rows, heads * HEAD_SIZE), BF16),
            jax.ShapeDtypeStruct((rows, heads * HEAD_SIZE), BF16),
            jax.ShapeDtypeStruct((8, rows), F32),
        ],
        scratch_shapes=[
            pltpu.VMEM((n_keys, HEAD_SIZE), BF16),
            pltpu.VMEM((n_keys, HEAD_SIZE), BF16),
            pltpu.VMEM((n_keys, rows), F32),
        ],
        compiler_params=kernel_params(),
        cost_estimate=SMALL,
        name="attention_forward",
    )(projected, cosine, sine, key_place, bounds, *key_value, *waits)


def attention_backward(
    query, head_gradient, lse, key_value, cosine, sine, key_place, bounds, heads
):
    rows = query.shape[0]
    n_keys = key_place.shape[0]
    n_parts = len(key_value)
    scale = HEAD_SIZE ** (-0.5)
    factor = scale * LOG2_E

    def kernel(query_ref, grad_ref, lse_ref, cos_ref, sin_ref, place_ref, bounds_ref, *refs):
        parts = refs[:n_parts]
        out_ref = refs[n_parts]
        part_outs = refs[n_parts + 1 : 2 * n_parts + 1]
        keys_ref, values_ref, bias_ref, grad_keys_ref, grad_values_ref = refs[2 * n_parts + 1 :]
        head = pl.program_id(0)

        @pl.when(head == 0)
        def _():
            fill_keys(parts, keys_ref, values_ref)
            fill_bias(place_ref, bounds_ref, bias_ref)
            grad_keys_ref[...] = jnp.zeros_like(grad_keys_ref)
            grad_values_ref[...] = jnp.zeros_like(grad_values_ref)

        for start in range(0, rows, ROW_TILE):
            tile = slice(start, start + ROW_TILE)
            query, grad = query_ref[tile, :], grad_ref[tile, :]
            scores = contract(keys_ref[...], query, 1, 1) * factor + bias_ref[:, tile]
            probs = jnp.exp2(scores - lse_ref[pl.ds(head, 1), tile])
            weighted = probs * contract(values_ref[...], grad, 1, 1)
            offset = jnp.sum(weighted, axis=0, keepdims=True)
            grad_scores = (weighted - probs * offset).astype(BF16)
            grad_keys_ref[...] += contract(grad_scores, query, 1, 0)
            grad_values_ref[...] += contract(probs.astype(BF16), grad, 1, 0)
            grad_query = contract(grad_scores, keys_ref[...], 0, 0) * scale
            out_ref[tile, :] = turned(grad_query, cos_ref[tile, :], -sin_ref[tile, :]).astype(BF16)

        @pl.when(head == heads - 1)
        def _():
            for i, out in enumerate(part_outs):
                n = out.shape[0]
                out[:, :HEAD_SIZE] = (grad_keys_ref[i * n : (i + 1) * n, :] * scale).astype(out.dtype)
                out[:, HEAD_SIZE:] = grad_values_ref[i * n : (i + 1) * n, :].astype(out.dtype)

    def fixed(shape):
        return pl.BlockSpec(shape, lambda h: (0,) * len(shape))

    by_head = pl.BlockSpec((rows, HEAD_SIZE), lambda h: (0, h))
    return pl.pallas_call(
        kernel,
        grid=(heads,),
        in_specs=[
            by_head,
            by_head,
            fixed(lse.shape),
            fixed(cosine.shape),
            fixed(sine.shape),
            fixed(key_place.shape),
            fixed(bounds.shape),
        ]
        + [fixed(p.shape) for p in key_value],
        out_specs=[by_head] + [fixed(p.shape) for p in key_value],
        out_shape=[jax.ShapeDtypeStruct((rows, heads * HEAD_SIZE), BF16)]
        + [
            jax.ShapeDtypeStruct(p.shape, F32 if i == 0 else BF16)
            for i, p in enumerate(key_value)
        ],
        scratch_shapes=[
            pltpu.VMEM((n_keys, HEAD_SIZE), BF16),
            pltpu.VMEM((n_keys, HEAD_SIZE), BF16),
            pltpu.VMEM((n_keys, rows), F32),
            pltpu.VMEM((n_keys, HEAD_SIZE), F32),
            pltpu.VMEM((n_keys, HEAD_SIZE), F32),
        ],
        compiler_params=kernel_params(),
        cost_estimate=SMALL,
        name="attention_backward",
    )(query, head_gradient, lse, cosine, sine, key_place, bounds, *key_value)


def expert_step(scalars, chunk, cot, gate_up, down, router, index, n_steps, buffers):
    rows, width = chunk[0].shape
    units = down.shape[0]
    n_chunk = len(chunk)
    n_rows = n_chunk * rows
    half_lanes = LANES // 2
    places = [slice(i * rows, (i + 1) * rows) for i in range(n_chunk)]

    def kernel(scalar_ref, router_ref, *refs):
        chunk_refs, cot_refs = refs[:n_chunk], refs[n_chunk : 2 * n_chunk]
        gate_up_ref, down_ref = refs[2 * n_chunk : 2 * n_chunk + 2]
        refs = refs[2 * n_chunk + 2 + len(buffers) :]
        part_outs, buffer_outs = refs[:n_chunk], refs[n_chunk : n_chunk + 5]
        row, cots, gate_w, up_w, down_w, part, gated, grad_gates, grad_ups, in_sems, out_sems = refs[
            n_chunk + 5 :
        ]
        loads, stores = [], []

        def load(source, target):
            copy = pltpu.make_async_copy(source, target, in_sems.at[len(loads)])
            copy.start()
            loads.append(copy)

        def store(source, target):
            copy = pltpu.make_async_copy(source, target, out_sems.at[len(stores)])
            copy.start()
            stores.append(copy)

        for ref, at in zip(chunk_refs, places):
            load(ref, row.at[at])
        load(gate_up_ref.at[:, :units], gate_w)
        load(gate_up_ref.at[:, units:], up_w)
        for ref, at in zip(cot_refs, places):
            load(ref.at[scalar_ref[1]], cots.at[at])
        load(down_ref, down_w)
        in_buffer = [slice(index * n_rows + at.start, index * n_rows + at.stop) for at in places]

        for copy in loads[: n_chunk + 1]:
            copy.wait()
        store(row, buffer_outs[0].at[index * n_rows : (index + 1) * n_rows])
        gates = [jnp.dot(row[at, :], gate_w[...], preferred_element_type=F32) for at in places]
        loads[n_chunk + 1].wait()
        ups = [jnp.dot(row[at, :], up_w[...], preferred_element_type=F32) for at in places]
        for copy in loads[n_chunk + 2 :]:
            copy.wait()
        store(cots.at[:, :width], buffer_outs[1].at[index * n_rows : (index + 1) * n_rows])

        lane = lax.broadcasted_iota(jnp.int32, (rows, LANES), 1)
        for at, gate, up, out, buffer_at in zip(places, gates, ups, part_outs, in_buffer):
            logits = jnp.dot(row[at, :], router_ref[...], preferred_element_type=F32)
            logits = jnp.where(cots[at, width:].astype(F32) > 0, logits, -jnp.inf)
            top = jnp.max(logits, axis=1, keepdims=True)
            weights = jnp.exp(logits - top)
            total = jnp.sum(weights, axis=1, keepdims=True)
            own = jnp.where(lane == scalar_ref[0] + ROUTER_LANE, weights, 0.0)
            weight = jnp.sum(own, axis=1, keepdims=True) / total

            grad_act = contract(cots[at, :width], down_w[...], 1, 1)
            square = gate * gate
            curve = jnp.tanh(GELU_ROOT * gate * (1.0 + GELU_CUBE * square))
            lifted = 0.5 + 0.5 * curve
            gelu = gate * lifted
            slope = lifted + (0.5 * GELU_ROOT) * gate * (1.0 - curve * curve) * (
                1.0 + (3.0 * GELU_CUBE) * square
            )
            act = gelu * up
            share = jnp.sum(act * grad_act, axis=1, keepdims=True)
            gated[at, :] = (act * weight).astype(BF16)
            grad_act = grad_act * weight
            grad_up = (grad_act * gelu).astype(BF16)
            grad_gate = (grad_act * up * slope).astype(BF16)
            grad_gates[at, :] = grad_gate
            grad_ups[at, :] = grad_up
            for source, target in zip((gated, grad_gates, grad_ups), buffer_outs[2:]):
                store(source.at[at], target.at[buffer_at])
            grad_row = contract(grad_gate, gate_w[...], 1, 1) + contract(grad_up, up_w[...], 1, 1)
            part[at, :width] = grad_row.astype(BF16)
            high = share.astype(BF16).astype(F32)
            part[at, width:] = jnp.where(
                lane == scalar_ref[0],
                high,
                jnp.where(lane == scalar_ref[0] + half_lanes, share - high, 0.0),
            ).astype(BF16)
            store(part.at[at], out)
        for copy in stores:
            copy.wait()

    anywhere = pl.BlockSpec(memory_space=pl.ANY)
    first_buffer = 2 + 2 * n_chunk + 2
    outs = pl.pallas_call(
        kernel,
        in_specs=[pl.BlockSpec(memory_space=pltpu.SMEM), pl.BlockSpec(memory_space=pltpu.VMEM)]
        + [anywhere] * (2 * n_chunk + 2 + len(buffers)),
        out_specs=[anywhere] * (n_chunk + 5),
        out_shape=[jax.ShapeDtypeStruct((rows, width + LANES), BF16)] * n_chunk
        + [jax.ShapeDtypeStruct((n_steps * n_rows, width), BF16)] * 2
        + [jax.ShapeDtypeStruct((n_steps * n_rows, units), BF16)] * 3,
        input_output_aliases={first_buffer + i: n_chunk + i for i in range(len(buffers))},
        scratch_shapes=[
            pltpu.VMEM((n_rows, width), BF16),
            pltpu.VMEM((n_rows, width + LANES), BF16),
            pltpu.VMEM((width, units), BF16),
            pltpu.VMEM((width, units), BF16),
            pltpu.VMEM((units, width), BF16),
            pltpu.VMEM((n_rows, width + LANES), BF16),
        ]
        + [pltpu.VMEM((n_rows, units), BF16)] * 3
        + [
            pltpu.SemaphoreType.DMA((2 * n_chunk + 3,)),
            pltpu.SemaphoreType.DMA((4 * n_chunk + 2,)),
        ],
        compiler_params=pltpu.CompilerParams(vmem_limit_bytes=56 * 1024 * 1024),
        cost_estimate=SMALL,
        name="expert_step",
    )(scalars, router, *chunk, *cot, gate_up, down, *buffers)
    return outs[:n_chunk], outs[n_chunk:]


def gate_up_grads(rows, grad_gate, grad_up):
    n_rows, width = rows.shape
    units = grad_gate.shape[1]
    tile = 256

    def kernel(rows_ref, gate_ref, up_ref, gate_out, up_out):
        for right, out in ((gate_ref, gate_out), (up_ref, up_out)):
            out[...] = contract(rows_ref[...], right[...], 0, 0).astype(BF16)

    whole = pl.BlockSpec((n_rows, units), lambda j: (0, 0))
    out = pl.BlockSpec((tile, units), lambda j: (j, 0))
    return pl.pallas_call(
        kernel,
        grid=(width // tile,),
        in_specs=[pl.BlockSpec((n_rows, tile), lambda j: (0, j)), whole, whole],
        out_specs=[out, out],
        out_shape=[jax.ShapeDtypeStruct((width, units), BF16)] * 2,
        compiler_params=kernel_params(),
        cost_estimate=SMALL,
        name="gate_up_grads",
    )(rows, grad_gate, grad_up)


def expert_weight_grads(gate_grad, up_grad, cot, gated):
    n_rows, width = cot.shape
    units = gated.shape[1]
    half = width // 2
    nx, ny = axis_len("dp"), axis_len("y")
    n_blocks = nx * ny
    gu_rows, down_rows = width // n_blocks, units // n_blocks
    n_out = 2 * n_blocks
    block_shape = (gu_rows + down_rows, half)
    chunk, tile = n_rows // 4, 256

    def kernel(place_ref, gate_ref, up_ref, cot_ref, gated_ref, *refs):
        outs, down_sum = refs[:n_out], refs[n_out]
        step = pl.program_id(0)

        @pl.when(step == 0)
        def _():
            down_sum[...] = jnp.zeros_like(down_sum)

        for at in range(0, width, tile):
            down_sum[:, at : at + tile] += contract(gated_ref[...], cot_ref[:, at : at + tile], 0, 0)

        def store(out, grad_ref, at, columns):
            out[:gu_rows, :] = grad_ref[at * gu_rows : (at + 1) * gu_rows, :]
            down = down_sum[at * down_rows : (at + 1) * down_rows, columns]
            out[gu_rows:, :] = down.astype(BF16)

        @pl.when(step == 3)
        def _():
            for at in range(n_blocks):
                x_step, y_step = step_to(place_ref, at)
                for s in range(nx):
                    for t in range(ny):

                        @pl.when((x_step == s) & (y_step == t))
                        def _(at=at, s=s, t=t):
                            store(outs[s * ny + t], gate_ref, at, slice(0, half))
                            store(outs[n_blocks + t * nx + s], up_ref, at, slice(half, width))

    def by_chunk(columns):
        return pl.BlockSpec((chunk, columns), lambda j, place: (j, 0))

    whole = pl.BlockSpec((width, units), lambda j, place: (0, 0))
    outs = pl.pallas_call(
        kernel,
        grid_spec=pltpu.PrefetchScalarGridSpec(
            num_scalar_prefetch=1,
            grid=(4,),
            in_specs=[whole, whole, by_chunk(width), by_chunk(units)],
            out_specs=[pl.BlockSpec(block_shape, lambda j, place: (0, 0))] * n_out,
            scratch_shapes=[pltpu.VMEM((units, width), F32)],
        ),
        out_shape=[jax.ShapeDtypeStruct(block_shape, BF16)] * n_out,
        compiler_params=kernel_params(),
        cost_estimate=SMALL,
        name="expert_weight_grads",
    )(plane_places(), gate_grad, up_grad, cot, gated)
    return [
        [outs[s * ny : (s + 1) * ny] for s in range(nx)],
        [outs[n_blocks + t * nx : n_blocks + (t + 1) * nx] for t in range(ny)],
    ]


def expert_results(gated, down):
    n_rows, units = gated.shape
    width = down.shape[1]
    half = n_rows // 8

    def kernel(gated_ref, down_ref, own_ref, other_ref):
        for i, out in enumerate((own_ref, other_ref)):
            rows = gated_ref[i * half : (i + 1) * half, :]
            out[...] = jnp.dot(rows, down_ref[...], preferred_element_type=F32).astype(BF16)

    out = pl.BlockSpec((half, width), lambda j: (2 * (1 - j % 2) + j // 2, 0))
    return pl.pallas_call(
        kernel,
        grid=(4,),
        in_specs=[
            pl.BlockSpec((2 * half, units), lambda j: (j, 0)),
            pl.BlockSpec(down.shape, lambda j: (0, 0)),
        ],
        out_specs=[out, out],
        out_shape=[jax.ShapeDtypeStruct((4 * half, width), BF16)] * 2,
        compiler_params=kernel_params(),
        cost_estimate=SMALL,
        name="expert_results",
    )(gated, down)


def branch_backward(grads, mixed, weight):
    rows, columns = mixed.shape
    width = weight.shape[0]
    half, chip_half = columns // 2, rows // 2
    block_rows = width // (axis_len("dp") * axis_len("y"))
    shapes = half_shapes([(block_rows, half)] * 2)
    n_out = len(shapes)
    together = width // block_rows
    tile = together * block_rows
    n_tiles = width // tile

    def kernel(place_ref, own_ref, other_ref, mixed_ref, weight_ref, *refs):
        out_ref, outs, total_ref = refs[0], refs[1 : 1 + n_out], refs[1 + n_out]
        at = pl.program_id(0)
        both = jnp.concatenate([own_ref[...], other_ref[...]], axis=0)
        part = jnp.dot(both, weight_ref[...], preferred_element_type=F32)

        @pl.when(at == 0)
        def _():
            total_ref[...] = part

        @pl.when(at > 0)
        def _():
            total_ref[...] += part

        product = contract(both, mixed_ref[...], 0, 0).astype(BF16)
        for i in range(together):
            block = product[i * block_rows : (i + 1) * block_rows]

            def first(out, block=block):
                out[...] = block[:, :half]

            def second(out, block=block):
                out[...] = block[:, half:]

            store_blocks(place_ref, at * together + i, outs, first, second)

        @pl.when(at == n_tiles - 1)
        def _():
            out_ref[...] = total_ref[...].astype(BF16)

    def fixed(shape):
        return pl.BlockSpec(shape, lambda j, place: (0,) * len(shape))

    by_columns = pl.BlockSpec((chip_half, tile), lambda j, place: (0, j))
    outs = pl.pallas_call(
        kernel,
        grid_spec=pltpu.PrefetchScalarGridSpec(
            num_scalar_prefetch=1,
            grid=(n_tiles,),
            in_specs=[
                by_columns,
                by_columns,
                fixed(mixed.shape),
                pl.BlockSpec((tile, columns), lambda j, place: (j, 0)),
            ],
            out_specs=[fixed(mixed.shape)] + [fixed(shape) for shape in shapes],
            scratch_shapes=[pltpu.VMEM((rows, columns), F32)],
        ),
        out_shape=[jax.ShapeDtypeStruct((rows, columns), BF16)]
        + [jax.ShapeDtypeStruct(shape, BF16) for shape in shapes],
        compiler_params=kernel_params(),
        cost_estimate=SMALL,
        name="branch_backward",
    )(plane_places(), *grads, mixed, weight)
    return outs[0], two_halves(outs[1:])


def projection_backward(
    normed, units, weight, grad_query, grad_key_value, split, extra_rows, extra_columns
):
    rows, width = normed.shape
    own_query = grad_query.shape[1]
    columns = own_query + grad_key_value.shape[1]
    half = rows // 2
    block_rows = width // (axis_len("dp") * axis_len("y"))
    shapes = half_shapes([(block_rows, split), (block_rows, columns - split + LANES)])
    together = blocks_a_step(block_rows)
    tile = together * block_rows

    def kernel(
        place_ref, normed_ref, unit_ref, other_unit_ref, weight_ref, query_ref, key_value_ref, *refs
    ):
        extra_refs, column_ref = refs[: len(extra_rows)], refs[len(extra_rows)]
        own_ref, other_ref = refs[len(extra_rows) + 1 : len(extra_rows) + 3]
        outs = refs[len(extra_rows) + 3 :]
        at = pl.program_id(0)
        part = contract(query_ref[...], weight_ref[:, :own_query], 1, 1) + contract(
            key_value_ref[...], weight_ref[:, own_query:], 1, 1
        )
        own_ref[...] = part[:half]
        other_ref[...] = part[half:].astype(BF16)
        both_units = jnp.concatenate([unit_ref[...], other_unit_ref[...]], axis=0)
        terms = (part * both_units.astype(F32)).astype(BF16)
        first = (lax.broadcasted_iota(jnp.int32, (rows, LANES), 1) == 0).astype(F32).astype(BF16)
        extra = contract(terms, first, 0, 0)
        row = 0
        for extra_ref in extra_refs:
            n = extra_ref.shape[0]
            extra += contract(extra_ref[...], column_ref[row : row + n, :], 0, 0)
            row += n
        by_query = contract(normed_ref[...], query_ref[...], 0, 0).astype(BF16)
        by_key_value = contract(normed_ref[...], key_value_ref[...], 0, 0).astype(BF16)
        extra = extra.astype(BF16)
        for i in range(together):
            these = slice(i * block_rows, (i + 1) * block_rows)

            def first(out, these=these):
                out[...] = by_query[these, :split]

            def second(out, these=these):
                out[:, : own_query - split] = by_query[these, split:]
                out[:, own_query - split : columns - split] = by_key_value[these]
                out[:, columns - split :] = extra[these]

            store_blocks(place_ref, at * together + i, outs, first, second)

    def fixed(shape):
        return pl.BlockSpec(shape, lambda j, place: (0,) * len(shape))

    def by_columns(n):
        return pl.BlockSpec((n, tile), lambda j, place: (0, j))

    outs = pl.pallas_call(
        kernel,
        grid_spec=pltpu.PrefetchScalarGridSpec(
            num_scalar_prefetch=1,
            grid=(width // tile,),
            in_specs=[
                by_columns(rows),
                by_columns(half),
                by_columns(half),
                pl.BlockSpec((tile, columns), lambda j, place: (j, 0)),
                fixed(grad_query.shape),
                fixed(grad_key_value.shape),
            ]
            + [by_columns(r.shape[0]) for r in extra_rows]
            + [fixed(extra_columns.shape)],
            out_specs=[by_columns(half), by_columns(half)] + [fixed(shape) for shape in shapes],
        ),
        out_shape=[
            jax.ShapeDtypeStruct((half, width), F32),
            jax.ShapeDtypeStruct((half, width), BF16),
        ]
        + [jax.ShapeDtypeStruct(shape, BF16) for shape in shapes],
        compiler_params=kernel_params(),
        cost_estimate=SMALL,
        name="projection_backward",
    )(
        plane_places(),
        normed,
        *units,
        weight,
        grad_query,
        grad_key_value,
        *extra_rows,
        extra_columns,
    )
    return (
        outs[0],
        outs[1],
        two_halves(outs[2:]),
    )


def middle_backward(backs, gates, middle, gain, router, grad_out):
    rows, width = middle.shape
    half_lanes = LANES // 2
    arrays = jax.tree.leaves(backs)
    n_backs = len(arrays)
    sizes = [len(jax.tree.leaves(back)) for back in backs]

    def kernel(*refs):
        gate_ref, middle_ref, gain_ref, router_ref, out_ref = refs[n_backs : n_backs + 5]
        grad_ref, rounded_ref, terms_ref, logits_ref = refs[n_backs + 5 :]
        came, at = 0.0, 0
        for n in sizes:
            pieces = [r[...].astype(F32) for r in refs[at : at + n]]
            came = came + (jnp.concatenate(pieces, axis=0) if n > 1 else pieces[0])
            at += n
        shares = came[:, width:]
        lane = lax.broadcasted_iota(jnp.int32, (rows, LANES), 1)
        shares = shares + pltpu.roll(shares, half_lanes, 1)
        shares = jnp.where(lane < half_lanes, shares, 0.0)
        shares = pltpu.roll(shares, ROUTER_LANE, 1)
        gate = gate_ref[...]
        mean = jnp.sum(gate * shares, axis=1, keepdims=True)
        logits = (gate * (shares - mean)).astype(BF16)
        logits_ref[...] = logits
        grad = came[:, :width] + contract(logits, router_ref[...], 1, 1)
        value = middle_ref[...]
        root = lax.rsqrt(jnp.mean(value * value, axis=-1, keepdims=True) + EPS)
        unit = value * root
        scaled = grad * gain_ref[...]
        along_unit = jnp.mean(scaled * unit, axis=-1, keepdims=True)
        total = out_ref[...] + root * (scaled - unit * along_unit)
        grad_ref[...] = total
        rounded_ref[...] = total.astype(BF16)
        terms_ref[...] = (grad * unit).astype(BF16)

    vmem = pl.BlockSpec(memory_space=pltpu.VMEM)
    return pl.pallas_call(
        kernel,
        in_specs=[vmem] * (n_backs + 5),
        out_specs=[vmem] * 4,
        out_shape=[
            jax.ShapeDtypeStruct((rows, width), F32),
            jax.ShapeDtypeStruct((rows, width), BF16),
            jax.ShapeDtypeStruct((rows, width), BF16),
            jax.ShapeDtypeStruct((rows, LANES), BF16),
        ],
        compiler_params=pltpu.CompilerParams(vmem_limit_bytes=48 * 1024 * 1024),
        cost_estimate=SMALL,
        name="middle_backward",
    )(*arrays, gates, middle, gain, router, grad_out)


def on_device(
    hidden_in,
    lengths,
    order,
    routes,
    cotangent,
    attn_gain,
    qkv_weight,
    out_weight,
    ffn_gain,
    router_weight,
    gate_up_weight,
    down_weight,
):
    hidden = hidden_in[0]
    grad_out = cotangent[0]
    rows, width = hidden.shape
    n_experts = router_weight.shape[1]
    nx, ny, nz = axis_len("dp"), axis_len("y"), axis_len("exp")
    core = lax.axis_index("ctx") % CORES
    other_core = 1 - core
    shard = qkv_weight.shape[0]
    chip_rows = CORES * rows
    query_width = QUERY_HEADS * HEAD_SIZE
    heads = QUERY_HEADS // KEY_VALUE_HEADS
    own_query = heads * HEAD_SIZE
    own_width = own_query + 2 * HEAD_SIZE
    hidden_units = gate_up_weight.shape[2] // 2
    scale = HEAD_SIZE ** (-0.5)

    extra = jnp.concatenate([attn_gain[:, None], ffn_gain[:, None], router_weight], axis=1)
    extra = jnp.pad(extra, ((0, 0), (0, LANES - extra.shape[1])))
    split = 5 * HEAD_SIZE

    def gather_z(pair, *waits):
        blocks = line_gather(pair.reshape(CORES * shard, -1), nz, *waits)
        place = lax.axis_index("exp")
        whole = jnp.zeros((CORES, nz, shard, pair.shape[2]), BF16)
        for step, block in enumerate(blocks):
            at = jnp.bitwise_xor(place, step)
            whole = lax.dynamic_update_slice_in_dim(
                whole, block.reshape(CORES, 1, shard, -1), at, 1
            )
        return whole.reshape(CORES * nz * shard, -1)

    weights = jnp.concatenate([qkv_weight, extra, out_weight.T], axis=1)
    weights = in_core_order(weights, core_swap(weights))
    key_at = query_width + core * HEAD_SIZE
    value_at = key_at + KEY_VALUE_HEADS * HEAD_SIZE
    extra_at = qkv_weight.shape[1]
    out_at = extra_at + LANES + core * own_query
    weights = jnp.concatenate(
        [
            lax.dynamic_slice_in_dim(weights, core * own_query, own_query, 2),
            lax.dynamic_slice_in_dim(weights, key_at, HEAD_SIZE, 2),
            lax.dynamic_slice_in_dim(weights, value_at, HEAD_SIZE, 2),
            weights[:, :, extra_at : extra_at + LANES],
            lax.dynamic_slice_in_dim(weights, out_at, own_query, 2),
        ],
        axis=2,
    )
    def expert_rows(which):
        return (
            lax.dynamic_index_in_dim(gate_up_weight, which, 0, keepdims=False),
            lax.dynamic_index_in_dim(down_weight, which, 0, keepdims=False),
        )

    gu_mine, down_mine = expert_rows(core)
    gu_shard, down_shard = gu_mine.shape[0], down_mine.shape[0]
    received = core_swap(after(jnp.concatenate(expert_rows(other_core), axis=0), weights))
    gu_pair = in_core_order(gu_mine, received[:gu_shard]).reshape(CORES * gu_shard, -1)
    down_pair = in_core_order(down_mine, received[gu_shard:]).reshape(CORES * down_shard, -1)
    half_width = width // 2
    expert_halves = (
        jnp.concatenate([gu_pair[:, :hidden_units], down_pair[:, :half_width]], axis=0),
        jnp.concatenate([gu_pair[:, hidden_units:], down_pair[:, half_width:]], axis=0),
    )
    expert_first = plane_first(*expert_halves)

    weights_z = after(gather_z(weights), expert_first)
    block_rows = CORES * nz * shard
    half_query = own_query // 2
    group = 4 if nz % 4 == 0 else nz
    phased = group == nz
    qkv_z, out_z = weights_z[:, : own_width + LANES], weights_z[:, own_width + LANES :]
    qkv_halves = (qkv_z[:, :split], qkv_z[:, split:])
    out_halves = (out_z[:, :half_query], out_z[:, half_query:])

    expert_ids = jnp.arange(n_experts, dtype=jnp.int32)
    used = jnp.any(routes[0][:, :, None] == expert_ids[None, None, :], axis=1)
    marks = jnp.pad(
        used.astype(BF16), ((0, 0), (ROUTER_LANE, LANES - ROUTER_LANE - n_experts))
    )
    cot_rows = jnp.concatenate([grad_out.astype(BF16), marks], axis=1)
    cot_all = lax.all_gather(after(cot_rows, weights_z), "exp", axis=0, tiled=False)

    units = unit_rows(hidden, weights_z)
    units_other = core_swap(units)
    qkv_first, qkv_second = plane_first(*qkv_halves), plane_second(*qkv_halves)
    qkv_first, qkv_second, out_halves = after((qkv_first, qkv_second, out_halves), units_other)
    qkv_third = plane_third(qkv_first)
    w_all, extra_all = place_blocks(
        qkv_halves,
        (qkv_first, qkv_second, qkv_third),
        ((0, block_rows, 0, own_width), (0, block_rows, own_width, LANES)),
    )
    out_halves = after(out_halves, w_all)
    out_first, out_second = plane_first(*out_halves), plane_second(*out_halves)
    gain_one = extra_all[:, 0].astype(F32)
    gain_two = extra_all[:, 1].astype(F32)
    lanes = jnp.arange(LANES)
    is_router = (lanes >= ROUTER_LANE) & (lanes < ROUTER_LANE + n_experts)
    router_all = jnp.where(is_router[None, :], extra_all, 0)

    normed = jnp.concatenate([units, units_other], axis=0)
    normed = (normed.astype(F32) * gain_one).astype(BF16)
    packed_all, all_lengths = after((order[0], lengths[0]), weights_z)
    starts_all = doc_starts(packed_all, all_lengths)

    def own_first(values):
        y_place, y_rows = axis_place("y"), chip_rows
        parts = []
        for t in range(ny):
            at = lax.rem(y_place - t + ny, ny) * y_rows
            for which in (core, other_core):
                parts.append(lax.dynamic_slice_in_dim(values, at + which * rows, rows, 0))
        return jnp.concatenate(parts, axis=0)

    packed_keys, starts = own_first(packed_all), own_first(starts_all)[:chip_rows]
    packed = packed_keys[:chip_rows]
    cosine, sine = rotation_tables(packed - starts)
    bounds = jnp.concatenate(
        [starts[None, :], packed[None, :], jnp.zeros((6, chip_rows), jnp.int32)], axis=0
    )
    key_place = packed_keys[:, None]
    projected = dot(normed, w_all)
    key_value = jnp.concatenate(
        [
            rotate(projected[:, own_query : own_query + HEAD_SIZE], cosine, sine),
            projected[:, own_query + HEAD_SIZE : own_width],
        ],
        axis=1,
    ).astype(BF16)
    key_value = [key_value] + [shifted(key_value, "y", t) for t in range(1, ny)]
    out_first, expert_halves, projected, cot_all = after(
        (out_first, expert_halves, projected, cot_all), key_value, out_second
    )
    out_third = plane_third(out_first)
    cot_other = core_swap(cot_all)
    expert_second = plane_second(*expert_halves)
    query_rows, mixed, lse = attention_forward(
        projected, key_value, cosine, sine, key_place, bounds, heads
    )
    mixed, expert_first = after((mixed, expert_first), out_third, cot_other)
    expert_third = plane_third(after(expert_first, expert_second))
    (out_turned,) = place_blocks(
        out_halves, (out_first, out_second, out_third), ((0, block_rows, 0, own_query),)
    )
    middle = hidden + core_sum(dot_turned(mixed, out_turned))
    inner = norm_rows(middle, gain_two).astype(BF16)
    gate_up_all, down_all = place_blocks(
        expert_halves,
        (expert_first, expert_second, expert_third),
        (
            (0, CORES * gu_shard, 0, 2 * hidden_units),
            (CORES * gu_shard, CORES * down_shard, 0, width),
        ),
    )

    logits = jnp.where(marks > 0, dot(inner, extra_all), -jnp.inf)
    gates = jax.nn.softmax(logits, axis=-1)
    place_z = lax.axis_index("exp")
    own_expert = place_z * CORES + core

    def expert_group(inner_rows, from_place):
        buffers = []

        def run(index, chunk):
            scalars = jnp.stack([own_expert, jnp.bitwise_xor(from_place, index)])
            (mine, other), filled = expert_step(
                scalars.astype(jnp.int32),
                chunk,
                [cot_all, cot_other],
                gate_up_all,
                down_all,
                extra_all,
                index,
                4,
                buffers,
            )
            buffers[:] = filled
            return mine, other

        def joined(mine, other):
            return (mine.astype(F32) + other.astype(F32)).astype(BF16)

        rows_1, rows_2 = xor_shift(inner_rows, 1), xor_shift(inner_rows, 2)
        mine_0, other_0 = run(0, [inner_rows, core_swap(inner_rows)])

        rows_1, rows_2 = after((rows_1, rows_2), other_0)
        rows_3 = xor_shift(rows_2, 1)
        swapped = [core_swap(rows_1), core_swap(rows_2)]
        rows_1, other_1_rows, other_2_rows = after((rows_1, *swapped))
        other_0 = core_swap(other_0)
        mine_1, other_1 = run(1, [rows_1, other_1_rows])

        rows_2, other_1, mine_1 = after((rows_2, other_1, mine_1), other_0)
        other_1 = core_swap(other_1)
        back_1 = joined(mine_1, other_1)
        rows_2, rows_3 = after((rows_2, rows_3), back_1)
        near = xor_shift(back_1, 1)
        other_3_rows = core_swap(rows_3)
        mine_2, other_2 = run(2, [rows_2, other_2_rows])

        rows_3, other_2 = after((rows_3, other_2), other_3_rows)
        other_2 = core_swap(other_2)
        mine_3, other_3 = run(3, [rows_3, other_3_rows])

        mine_3, other_3 = after((mine_3, other_3), other_2, near)
        back_3 = joined(mine_3, core_swap(other_3))
        handed = xor_shift(back_3, 1)
        all_rows, all_cots, gated_all, grad_gates, grad_ups = after(buffers, back_3)
        if phased:
            grad_gate, grad_up = gate_up_grads(all_rows, grad_gates, grad_ups)
            grad_gate, grad_up, handed = after((grad_gate, grad_up, handed))
        mine_0, mine_2 = after((mine_0, mine_2), back_3)
        back_2 = joined(mine_2, other_2)
        (pair,) = line_pairs([None, None, back_2, None], [handed])
        if phased:
            grad_gate, gated_all, pair = after((grad_gate, gated_all, pair), gates)
        pieces = [pair[: rows // 2], pair[rows // 2 :]]
        moved, received = xor_shift(pieces[0], 2), []
        if phased:
            weight_grads = expert_weight_grads(grad_gate, grad_up, all_cots, gated_all)
            weight_grads, gated_all, moved, pieces = after((weight_grads, gated_all, moved, pieces))
            received = plane_moved_part(weight_grads, True)
        else:
            weight_grads = (
                dot_rows(all_rows, grad_gates),
                dot_rows(all_rows, grad_ups),
                dot_rows(gated_all, all_cots),
            )
        moved_more = xor_shift(pieces[1], 2)
        back_0 = joined(mine_0, other_0)
        outs, outs_other = expert_results(gated_all, down_all)
        outs, outs_other, moved_more, received, weight_grads = after(
            (outs, outs_other, moved_more, received, weight_grads), back_0
        )
        if phased:
            received = plane_joined(plane_moved_part(weight_grads, False), received)
        outs_other = core_swap(outs_other)
        outs = [
            (outs[half].astype(F32) + outs_other[half].astype(F32)).astype(BF16)
            for half in (slice(0, 2 * rows), slice(2 * rows, 4 * rows))
        ]
        return (back_0, near, (moved, moved_more)), outs, weight_grads, received

    if phased:
        backs, outs, expert_grads, expert_received = expert_group(inner, place_z)
    else:

        def visit(turn, state):
            inner_here, back, out, sums = state
            more_back, outs, more, _ = expert_group(
                inner_here, lax.rem(place_z + turn * group, nz)
            )
            back = back + more_back[0].astype(F32) + more_back[1].astype(F32)
            back = back + jnp.concatenate(more_back[2], axis=0).astype(F32)
            odd, even = (o.reshape(2, rows, width) for o in outs)
            out = out + line_scatter([even[0], odd[0], even[1], odd[1]])[0]
            sums = tuple(a + b for a, b in zip(sums, more))
            return (*(shifted(v, "exp", nz - group) for v in (inner_here, back, out)), sums)

        sums = (
            jnp.zeros((width, hidden_units), F32),
            jnp.zeros((width, hidden_units), F32),
            jnp.zeros((hidden_units, width), F32),
        )
        start = (jnp.zeros((rows, width + LANES), F32), jnp.zeros((rows, width), F32), sums)
        _, back, moe, sums = lax.fori_loop(0, nz // group, visit, (inner, *start))
        backs = (back,)
        gate, up, down = (w.astype(BF16) for w in sums)
        gate, up = (w.reshape(nx, ny, CORES * gu_shard, hidden_units) for w in (gate, up))
        down = down.reshape(nx, ny, CORES * down_shard, width)
        expert_grads = [
            plane_blocks([gate, down[..., :half_width]], PLANE_AXES[0]),
            plane_blocks([up, down[..., half_width:]], PLANE_AXES[1]),
        ]
        expert_received = plane_joined(
            plane_moved_part(expert_grads, False), plane_moved_part(expert_grads, True)
        )
    gu_block = CORES * gu_shard

    if phased:
        results_handed = xor_shift(outs[0][rows:], 1)

    grad_middle, grad_branch, ffn_terms, grad_logits = middle_backward(
        backs, gates, middle, gain_two[None, :], router_all, grad_out
    )
    grad_branch = [grad_branch, core_swap(grad_branch)]
    blended_gradient, out_grads = branch_backward(grad_branch, mixed, out_turned)
    if phased:
        blended_gradient = after(blended_gradient, outs[0])
    grad_query, grad_kv_own, *grad_kv_parts = attention_backward(
        query_rows, blended_gradient, lse, key_value, cosine, sine, key_place, bounds, heads
    )

    if phased:
        grad_query, grad_kv_own, grad_kv_parts, results_handed = after(
            (grad_query, grad_kv_own, grad_kv_parts, results_handed)
        )
    grad_kv_parts = [shifted(part, "y", ny - t) for t, part in enumerate(grad_kv_parts, 1)]
    out_grads = after(out_grads, grad_kv_parts)
    out_received = plane_moved(out_grads)
    if phased:
        pair = (outs[1][rows:].astype(F32) + results_handed.astype(F32)).astype(BF16)
        cut = rows // 4
        moe_far = [xor_shift(pair[:cut], 2)]
        results_near = xor_shift(after(outs[0][:rows], pair), 1)

    for part in grad_kv_parts:
        grad_kv_own = grad_kv_own + part.astype(F32)
    grad_key_value = jnp.concatenate(
        [rotate(grad_kv_own[:, :HEAD_SIZE], cosine, -sine), grad_kv_own[:, HEAD_SIZE:]], axis=1
    ).astype(BF16)
    if phased:
        grad_key_value = after(grad_key_value, pair)
    is_ffn = (lax.broadcasted_iota(jnp.int32, (rows, LANES), 1) == 1).astype(BF16)
    grad_normed, grad_normed_other, qkv_grads = projection_backward(
        normed,
        [units, units_other],
        w_all,
        grad_query,
        grad_key_value,
        split,
        [ffn_terms, inner],
        jnp.concatenate([is_ffn, grad_logits], axis=0),
    )
    if phased:
        qkv_grads, moe_far, pair = after((qkv_grads, moe_far, pair))
        moe_far.append(xor_shift(pair[cut:], 2))
    qkv_grads, out_received = after((qkv_grads, out_received))

    def line_sum(first, second):
        summed = jnp.concatenate([first, second], axis=1).astype(BF16)
        summed = summed.reshape(CORES, nz, shard, -1)
        place = lax.axis_index("exp")
        return line_scatter(
            [
                lax.dynamic_index_in_dim(summed, jnp.bitwise_xor(place, step), 1, keepdims=False)
                for step in range(nz)
            ]
        )

    def of_core(value, which):
        return lax.dynamic_index_in_dim(value, which, 0, keepdims=False)

    qkv_received = plane_moved(qkv_grads)
    qkv_hand_on = plane_hand_on(qkv_grads, qkv_received)
    qkv_handed = plane_handed(qkv_hand_on)
    expert_received = after(expert_received, qkv_grads)
    expert_hand_on = plane_hand_on(expert_grads, expert_received)
    out_received = after(out_received, qkv_hand_on)
    out_handed = plane_handed(plane_hand_on(out_grads, out_received))
    if phased:
        moe_far, results_near = after((moe_far, results_near), qkv_hand_on)
        moe = outs[1][:rows].astype(F32) + results_near.astype(F32)
        moe = moe + jnp.concatenate(moe_far, axis=0).astype(F32)
    grad_normed_other = after(grad_normed_other, qkv_hand_on)
    grad_normed = grad_normed + core_swap(grad_normed_other).astype(F32)
    grad_hidden_norm, _ = norm_back(hidden, gain_one, grad_normed)
    grad_input = grad_middle + grad_hidden_norm
    output = middle + moe
    expert_handed = plane_handed(after(expert_hand_on, out_handed))
    qkv_sum, qkv_pairs = line_sum(*plane_sum(qkv_grads, qkv_received, qkv_handed))
    out_handed = after(out_handed, qkv_handed)
    out_sum, out_pairs = line_sum(*plane_sum(out_grads, out_received, out_handed))
    expert_handed = after(expert_handed, qkv_pairs, out_pairs)
    out_other = core_swap(of_core(out_sum, other_core).astype(BF16)).astype(F32)
    out_sum = in_core_order(of_core(out_sum, core), out_other)
    grad_out_proj = out_sum.swapaxes(0, 1).reshape(shard, query_width).T

    first_sum, second_sum = plane_sum(expert_grads, expert_received, expert_handed)
    gu_sum = jnp.concatenate([first_sum[:gu_block], second_sum[:gu_block]], axis=1)
    down_sum = jnp.concatenate([first_sum[gu_block:], second_sum[gu_block:]], axis=1)
    gu_sum = gu_sum.reshape(CORES, gu_shard, 2 * hidden_units)
    down_sum = down_sum.reshape(CORES, down_shard, width)
    to_other = jnp.concatenate([of_core(gu_sum, other_core), of_core(down_sum, other_core)], 0)
    to_other = to_other.astype(BF16)
    qkv_sum = after(qkv_sum, to_other)
    received = core_swap(to_other).astype(F32)
    grad_gate_up = in_core_order(of_core(gu_sum, core), received[:gu_shard])
    grad_down = in_core_order(of_core(down_sum, core), received[gu_shard:])

    qkv_other = core_swap(of_core(qkv_sum, other_core).astype(BF16)).astype(F32)
    qkv_mine = of_core(qkv_sum, core)
    extra_sum = qkv_mine[:, own_width:] + qkv_other[:, own_width:]
    pair = in_core_order(qkv_mine[:, :own_width], qkv_other[:, :own_width])
    key_at, value_at = own_query, own_query + HEAD_SIZE
    grad_qkv = jnp.concatenate(
        [
            pair[:, :, :key_at].swapaxes(0, 1).reshape(shard, -1),
            pair[:, :, key_at:value_at].swapaxes(0, 1).reshape(shard, -1),
            pair[:, :, value_at:].swapaxes(0, 1).reshape(shard, -1),
        ],
        axis=1,
    )
    return (
        output[None],
        grad_input[None],
        extra_sum[:, 0],
        grad_qkv,
        grad_out_proj,
        extra_sum[:, 1],
        extra_sum[:, 2 : 2 + n_experts],
        grad_gate_up,
        grad_down,
    )


def solution(mesh):
    return jax.shard_map(
        on_device,
        mesh=mesh,
        in_specs=(
            P(("dp", "exp"), "ctx", None),
            P(("dp", "exp"), None),
            P(("dp", "exp"), None),
            P(("dp", "exp"), "ctx", None),
            P(("dp", "exp"), "ctx", None),
            P(("dp", "ctx", "exp")),
            P(("dp", "ctx", "exp"), None),
            P(None, ("dp", "ctx", "exp")),
            P(("dp", "ctx", "exp")),
            P(("dp", "ctx", "exp"), None),
            P("exp", ("dp", "ctx"), None),
            P("exp", ("dp", "ctx"), None),
        ),
        out_specs=(
            P(("dp", "exp"), "ctx", None),
            P(("dp", "exp"), "ctx", None),
            P(("dp", "ctx", "exp")),
            P(("dp", "ctx", "exp"), None),
            P(None, ("dp", "ctx", "exp")),
            P(("dp", "ctx", "exp")),
            P(("dp", "ctx", "exp"), None),
            P("exp", ("dp", "ctx"), None),
            P("exp", ("dp", "ctx"), None),
        ),
        check_vma=False,
    )
```

```python
import math

import jax
import jax.numpy as jnp
from jax import lax
from jax.experimental import pallas as pl
from jax.experimental.pallas import tpu as pltpu
from jax.sharding import PartitionSpec as P

QUERY_HEADS = 12
KEY_VALUE_HEADS = 2
HEAD_SIZE = 128
TOP = 4
CORES = 2
LANES = 128
ROUTER_LANE = 2


EPS = 1e-06
BASE = 1000000.0
BF16 = jnp.bfloat16
F32 = jnp.float32


def norm_rows(v, gain):
    return v * lax.rsqrt(jnp.mean(v * v, axis=-1, keepdims=True) + EPS) * gain


def norm_back(v, gain, grad):
    root = lax.rsqrt(jnp.mean(v * v, axis=-1, keepdims=True) + EPS)
    unit = v * root
    scaled = grad * gain
    along = jnp.mean(scaled * unit, axis=-1, keepdims=True)
    return root * (scaled - unit * along), (grad * unit).astype(BF16)


def rotation_tables(slot_position):
    half = HEAD_SIZE // 2
    freq = jnp.exp(jnp.arange(half, dtype=F32) * (-2.0 * math.log(BASE) / HEAD_SIZE))
    angle = slot_position.astype(F32)[:, None] * freq[None, :]
    cosine, sine = jnp.cos(angle), jnp.sin(angle)
    return jnp.concatenate([cosine, cosine], axis=1), jnp.concatenate([-sine, sine], axis=1)


def rotate(t, cosine, sine):
    half = HEAD_SIZE // 2
    return t * cosine + jnp.concatenate([t[:, half:], t[:, :half]], axis=1) * sine


def doc_starts(packed, lengths):
    ends = jnp.cumsum(lengths)
    return jnp.max(jnp.where(packed[:, None] >= ends[None, :], ends[None, :], 0), axis=1)


def dot(a, b):
    return jnp.dot(a, b, preferred_element_type=F32)


def dot_turned(a, b):
    return lax.dot_general(a, b, (((1,), (1,)), ((), ())), preferred_element_type=F32)


def dot_rows(a, b):
    return lax.dot_general(a, b, (((0,), (0,)), ((), ())), preferred_element_type=F32)


def after(value, *others):
    values, tree = jax.tree.flatten(value)
    others = jax.tree.leaves(others)

    def kernel(*refs):
        pass

    anywhere = pl.BlockSpec(memory_space=pl.ANY)
    tied = pl.pallas_call(
        kernel,
        out_shape=[jax.ShapeDtypeStruct(v.shape, v.dtype) for v in values],
        in_specs=[anywhere] * (len(values) + len(others)),
        out_specs=[anywhere] * len(values),
        input_output_aliases={i: i for i in range(len(values))},
        cost_estimate=pl.CostEstimate(flops=1, bytes_accessed=1, transcendentals=0),
        name="after",
    )(*values, *others)
    return jax.tree.unflatten(tree, tied)


def axis_len(axis):
    if axis == "y":
        return lax.axis_size("ctx") // CORES
    return lax.axis_size(axis)


def axis_place(axis):
    if axis == "y":
        return lax.axis_index("ctx") // CORES
    return lax.axis_index(axis)


def shifted(value, axis, step):
    name, stride = ("ctx", CORES) if axis == "y" else (axis, 1)
    n = lax.axis_size(name)
    return lax.ppermute(value, name, [(i, (i + step * stride) % n) for i in range(n)])


def core_swap(value):
    n = lax.axis_size("ctx")
    return lax.ppermute(value, "ctx", [(i, i ^ 1) for i in range(n)])


def both_cores(value):
    return jnp.concatenate([value, core_swap(value)], axis=0)


def core_sum(value):
    half = value.shape[0] // 2
    other = core_swap(value[half:].astype(BF16))
    return value[:half].astype(F32) + other.astype(F32)


def in_core_order(mine, other):
    core = lax.axis_index("ctx") % CORES
    return jnp.where(core == 0, jnp.stack([mine, other]), jnp.stack([other, mine]))


def plane_first(first, second):
    nx, ny = axis_len("dp"), axis_len("y")
    return (
        {(s, 0): shifted(first, "dp", s) for s in range(1, nx)},
        {(0, t): shifted(second, "y", t) for t in range(1, ny)},
    )


def plane_second(first, second):
    nx, ny = axis_len("dp"), axis_len("y")
    return (
        {(0, t): shifted(first, "y", t) for t in range(1, ny)},
        {(s, 0): shifted(second, "dp", s) for s in range(1, nx)},
    )


def plane_third(came):
    nx, ny = axis_len("dp"), axis_len("y")
    return (
        {(s, t): shifted(came[0][s, 0], "y", t) for s in range(1, nx) for t in range(1, ny)},
        {(s, t): shifted(came[1][0, t], "dp", s) for s in range(1, nx) for t in range(1, ny)},
    )


def place_blocks(halves, came, parts):
    nx, ny = axis_len("dp"), axis_len("y")
    steps = [(s, t) for s in range(nx) for t in range(ny)]
    blocks = []
    for k, half in enumerate(halves):
        known = {(0, 0): half}
        for pair in came:
            known.update(pair[k])
        blocks.append([known[step] for step in steps])

    def kernel(place_ref, *refs):
        first_refs, second_refs = refs[: len(steps)], refs[len(steps) : 2 * len(steps)]
        outs = refs[2 * len(steps) :]
        at = pl.program_id(0)
        x_step = lax.rem(place_ref[0] - at // ny + nx, nx)
        y_step = lax.rem(place_ref[1] - at % ny + ny, ny)
        left = first_refs[0].shape[1]
        for step, first, second in zip(steps, first_refs, second_refs):

            @pl.when((x_step == step[0]) & (y_step == step[1]))
            def _(first=first, second=second):
                for (row, n_rows, column, columns), out in zip(parts, outs):
                    for block, low, high in (
                        (first, 0, left),
                        (second, left, left + second.shape[1]),
                    ):
                        begin, end = max(column, low), min(column + columns, high)
                        if begin < end:
                            out[:, begin - column : end - column] = block[
                                row : row + n_rows, begin - low : end - low
                            ]

    whole = [pl.BlockSpec(v.shape, lambda i, place_ref: (0, 0)) for v in (*blocks[0], *blocks[1])]
    return pl.pallas_call(
        kernel,
        grid_spec=pltpu.PrefetchScalarGridSpec(
            num_scalar_prefetch=1,
            grid=(nx * ny,),
            in_specs=whole,
            out_specs=[
                pl.BlockSpec((n_rows, columns), lambda i, place_ref: (i, 0))
                for _, n_rows, _, columns in parts
            ],
        ),
        out_shape=[
            jax.ShapeDtypeStruct((nx * ny * n_rows, columns), BF16)
            for _, n_rows, _, columns in parts
        ],
        compiler_params=pltpu.CompilerParams(vmem_limit_bytes=48 * 1024 * 1024),
        cost_estimate=pl.CostEstimate(flops=1, bytes_accessed=1, transcendentals=0),
        name="place_blocks",
    )(jnp.stack([axis_place("dp"), axis_place("y")]).astype(jnp.int32), *blocks[0], *blocks[1])


def xor_shift(value, step):
    n = lax.axis_size("exp")
    return lax.ppermute(value, "exp", [(i, i ^ step) for i in range(n)])


def line_gather(value, n, *waits):
    blocks = [value]
    for step in range(1, n):
        if step % 2 == 1:
            handed = blocks[step - 1]
            if waits and step > 1:
                handed = blocks[step - 1] = after(handed, *waits)
            blocks.append(xor_shift(handed, 1))
        else:
            blocks.append(xor_shift(value, step))
    return blocks


def line_pairs(blocks, handed):
    return [
        (blocks[step].astype(F32) + other.astype(F32)).astype(BF16)
        for step, other in zip(range(2, len(blocks), 2), handed)
    ]


def line_far(blocks, near, pairs):
    total = blocks[0].astype(F32) + near.astype(F32)
    for step, pair in zip(range(2, len(blocks), 2), pairs):
        total = total + xor_shift(pair, step).astype(F32)
    return total


def line_scatter(blocks):
    odd = xor_shift(jnp.stack(blocks[1::2]), 1)
    pairs = line_pairs(blocks, odd[1:])
    return line_far(blocks, odd[0], pairs), pairs


PLANE_AXES = (("dp", "y"), ("y", "dp"))


def plane_places():
    return jnp.stack([axis_place("dp"), axis_place("y")]).astype(jnp.int32)


def plane_blocks(parts, axes):
    half = []
    for near in range(axis_len(axes[0])):
        blocks = []
        for far in range(axis_len(axes[1])):
            s, t = (near, far) if axes[0] == "dp" else (far, near)
            x = lax.rem(axis_place("dp") + s, axis_len("dp"))
            y = lax.rem(axis_place("y") + t, axis_len("y"))
            taken = [
                lax.dynamic_slice(part, (x, y, 0, 0), (1, 1, *part.shape[2:])).reshape(
                    part.shape[2:]
                )
                for part in parts
            ]
            blocks.append(jnp.concatenate(taken, axis=0))
        half.append(blocks)
    return half


def plane_moved(halves):
    return [
        [shifted(blocks, axes[0], near) for near, blocks in enumerate(half) if near > 0]
        for half, axes in zip(halves, PLANE_AXES)
    ]


def plane_moved_part(halves, handed_on):
    return [
        [
            [shifted(block, axes[0], near) for block in (blocks[1:] if handed_on else blocks[:1])]
            for near, blocks in enumerate(half)
            if near > 0
        ]
        for half, axes in zip(halves, PLANE_AXES)
    ]


def plane_joined(stay, handed_on):
    return [[a + b for a, b in zip(*half)] for half in zip(stay, handed_on)]


def half_sum(half, received, far):
    total = half[0][far].astype(F32)
    for blocks in received:
        total = total + blocks[far].astype(F32)
    return total


def plane_hand_on(halves, received):
    return [
        [half_sum(half, came, far).astype(BF16) for far in range(1, len(half[0]))]
        for half, came in zip(halves, received)
    ]


def plane_handed(handed):
    return [
        [shifted(block, axes[1], far) for far, block in enumerate(blocks, 1)]
        for blocks, axes in zip(handed, PLANE_AXES)
    ]


def plane_sum(halves, received, handed):
    sums = []
    for half, came, last in zip(halves, received, handed):
        total = half_sum(half, came, 0)
        for block in last:
            total = total + block.astype(F32)
        sums.append(total)
    return sums


def half_shapes(shapes):
    counts = [(axis_len(axes[0]), axis_len(axes[1])) for axes in PLANE_AXES]
    return [(far, *shape) for (near, far), shape in zip(counts, shapes) for _ in range(near)]


def two_halves(arrays):
    n = axis_len("dp")
    return [list(arrays[:n]), list(arrays[n:])]


def store_blocks(place_ref, at, outs, first, second):
    nx, ny = axis_len("dp"), axis_len("y")
    x_step, y_step = step_to(place_ref, at)
    for s in range(nx):

        @pl.when(x_step == s)
        def _(s=s):
            first(outs[s].at[y_step])

    for t in range(ny):

        @pl.when(y_step == t)
        def _(t=t):
            second(outs[nx + t].at[x_step])


def blocks_a_step(block_rows):
    n = 1
    while n * block_rows % LANES != 0:
        n += 1
    return n


def step_to(place_ref, at):
    nx, ny = axis_len("dp"), axis_len("y")
    return lax.rem(at // ny - place_ref[0] + nx, nx), lax.rem(at % ny - place_ref[1] + ny, ny)


SMALL = pl.CostEstimate(flops=1, bytes_accessed=1, transcendentals=0)
LOG2_E = 1.4426950408889634
GELU_ROOT = math.sqrt(2.0 / math.pi)
GELU_CUBE = 0.044715
ROW_TILE = 512


def kernel_params(n_axes=1):
    return pltpu.CompilerParams(
        dimension_semantics=("arbitrary",) * n_axes, vmem_limit_bytes=56 * 1024 * 1024
    )


def contract(a, b, a_dim, b_dim):
    return lax.dot_general(a, b, (((a_dim,), (b_dim,)), ((), ())), preferred_element_type=F32)


def turned(t, cosine, sine):
    return t * cosine + pltpu.roll(t, HEAD_SIZE // 2, 1) * sine


def fill_keys(parts, keys_ref, values_ref):
    for i, part in enumerate(parts):
        n = part.shape[0]
        keys_ref[i * n : (i + 1) * n, :] = part[:, :HEAD_SIZE]
        values_ref[i * n : (i + 1) * n, :] = part[:, HEAD_SIZE:]


def fill_bias(key_place_ref, bounds_ref, bias_ref):
    place = key_place_ref[...]
    allowed = (place >= bounds_ref[0:1, :]) & (place <= bounds_ref[1:2, :])
    bias_ref[...] = jnp.where(allowed, 0.0, -1e30)


def unit_rows(rows, *waits):
    def kernel(rows_ref, *refs):
        value = rows_ref[...]
        root = lax.rsqrt(jnp.mean(value * value, axis=-1, keepdims=True) + EPS)
        refs[-1][...] = (value * root).astype(BF16)

    return pl.pallas_call(
        kernel,
        in_specs=[pl.BlockSpec(memory_space=pltpu.VMEM)]
        + [pl.BlockSpec(memory_space=pl.ANY)] * len(waits),
        out_specs=pl.BlockSpec(memory_space=pltpu.VMEM),
        out_shape=jax.ShapeDtypeStruct(rows.shape, BF16),
        compiler_params=pltpu.CompilerParams(vmem_limit_bytes=32 * 1024 * 1024),
        cost_estimate=SMALL,
        name="unit_rows",
    )(rows, *waits)


def attention_forward(projected, key_value, cosine, sine, key_place, bounds, heads, *waits):
    rows = projected.shape[0]
    n_keys = key_place.shape[0]
    n_parts = len(key_value)
    factor = HEAD_SIZE ** (-0.5) * LOG2_E

    def kernel(projected_ref, cos_ref, sin_ref, place_ref, bounds_ref, *refs):
        parts = refs[:n_parts]
        query_ref, mixed_ref, lse_ref, keys_ref, values_ref, bias_ref = refs[n_parts + len(waits) :]
        head = pl.program_id(0)

        @pl.when(head == 0)
        def _():
            fill_keys(parts, keys_ref, values_ref)
            fill_bias(place_ref, bounds_ref, bias_ref)

        for start in range(0, rows, ROW_TILE):
            tile = slice(start, start + ROW_TILE)
            query = turned(projected_ref[tile, :], cos_ref[tile, :], sin_ref[tile, :]).astype(BF16)
            query_ref[tile, :] = query
            scores = contract(keys_ref[...], query, 1, 1) * factor + bias_ref[:, tile]
            top = jnp.max(scores, axis=0, keepdims=True)
            weights = jnp.exp2(scores - top)
            total = jnp.sum(weights, axis=0, keepdims=True)
            probs = (weights * (1.0 / total)).astype(BF16)
            mixed_ref[tile, :] = contract(probs, values_ref[...], 0, 0).astype(BF16)
            lse_ref[pl.ds(head, 1), tile] = top + jnp.log2(total)

    def fixed(shape):
        return pl.BlockSpec(shape, lambda h: (0,) * len(shape))

    by_head = pl.BlockSpec((rows, HEAD_SIZE), lambda h: (0, h))
    return pl.pallas_call(
        kernel,
        grid=(heads,),
        in_specs=[
            by_head,
            fixed(cosine.shape),
            fixed(sine.shape),
            fixed(key_place.shape),
            fixed(bounds.shape),
        ]
        + [fixed(p.shape) for p in key_value]
        + [pl.BlockSpec(memory_space=pl.ANY)] * len(waits),
        out_specs=[by_head, by_head, fixed((8, rows))],
        out_shape=[
            jax.ShapeDtypeStruct((rows, heads * HEAD_SIZE), BF16),
            jax.ShapeDtypeStruct((rows, heads * HEAD_SIZE), BF16),
            jax.ShapeDtypeStruct((8, rows), F32),
        ],
        scratch_shapes=[
            pltpu.VMEM((n_keys, HEAD_SIZE), BF16),
            pltpu.VMEM((n_keys, HEAD_SIZE), BF16),
            pltpu.VMEM((n_keys, rows), F32),
        ],
        compiler_params=kernel_params(),
        cost_estimate=SMALL,
        name="attention_forward",
    )(projected, cosine, sine, key_place, bounds, *key_value, *waits)


def attention_backward(
    query, head_gradient, lse, key_value, cosine, sine, key_place, bounds, heads
):
    rows = query.shape[0]
    n_keys = key_place.shape[0]
    n_parts = len(key_value)
    scale = HEAD_SIZE ** (-0.5)
    factor = scale * LOG2_E

    def kernel(query_ref, grad_ref, lse_ref, cos_ref, sin_ref, place_ref, bounds_ref, *refs):
        parts = refs[:n_parts]
        out_ref = refs[n_parts]
        part_outs = refs[n_parts + 1 : 2 * n_parts + 1]
        keys_ref, values_ref, bias_ref, grad_keys_ref, grad_values_ref = refs[2 * n_parts + 1 :]
        head = pl.program_id(0)

        @pl.when(head == 0)
        def _():
            fill_keys(parts, keys_ref, values_ref)
            fill_bias(place_ref, bounds_ref, bias_ref)
            grad_keys_ref[...] = jnp.zeros_like(grad_keys_ref)
            grad_values_ref[...] = jnp.zeros_like(grad_values_ref)

        for start in range(0, rows, ROW_TILE):
            tile = slice(start, start + ROW_TILE)
            query, grad = query_ref[tile, :], grad_ref[tile, :]
            scores = contract(keys_ref[...], query, 1, 1) * factor + bias_ref[:, tile]
            probs = jnp.exp2(scores - lse_ref[pl.ds(head, 1), tile])
            weighted = probs * contract(values_ref[...], grad, 1, 1)
            offset = jnp.sum(weighted, axis=0, keepdims=True)
            grad_scores = (weighted - probs * offset).astype(BF16)
            grad_keys_ref[...] += contract(grad_scores, query, 1, 0)
            grad_values_ref[...] += contract(probs.astype(BF16), grad, 1, 0)
            grad_query = contract(grad_scores, keys_ref[...], 0, 0) * scale
            out_ref[tile, :] = turned(grad_query, cos_ref[tile, :], -sin_ref[tile, :]).astype(BF16)

        @pl.when(head == heads - 1)
        def _():
            for i, out in enumerate(part_outs):
                n = out.shape[0]
                out[:, :HEAD_SIZE] = (grad_keys_ref[i * n : (i + 1) * n, :] * scale).astype(out.dtype)
                out[:, HEAD_SIZE:] = grad_values_ref[i * n : (i + 1) * n, :].astype(out.dtype)

    def fixed(shape):
        return pl.BlockSpec(shape, lambda h: (0,) * len(shape))

    by_head = pl.BlockSpec((rows, HEAD_SIZE), lambda h: (0, h))
    return pl.pallas_call(
        kernel,
        grid=(heads,),
        in_specs=[
            by_head,
            by_head,
            fixed(lse.shape),
            fixed(cosine.shape),
            fixed(sine.shape),
            fixed(key_place.shape),
            fixed(bounds.shape),
        ]
        + [fixed(p.shape) for p in key_value],
        out_specs=[by_head] + [fixed(p.shape) for p in key_value],
        out_shape=[jax.ShapeDtypeStruct((rows, heads * HEAD_SIZE), BF16)]
        + [
            jax.ShapeDtypeStruct(p.shape, F32 if i == 0 else BF16)
            for i, p in enumerate(key_value)
        ],
        scratch_shapes=[
            pltpu.VMEM((n_keys, HEAD_SIZE), BF16),
            pltpu.VMEM((n_keys, HEAD_SIZE), BF16),
            pltpu.VMEM((n_keys, rows), F32),
            pltpu.VMEM((n_keys, HEAD_SIZE), F32),
            pltpu.VMEM((n_keys, HEAD_SIZE), F32),
        ],
        compiler_params=kernel_params(),
        cost_estimate=SMALL,
        name="attention_backward",
    )(query, head_gradient, lse, cosine, sine, key_place, bounds, *key_value)


def expert_step(scalars, chunk, cot, gate_up, down, router, index, n_steps, buffers):
    rows, width = chunk[0].shape
    units = down.shape[0]
    n_chunk = len(chunk)
    n_rows = n_chunk * rows
    half_lanes = LANES // 2
    places = [slice(i * rows, (i + 1) * rows) for i in range(n_chunk)]

    def kernel(scalar_ref, router_ref, *refs):
        chunk_refs, cot_refs = refs[:n_chunk], refs[n_chunk : 2 * n_chunk]
        gate_up_ref, down_ref = refs[2 * n_chunk : 2 * n_chunk + 2]
        refs = refs[2 * n_chunk + 2 + len(buffers) :]
        part_outs, buffer_outs = refs[:n_chunk], refs[n_chunk : n_chunk + 5]
        row, cots, gate_w, up_w, down_w, part, gated, grad_gates, grad_ups, in_sems, out_sems = refs[
            n_chunk + 5 :
        ]
        loads, stores = [], []

        def load(source, target):
            copy = pltpu.make_async_copy(source, target, in_sems.at[len(loads)])
            copy.start()
            loads.append(copy)

        def store(source, target):
            copy = pltpu.make_async_copy(source, target, out_sems.at[len(stores)])
            copy.start()
            stores.append(copy)

        for ref, at in zip(chunk_refs, places):
            load(ref, row.at[at])
        load(gate_up_ref.at[:, :units], gate_w)
        load(gate_up_ref.at[:, units:], up_w)
        for ref, at in zip(cot_refs, places):
            load(ref.at[scalar_ref[1]], cots.at[at])
        load(down_ref, down_w)
        in_buffer = [slice(index * n_rows + at.start, index * n_rows + at.stop) for at in places]

        for copy in loads[: n_chunk + 1]:
            copy.wait()
        store(row, buffer_outs[0].at[index * n_rows : (index + 1) * n_rows])
        gates = [jnp.dot(row[at, :], gate_w[...], preferred_element_type=F32) for at in places]
        loads[n_chunk + 1].wait()
        ups = [jnp.dot(row[at, :], up_w[...], preferred_element_type=F32) for at in places]
        for copy in loads[n_chunk + 2 :]:
            copy.wait()
        store(cots.at[:, :width], buffer_outs[1].at[index * n_rows : (index + 1) * n_rows])

        lane = lax.broadcasted_iota(jnp.int32, (rows, LANES), 1)
        for at, gate, up, out, buffer_at in zip(places, gates, ups, part_outs, in_buffer):
            logits = jnp.dot(row[at, :], router_ref[...], preferred_element_type=F32)
            logits = jnp.where(cots[at, width:].astype(F32) > 0, logits, -jnp.inf)
            top = jnp.max(logits, axis=1, keepdims=True)
            weights = jnp.exp(logits - top)
            total = jnp.sum(weights, axis=1, keepdims=True)
            own = jnp.where(lane == scalar_ref[0] + ROUTER_LANE, weights, 0.0)
            weight = jnp.sum(own, axis=1, keepdims=True) / total

            grad_act = contract(cots[at, :width], down_w[...], 1, 1)
            square = gate * gate
            curve = jnp.tanh(GELU_ROOT * gate * (1.0 + GELU_CUBE * square))
            lifted = 0.5 + 0.5 * curve
            gelu = gate * lifted
            slope = lifted + (0.5 * GELU_ROOT) * gate * (1.0 - curve * curve) * (
                1.0 + (3.0 * GELU_CUBE) * square
            )
            act = gelu * up
            share = jnp.sum(act * grad_act, axis=1, keepdims=True)
            gated[at, :] = (act * weight).astype(BF16)
            grad_act = grad_act * weight
            grad_up = (grad_act * gelu).astype(BF16)
            grad_gate = (grad_act * up * slope).astype(BF16)
            grad_gates[at, :] = grad_gate
            grad_ups[at, :] = grad_up
            for source, target in zip((gated, grad_gates, grad_ups), buffer_outs[2:]):
                store(source.at[at], target.at[buffer_at])
            grad_row = contract(grad_gate, gate_w[...], 1, 1) + contract(grad_up, up_w[...], 1, 1)
            part[at, :width] = grad_row.astype(BF16)
            high = share.astype(BF16).astype(F32)
            part[at, width:] = jnp.where(
                lane == scalar_ref[0],
                high,
                jnp.where(lane == scalar_ref[0] + half_lanes, share - high, 0.0),
            ).astype(BF16)
            store(part.at[at], out)
        for copy in stores:
            copy.wait()

    anywhere = pl.BlockSpec(memory_space=pl.ANY)
    first_buffer = 2 + 2 * n_chunk + 2
    outs = pl.pallas_call(
        kernel,
        in_specs=[pl.BlockSpec(memory_space=pltpu.SMEM), pl.BlockSpec(memory_space=pltpu.VMEM)]
        + [anywhere] * (2 * n_chunk + 2 + len(buffers)),
        out_specs=[anywhere] * (n_chunk + 5),
        out_shape=[jax.ShapeDtypeStruct((rows, width + LANES), BF16)] * n_chunk
        + [jax.ShapeDtypeStruct((n_steps * n_rows, width), BF16)] * 2
        + [jax.ShapeDtypeStruct((n_steps * n_rows, units), BF16)] * 3,
        input_output_aliases={first_buffer + i: n_chunk + i for i in range(len(buffers))},
        scratch_shapes=[
            pltpu.VMEM((n_rows, width), BF16),
            pltpu.VMEM((n_rows, width + LANES), BF16),
            pltpu.VMEM((width, units), BF16),
            pltpu.VMEM((width, units), BF16),
            pltpu.VMEM((units, width), BF16),
            pltpu.VMEM((n_rows, width + LANES), BF16),
        ]
        + [pltpu.VMEM((n_rows, units), BF16)] * 3
        + [
            pltpu.SemaphoreType.DMA((2 * n_chunk + 3,)),
            pltpu.SemaphoreType.DMA((4 * n_chunk + 2,)),
        ],
        compiler_params=pltpu.CompilerParams(vmem_limit_bytes=56 * 1024 * 1024),
        cost_estimate=SMALL,
        name="expert_step",
    )(scalars, router, *chunk, *cot, gate_up, down, *buffers)
    return outs[:n_chunk], outs[n_chunk:]


def gate_up_grads(rows, grad_gate, grad_up):
    n_rows, width = rows.shape
    units = grad_gate.shape[1]
    tile = 256

    def kernel(rows_ref, gate_ref, up_ref, gate_out, up_out):
        for right, out in ((gate_ref, gate_out), (up_ref, up_out)):
            out[...] = contract(rows_ref[...], right[...], 0, 0).astype(BF16)

    whole = pl.BlockSpec((n_rows, units), lambda j: (0, 0))
    out = pl.BlockSpec((tile, units), lambda j: (j, 0))
    return pl.pallas_call(
        kernel,
        grid=(width // tile,),
        in_specs=[pl.BlockSpec((n_rows, tile), lambda j: (0, j)), whole, whole],
        out_specs=[out, out],
        out_shape=[jax.ShapeDtypeStruct((width, units), BF16)] * 2,
        compiler_params=kernel_params(),
        cost_estimate=SMALL,
        name="gate_up_grads",
    )(rows, grad_gate, grad_up)


def expert_weight_grads(gate_grad, up_grad, cot, gated):
    n_rows, width = cot.shape
    units = gated.shape[1]
    half = width // 2
    nx, ny = axis_len("dp"), axis_len("y")
    n_blocks = nx * ny
    gu_rows, down_rows = width // n_blocks, units // n_blocks
    n_out = 2 * n_blocks
    block_shape = (gu_rows + down_rows, half)
    chunk, tile = n_rows // 4, 256

    def kernel(place_ref, gate_ref, up_ref, cot_ref, gated_ref, *refs):
        outs, down_sum = refs[:n_out], refs[n_out]
        step = pl.program_id(0)

        @pl.when(step == 0)
        def _():
            down_sum[...] = jnp.zeros_like(down_sum)

        for at in range(0, width, tile):
            down_sum[:, at : at + tile] += contract(gated_ref[...], cot_ref[:, at : at + tile], 0, 0)

        def store(out, grad_ref, at, columns):
            out[:gu_rows, :] = grad_ref[at * gu_rows : (at + 1) * gu_rows, :]
            down = down_sum[at * down_rows : (at + 1) * down_rows, columns]
            out[gu_rows:, :] = down.astype(BF16)

        @pl.when(step == 3)
        def _():
            for at in range(n_blocks):
                x_step, y_step = step_to(place_ref, at)
                for s in range(nx):
                    for t in range(ny):

                        @pl.when((x_step == s) & (y_step == t))
                        def _(at=at, s=s, t=t):
                            store(outs[s * ny + t], gate_ref, at, slice(0, half))
                            store(outs[n_blocks + t * nx + s], up_ref, at, slice(half, width))

    def by_chunk(columns):
        return pl.BlockSpec((chunk, columns), lambda j, place: (j, 0))

    whole = pl.BlockSpec((width, units), lambda j, place: (0, 0))
    outs = pl.pallas_call(
        kernel,
        grid_spec=pltpu.PrefetchScalarGridSpec(
            num_scalar_prefetch=1,
            grid=(4,),
            in_specs=[whole, whole, by_chunk(width), by_chunk(units)],
            out_specs=[pl.BlockSpec(block_shape, lambda j, place: (0, 0))] * n_out,
            scratch_shapes=[pltpu.VMEM((units, width), F32)],
        ),
        out_shape=[jax.ShapeDtypeStruct(block_shape, BF16)] * n_out,
        compiler_params=kernel_params(),
        cost_estimate=SMALL,
        name="expert_weight_grads",
    )(plane_places(), gate_grad, up_grad, cot, gated)
    return [
        [outs[s * ny : (s + 1) * ny] for s in range(nx)],
        [outs[n_blocks + t * nx : n_blocks + (t + 1) * nx] for t in range(ny)],
    ]


def expert_results(gated, down):
    n_rows, units = gated.shape
    width = down.shape[1]
    half = n_rows // 8

    def kernel(gated_ref, down_ref, own_ref, other_ref):
        for i, out in enumerate((own_ref, other_ref)):
            rows = gated_ref[i * half : (i + 1) * half, :]
            out[...] = jnp.dot(rows, down_ref[...], preferred_element_type=F32).astype(BF16)

    out = pl.BlockSpec((half, width), lambda j: (2 * (1 - j % 2) + j // 2, 0))
    return pl.pallas_call(
        kernel,
        grid=(4,),
        in_specs=[
            pl.BlockSpec((2 * half, units), lambda j: (j, 0)),
            pl.BlockSpec(down.shape, lambda j: (0, 0)),
        ],
        out_specs=[out, out],
        out_shape=[jax.ShapeDtypeStruct((4 * half, width), BF16)] * 2,
        compiler_params=kernel_params(),
        cost_estimate=SMALL,
        name="expert_results",
    )(gated, down)


def branch_backward(grads, mixed, weight):
    rows, columns = mixed.shape
    width = weight.shape[0]
    half, chip_half = columns // 2, rows // 2
    block_rows = width // (axis_len("dp") * axis_len("y"))
    shapes = half_shapes([(block_rows, half)] * 2)
    n_out = len(shapes)
    together = width // block_rows
    tile = together * block_rows
    n_tiles = width // tile

    def kernel(place_ref, own_ref, other_ref, mixed_ref, weight_ref, *refs):
        out_ref, outs, total_ref = refs[0], refs[1 : 1 + n_out], refs[1 + n_out]
        at = pl.program_id(0)
        both = jnp.concatenate([own_ref[...], other_ref[...]], axis=0)
        part = jnp.dot(both, weight_ref[...], preferred_element_type=F32)

        @pl.when(at == 0)
        def _():
            total_ref[...] = part

        @pl.when(at > 0)
        def _():
            total_ref[...] += part

        product = contract(both, mixed_ref[...], 0, 0).astype(BF16)
        for i in range(together):
            block = product[i * block_rows : (i + 1) * block_rows]

            def first(out, block=block):
                out[...] = block[:, :half]

            def second(out, block=block):
                out[...] = block[:, half:]

            store_blocks(place_ref, at * together + i, outs, first, second)

        @pl.when(at == n_tiles - 1)
        def _():
            out_ref[...] = total_ref[...].astype(BF16)

    def fixed(shape):
        return pl.BlockSpec(shape, lambda j, place: (0,) * len(shape))

    by_columns = pl.BlockSpec((chip_half, tile), lambda j, place: (0, j))
    outs = pl.pallas_call(
        kernel,
        grid_spec=pltpu.PrefetchScalarGridSpec(
            num_scalar_prefetch=1,
            grid=(n_tiles,),
            in_specs=[
                by_columns,
                by_columns,
                fixed(mixed.shape),
                pl.BlockSpec((tile, columns), lambda j, place: (j, 0)),
            ],
            out_specs=[fixed(mixed.shape)] + [fixed(shape) for shape in shapes],
            scratch_shapes=[pltpu.VMEM((rows, columns), F32)],
        ),
        out_shape=[jax.ShapeDtypeStruct((rows, columns), BF16)]
        + [jax.ShapeDtypeStruct(shape, BF16) for shape in shapes],
        compiler_params=kernel_params(),
        cost_estimate=SMALL,
        name="branch_backward",
    )(plane_places(), *grads, mixed, weight)
    return outs[0], two_halves(outs[1:])


def projection_backward(
    normed, units, weight, grad_query, grad_key_value, split, extra_rows, extra_columns
):
    rows, width = normed.shape
    own_query = grad_query.shape[1]
    columns = own_query + grad_key_value.shape[1]
    half = rows // 2
    block_rows = width // (axis_len("dp") * axis_len("y"))
    shapes = half_shapes([(block_rows, split), (block_rows, columns - split + LANES)])
    together = blocks_a_step(block_rows)
    tile = together * block_rows

    def kernel(
        place_ref, normed_ref, unit_ref, other_unit_ref, weight_ref, query_ref, key_value_ref, *refs
    ):
        extra_refs, column_ref = refs[: len(extra_rows)], refs[len(extra_rows)]
        own_ref, other_ref = refs[len(extra_rows) + 1 : len(extra_rows) + 3]
        outs = refs[len(extra_rows) + 3 :]
        at = pl.program_id(0)
        part = contract(query_ref[...], weight_ref[:, :own_query], 1, 1) + contract(
            key_value_ref[...], weight_ref[:, own_query:], 1, 1
        )
        own_ref[...] = part[:half]
        other_ref[...] = part[half:].astype(BF16)
        both_units = jnp.concatenate([unit_ref[...], other_unit_ref[...]], axis=0)
        terms = (part * both_units.astype(F32)).astype(BF16)
        first = (lax.broadcasted_iota(jnp.int32, (rows, LANES), 1) == 0).astype(F32).astype(BF16)
        extra = contract(terms, first, 0, 0)
        row = 0
        for extra_ref in extra_refs:
            n = extra_ref.shape[0]
            extra += contract(extra_ref[...], column_ref[row : row + n, :], 0, 0)
            row += n
        by_query = contract(normed_ref[...], query_ref[...], 0, 0).astype(BF16)
        by_key_value = contract(normed_ref[...], key_value_ref[...], 0, 0).astype(BF16)
        extra = extra.astype(BF16)
        for i in range(together):
            these = slice(i * block_rows, (i + 1) * block_rows)

            def first(out, these=these):
                out[...] = by_query[these, :split]

            def second(out, these=these):
                out[:, : own_query - split] = by_query[these, split:]
                out[:, own_query - split : columns - split] = by_key_value[these]
                out[:, columns - split :] = extra[these]

            store_blocks(place_ref, at * together + i, outs, first, second)

    def fixed(shape):
        return pl.BlockSpec(shape, lambda j, place: (0,) * len(shape))

    def by_columns(n):
        return pl.BlockSpec((n, tile), lambda j, place: (0, j))

    outs = pl.pallas_call(
        kernel,
        grid_spec=pltpu.PrefetchScalarGridSpec(
            num_scalar_prefetch=1,
            grid=(width // tile,),
            in_specs=[
                by_columns(rows),
                by_columns(half),
                by_columns(half),
                pl.BlockSpec((tile, columns), lambda j, place: (j, 0)),
                fixed(grad_query.shape),
                fixed(grad_key_value.shape),
            ]
            + [by_columns(r.shape[0]) for r in extra_rows]
            + [fixed(extra_columns.shape)],
            out_specs=[by_columns(half), by_columns(half)] + [fixed(shape) for shape in shapes],
        ),
        out_shape=[
            jax.ShapeDtypeStruct((half, width), F32),
            jax.ShapeDtypeStruct((half, width), BF16),
        ]
        + [jax.ShapeDtypeStruct(shape, BF16) for shape in shapes],
        compiler_params=kernel_params(),
        cost_estimate=SMALL,
        name="projection_backward",
    )(
        plane_places(),
        normed,
        *units,
        weight,
        grad_query,
        grad_key_value,
        *extra_rows,
        extra_columns,
    )
    return (
        outs[0],
        outs[1],
        two_halves(outs[2:]),
    )


def middle_backward(backs, gates, middle, gain, router, grad_out):
    rows, width = middle.shape
    half_lanes = LANES // 2
    arrays = jax.tree.leaves(backs)
    n_backs = len(arrays)
    sizes = [len(jax.tree.leaves(back)) for back in backs]

    def kernel(*refs):
        gate_ref, middle_ref, gain_ref, router_ref, out_ref = refs[n_backs : n_backs + 5]
        grad_ref, rounded_ref, terms_ref, logits_ref = refs[n_backs + 5 :]
        came, at = 0.0, 0
        for n in sizes:
            pieces = [r[...].astype(F32) for r in refs[at : at + n]]
            came = came + (jnp.concatenate(pieces, axis=0) if n > 1 else pieces[0])
            at += n
        shares = came[:, width:]
        lane = lax.broadcasted_iota(jnp.int32, (rows, LANES), 1)
        shares = shares + pltpu.roll(shares, half_lanes, 1)
        shares = jnp.where(lane < half_lanes, shares, 0.0)
        shares = pltpu.roll(shares, ROUTER_LANE, 1)
        gate = gate_ref[...]
        mean = jnp.sum(gate * shares, axis=1, keepdims=True)
        logits = (gate * (shares - mean)).astype(BF16)
        logits_ref[...] = logits
        grad = came[:, :width] + contract(logits, router_ref[...], 1, 1)
        value = middle_ref[...]
        root = lax.rsqrt(jnp.mean(value * value, axis=-1, keepdims=True) + EPS)
        unit = value * root
        scaled = grad * gain_ref[...]
        along_unit = jnp.mean(scaled * unit, axis=-1, keepdims=True)
        total = out_ref[...] + root * (scaled - unit * along_unit)
        grad_ref[...] = total
        rounded_ref[...] = total.astype(BF16)
        terms_ref[...] = (grad * unit).astype(BF16)

    vmem = pl.BlockSpec(memory_space=pltpu.VMEM)
    return pl.pallas_call(
        kernel,
        in_specs=[vmem] * (n_backs + 5),
        out_specs=[vmem] * 4,
        out_shape=[
            jax.ShapeDtypeStruct((rows, width), F32),
            jax.ShapeDtypeStruct((rows, width), BF16),
            jax.ShapeDtypeStruct((rows, width), BF16),
            jax.ShapeDtypeStruct((rows, LANES), BF16),
        ],
        compiler_params=pltpu.CompilerParams(vmem_limit_bytes=48 * 1024 * 1024),
        cost_estimate=SMALL,
        name="middle_backward",
    )(*arrays, gates, middle, gain, router, grad_out)


def expert_sums(core, halves, gu_shard, down_shard):
    block_rows, half = halves[0][0].shape
    counts = [len(blocks) for blocks in halves]
    kept = gu_shard + down_shard

    def kernel(core_ref, *refs):
        mine_ref, other_ref, total = refs[sum(counts) :]
        at = 0
        for i, n in enumerate(counts):
            columns = slice(i * half, (i + 1) * half)
            total[:, columns] = sum(r[...].astype(F32) for r in refs[at : at + n])
            at += n
        core = core_ref[0]
        for which, out in ((core, mine_ref), (1 - core, other_ref)):
            gu = pl.ds(pl.multiple_of(which * gu_shard, 8), gu_shard)
            down = pl.ds(pl.multiple_of(CORES * gu_shard + which * down_shard, 8), down_shard)
            out[:gu_shard, :] = total[gu, :].astype(out.dtype)
            out[gu_shard:, :] = total[down, :].astype(out.dtype)

    vmem = pl.BlockSpec(memory_space=pltpu.VMEM)
    return pl.pallas_call(
        kernel,
        in_specs=[pl.BlockSpec(memory_space=pltpu.SMEM)] + [vmem] * sum(counts),
        out_specs=[vmem, vmem],
        out_shape=[
            jax.ShapeDtypeStruct((kept, 2 * half), F32),
            jax.ShapeDtypeStruct((kept, 2 * half), BF16),
        ],
        scratch_shapes=[pltpu.VMEM((block_rows, 2 * half), F32)],
        compiler_params=pltpu.CompilerParams(vmem_limit_bytes=48 * 1024 * 1024),
        cost_estimate=SMALL,
        name="expert_sums",
    )(core.astype(jnp.int32).reshape(1), *halves[0], *halves[1])


def expert_shards(core, mine, received, gu_shard, down_shard):
    width = mine.shape[1]

    def kernel(core_ref, mine_ref, received_ref, gu_ref, down_ref):
        core = core_ref[0]
        for which, rows in ((core, mine_ref), (1 - core, received_ref)):
            gu_ref[which] = rows[:gu_shard, :].astype(F32)
            down_ref[which] = rows[gu_shard:, :].astype(F32)

    vmem = pl.BlockSpec(memory_space=pltpu.VMEM)
    return pl.pallas_call(
        kernel,
        in_specs=[pl.BlockSpec(memory_space=pltpu.SMEM), vmem, vmem],
        out_specs=[vmem, vmem],
        out_shape=[
            jax.ShapeDtypeStruct((CORES, gu_shard, width), F32),
            jax.ShapeDtypeStruct((CORES, down_shard, width), F32),
        ],
        compiler_params=pltpu.CompilerParams(vmem_limit_bytes=48 * 1024 * 1024),
        cost_estimate=SMALL,
        name="expert_shards",
    )(core.astype(jnp.int32).reshape(1), mine, received)


def projection_shards(core, summed, received, columns):
    own_query, whole = columns
    rows = summed.shape[1]
    own_width = own_query + 2 * HEAD_SIZE
    key_at = KEY_VALUE_HEADS * own_query
    value_at = key_at + KEY_VALUE_HEADS * HEAD_SIZE

    def kernel(core_ref, summed_ref, received_ref, out_ref, extra_ref):
        core = core_ref[0]
        mine, other = summed_ref[core], received_ref[...].astype(F32)
        for which, part in ((core, mine), (1 - core, other)):
            for start, size, at in (
                (0, own_query, 0),
                (key_at, HEAD_SIZE, own_query),
                (value_at, HEAD_SIZE, own_query + HEAD_SIZE),
            ):
                target = pl.ds(pl.multiple_of(start + which * size, LANES), size)
                out_ref[:, target] = part[:, at : at + size]
        extra_ref[...] = mine[:, own_width:] + other[:, own_width:]

    vmem = pl.BlockSpec(memory_space=pltpu.VMEM)
    return pl.pallas_call(
        kernel,
        in_specs=[pl.BlockSpec(memory_space=pltpu.SMEM), vmem, vmem],
        out_specs=[vmem, vmem],
        out_shape=[
            jax.ShapeDtypeStruct((rows, whole), F32),
            jax.ShapeDtypeStruct((rows, LANES), F32),
        ],
        cost_estimate=SMALL,
        name="projection_shards",
    )(core.astype(jnp.int32).reshape(1), summed, received)


def on_device(
    hidden_in,
    lengths,
    order,
    routes,
    cotangent,
    attn_gain,
    qkv_weight,
    out_weight,
    ffn_gain,
    router_weight,
    gate_up_weight,
    down_weight,
):
    hidden = hidden_in[0]
    grad_out = cotangent[0]
    rows, width = hidden.shape
    n_experts = router_weight.shape[1]
    nx, ny, nz = axis_len("dp"), axis_len("y"), axis_len("exp")
    core = lax.axis_index("ctx") % CORES
    other_core = 1 - core
    shard = qkv_weight.shape[0]
    chip_rows = CORES * rows
    query_width = QUERY_HEADS * HEAD_SIZE
    heads = QUERY_HEADS // KEY_VALUE_HEADS
    own_query = heads * HEAD_SIZE
    own_width = own_query + 2 * HEAD_SIZE
    hidden_units = gate_up_weight.shape[2] // 2
    scale = HEAD_SIZE ** (-0.5)

    extra = jnp.concatenate([attn_gain[:, None], ffn_gain[:, None], router_weight], axis=1)
    extra = jnp.pad(extra, ((0, 0), (0, LANES - extra.shape[1])))
    split = 5 * HEAD_SIZE

    def gather_z(pair, *waits):
        blocks = line_gather(pair.reshape(CORES * shard, -1), nz, *waits)
        place = lax.axis_index("exp")
        whole = jnp.zeros((CORES, nz, shard, pair.shape[2]), BF16)
        for step, block in enumerate(blocks):
            at = jnp.bitwise_xor(place, step)
            whole = lax.dynamic_update_slice_in_dim(
                whole, block.reshape(CORES, 1, shard, -1), at, 1
            )
        return whole.reshape(CORES * nz * shard, -1)

    weights = jnp.concatenate([qkv_weight, extra, out_weight.T], axis=1)
    weights = in_core_order(weights, core_swap(weights))
    key_at = query_width + core * HEAD_SIZE
    value_at = key_at + KEY_VALUE_HEADS * HEAD_SIZE
    extra_at = qkv_weight.shape[1]
    out_at = extra_at + LANES + core * own_query
    weights = jnp.concatenate(
        [
            lax.dynamic_slice_in_dim(weights, core * own_query, own_query, 2),
            lax.dynamic_slice_in_dim(weights, key_at, HEAD_SIZE, 2),
            lax.dynamic_slice_in_dim(weights, value_at, HEAD_SIZE, 2),
            weights[:, :, extra_at : extra_at + LANES],
            lax.dynamic_slice_in_dim(weights, out_at, own_query, 2),
        ],
        axis=2,
    )
    def expert_rows(which):
        return (
            lax.dynamic_index_in_dim(gate_up_weight, which, 0, keepdims=False),
            lax.dynamic_index_in_dim(down_weight, which, 0, keepdims=False),
        )

    gu_mine, down_mine = expert_rows(core)
    gu_shard, down_shard = gu_mine.shape[0], down_mine.shape[0]
    received = core_swap(after(jnp.concatenate(expert_rows(other_core), axis=0), weights))
    gu_pair = in_core_order(gu_mine, received[:gu_shard]).reshape(CORES * gu_shard, -1)
    down_pair = in_core_order(down_mine, received[gu_shard:]).reshape(CORES * down_shard, -1)
    half_width = width // 2
    expert_halves = (
        jnp.concatenate([gu_pair[:, :hidden_units], down_pair[:, :half_width]], axis=0),
        jnp.concatenate([gu_pair[:, hidden_units:], down_pair[:, half_width:]], axis=0),
    )
    expert_first = plane_first(*expert_halves)

    weights_z = after(gather_z(weights), expert_first)
    block_rows = CORES * nz * shard
    half_query = own_query // 2
    group = 4 if nz % 4 == 0 else nz
    phased = group == nz
    qkv_z, out_z = weights_z[:, : own_width + LANES], weights_z[:, own_width + LANES :]
    qkv_halves = (qkv_z[:, :split], qkv_z[:, split:])
    out_halves = (out_z[:, :half_query], out_z[:, half_query:])

    expert_ids = jnp.arange(n_experts, dtype=jnp.int32)
    used = jnp.any(routes[0][:, :, None] == expert_ids[None, None, :], axis=1)
    marks = jnp.pad(
        used.astype(BF16), ((0, 0), (ROUTER_LANE, LANES - ROUTER_LANE - n_experts))
    )
    cot_rows = jnp.concatenate([grad_out.astype(BF16), marks], axis=1)
    cot_all = lax.all_gather(after(cot_rows, weights_z), "exp", axis=0, tiled=False)

    units = unit_rows(hidden, weights_z)
    units_other = core_swap(units)
    qkv_first, qkv_second = plane_first(*qkv_halves), plane_second(*qkv_halves)
    qkv_first, qkv_second, out_halves = after((qkv_first, qkv_second, out_halves), units_other)
    qkv_third = plane_third(qkv_first)
    w_all, extra_all = place_blocks(
        qkv_halves,
        (qkv_first, qkv_second, qkv_third),
        ((0, block_rows, 0, own_width), (0, block_rows, own_width, LANES)),
    )
    out_halves = after(out_halves, w_all)
    out_first, out_second = plane_first(*out_halves), plane_second(*out_halves)
    gain_one = extra_all[:, 0].astype(F32)
    gain_two = extra_all[:, 1].astype(F32)
    lanes = jnp.arange(LANES)
    is_router = (lanes >= ROUTER_LANE) & (lanes < ROUTER_LANE + n_experts)
    router_all = jnp.where(is_router[None, :], extra_all, 0)

    normed = jnp.concatenate([units, units_other], axis=0)
    normed = (normed.astype(F32) * gain_one).astype(BF16)
    packed_all, all_lengths = after((order[0], lengths[0]), weights_z)
    starts_all = doc_starts(packed_all, all_lengths)

    def own_first(values):
        y_place, y_rows = axis_place("y"), chip_rows
        parts = []
        for t in range(ny):
            at = lax.rem(y_place - t + ny, ny) * y_rows
            for which in (core, other_core):
                parts.append(lax.dynamic_slice_in_dim(values, at + which * rows, rows, 0))
        return jnp.concatenate(parts, axis=0)

    packed_keys, starts = own_first(packed_all), own_first(starts_all)[:chip_rows]
    packed = packed_keys[:chip_rows]
    cosine, sine = rotation_tables(packed - starts)
    bounds = jnp.concatenate(
        [starts[None, :], packed[None, :], jnp.zeros((6, chip_rows), jnp.int32)], axis=0
    )
    key_place = packed_keys[:, None]
    projected = dot(normed, w_all)
    key_value = jnp.concatenate(
        [
            rotate(projected[:, own_query : own_query + HEAD_SIZE], cosine, sine),
            projected[:, own_query + HEAD_SIZE : own_width],
        ],
        axis=1,
    ).astype(BF16)
    key_value = [key_value] + [shifted(key_value, "y", t) for t in range(1, ny)]
    out_first, expert_halves, projected, cot_all = after(
        (out_first, expert_halves, projected, cot_all), key_value, out_second
    )
    out_third = plane_third(out_first)
    cot_other = core_swap(cot_all)
    expert_second = plane_second(*expert_halves)
    query_rows, mixed, lse = attention_forward(
        projected, key_value, cosine, sine, key_place, bounds, heads
    )
    mixed, expert_first = after((mixed, expert_first), out_third, cot_other)
    expert_third = plane_third(after(expert_first, expert_second))
    (out_turned,) = place_blocks(
        out_halves, (out_first, out_second, out_third), ((0, block_rows, 0, own_query),)
    )
    middle = hidden + core_sum(dot_turned(mixed, out_turned))
    inner = norm_rows(middle, gain_two).astype(BF16)
    gate_up_all, down_all = place_blocks(
        expert_halves,
        (expert_first, expert_second, expert_third),
        (
            (0, CORES * gu_shard, 0, 2 * hidden_units),
            (CORES * gu_shard, CORES * down_shard, 0, width),
        ),
    )

    logits = jnp.where(marks > 0, dot(inner, extra_all), -jnp.inf)
    gates = jax.nn.softmax(logits, axis=-1)
    place_z = lax.axis_index("exp")
    own_expert = place_z * CORES + core

    def expert_group(inner_rows, from_place):
        buffers = []

        def run(index, chunk):
            scalars = jnp.stack([own_expert, jnp.bitwise_xor(from_place, index)])
            (mine, other), filled = expert_step(
                scalars.astype(jnp.int32),
                chunk,
                [cot_all, cot_other],
                gate_up_all,
                down_all,
                extra_all,
                index,
                4,
                buffers,
            )
            buffers[:] = filled
            return mine, other

        def joined(mine, other):
            return (mine.astype(F32) + other.astype(F32)).astype(BF16)

        rows_1, rows_2 = xor_shift(inner_rows, 1), xor_shift(inner_rows, 2)
        mine_0, other_0 = run(0, [inner_rows, core_swap(inner_rows)])

        rows_1, rows_2 = after((rows_1, rows_2), other_0)
        rows_3 = xor_shift(rows_2, 1)
        swapped = [core_swap(rows_1), core_swap(rows_2)]
        rows_1, other_1_rows, other_2_rows = after((rows_1, *swapped))
        other_0 = core_swap(other_0)
        mine_1, other_1 = run(1, [rows_1, other_1_rows])

        rows_2, other_1, mine_1 = after((rows_2, other_1, mine_1), other_0)
        other_1 = core_swap(other_1)
        back_1 = joined(mine_1, other_1)
        rows_2, rows_3 = after((rows_2, rows_3), back_1)
        near = xor_shift(back_1, 1)
        other_3_rows = core_swap(rows_3)
        mine_2, other_2 = run(2, [rows_2, other_2_rows])

        rows_3, other_2 = after((rows_3, other_2), other_3_rows)
        other_2 = core_swap(other_2)
        mine_3, other_3 = run(3, [rows_3, other_3_rows])

        mine_3, other_3 = after((mine_3, other_3), other_2, near)
        back_3 = joined(mine_3, core_swap(other_3))
        handed = xor_shift(back_3, 1)
        all_rows, all_cots, gated_all, grad_gates, grad_ups = after(buffers, back_3)
        if phased:
            grad_gate, grad_up = gate_up_grads(all_rows, grad_gates, grad_ups)
            grad_gate, grad_up, handed = after((grad_gate, grad_up, handed))
        mine_0, mine_2 = after((mine_0, mine_2), back_3)
        back_2 = joined(mine_2, other_2)
        (pair,) = line_pairs([None, None, back_2, None], [handed])
        if phased:
            grad_gate, gated_all, pair = after((grad_gate, gated_all, pair), gates)
        pieces = [pair[: rows // 2], pair[rows // 2 :]]
        moved, received = xor_shift(pieces[0], 2), []
        if phased:
            weight_grads = expert_weight_grads(grad_gate, grad_up, all_cots, gated_all)
            weight_grads, gated_all, moved, pieces = after((weight_grads, gated_all, moved, pieces))
            received = plane_moved_part(weight_grads, True)
        else:
            weight_grads = (
                dot_rows(all_rows, grad_gates),
                dot_rows(all_rows, grad_ups),
                dot_rows(gated_all, all_cots),
            )
        moved_more = xor_shift(pieces[1], 2)
        back_0 = joined(mine_0, other_0)
        outs, outs_other = expert_results(gated_all, down_all)
        outs, outs_other, moved_more, received, weight_grads = after(
            (outs, outs_other, moved_more, received, weight_grads), back_0
        )
        if phased:
            received = plane_joined(plane_moved_part(weight_grads, False), received)
        outs_other = core_swap(outs_other)
        outs = [
            (outs[half].astype(F32) + outs_other[half].astype(F32)).astype(BF16)
            for half in (slice(0, 2 * rows), slice(2 * rows, 4 * rows))
        ]
        return (back_0, near, (moved, moved_more)), outs, weight_grads, received

    if phased:
        backs, outs, expert_grads, expert_received = expert_group(inner, place_z)
    else:

        def visit(turn, state):
            inner_here, back, out, sums = state
            more_back, outs, more, _ = expert_group(
                inner_here, lax.rem(place_z + turn * group, nz)
            )
            back = back + more_back[0].astype(F32) + more_back[1].astype(F32)
            back = back + jnp.concatenate(more_back[2], axis=0).astype(F32)
            odd, even = (o.reshape(2, rows, width) for o in outs)
            out = out + line_scatter([even[0], odd[0], even[1], odd[1]])[0]
            sums = tuple(a + b for a, b in zip(sums, more))
            return (*(shifted(v, "exp", nz - group) for v in (inner_here, back, out)), sums)

        sums = (
            jnp.zeros((width, hidden_units), F32),
            jnp.zeros((width, hidden_units), F32),
            jnp.zeros((hidden_units, width), F32),
        )
        start = (jnp.zeros((rows, width + LANES), F32), jnp.zeros((rows, width), F32), sums)
        _, back, moe, sums = lax.fori_loop(0, nz // group, visit, (inner, *start))
        backs = (back,)
        gate, up, down = (w.astype(BF16) for w in sums)
        gate, up = (w.reshape(nx, ny, CORES * gu_shard, hidden_units) for w in (gate, up))
        down = down.reshape(nx, ny, CORES * down_shard, width)
        expert_grads = [
            plane_blocks([gate, down[..., :half_width]], PLANE_AXES[0]),
            plane_blocks([up, down[..., half_width:]], PLANE_AXES[1]),
        ]
        expert_received = plane_joined(
            plane_moved_part(expert_grads, False), plane_moved_part(expert_grads, True)
        )

    if phased:
        results_handed = xor_shift(outs[0][rows:], 1)

    grad_middle, grad_branch, ffn_terms, grad_logits = middle_backward(
        backs, gates, middle, gain_two[None, :], router_all, grad_out
    )
    grad_branch = [grad_branch, core_swap(grad_branch)]
    blended_gradient, out_grads = branch_backward(grad_branch, mixed, out_turned)
    if phased:
        blended_gradient = after(blended_gradient, outs[0])
    grad_query, grad_kv_own, *grad_kv_parts = attention_backward(
        query_rows, blended_gradient, lse, key_value, cosine, sine, key_place, bounds, heads
    )

    if phased:
        grad_query, grad_kv_own, grad_kv_parts, results_handed = after(
            (grad_query, grad_kv_own, grad_kv_parts, results_handed)
        )
    grad_kv_parts = [shifted(part, "y", ny - t) for t, part in enumerate(grad_kv_parts, 1)]
    out_grads = after(out_grads, grad_kv_parts)
    out_received = plane_moved(out_grads)
    if phased:
        pair = (outs[1][rows:].astype(F32) + results_handed.astype(F32)).astype(BF16)
        cut = rows // 4
        moe_far = [xor_shift(pair[:cut], 2)]
        results_near = xor_shift(after(outs[0][:rows], pair), 1)

    for part in grad_kv_parts:
        grad_kv_own = grad_kv_own + part.astype(F32)
    grad_key_value = jnp.concatenate(
        [rotate(grad_kv_own[:, :HEAD_SIZE], cosine, -sine), grad_kv_own[:, HEAD_SIZE:]], axis=1
    ).astype(BF16)
    if phased:
        grad_key_value = after(grad_key_value, pair)
    is_ffn = (lax.broadcasted_iota(jnp.int32, (rows, LANES), 1) == 1).astype(BF16)
    grad_normed, grad_normed_other, qkv_grads = projection_backward(
        normed,
        [units, units_other],
        w_all,
        grad_query,
        grad_key_value,
        split,
        [ffn_terms, inner],
        jnp.concatenate([is_ffn, grad_logits], axis=0),
    )
    if phased:
        qkv_grads, moe_far, pair = after((qkv_grads, moe_far, pair))
        moe_far.append(xor_shift(pair[cut:], 2))
    qkv_grads, out_received = after((qkv_grads, out_received))

    def line_sum(first, second):
        summed = jnp.concatenate([first, second], axis=1).astype(BF16)
        summed = summed.reshape(CORES, nz, shard, -1)
        place = lax.axis_index("exp")
        return line_scatter(
            [
                lax.dynamic_index_in_dim(summed, jnp.bitwise_xor(place, step), 1, keepdims=False)
                for step in range(nz)
            ]
        )

    def of_core(value, which):
        return lax.dynamic_index_in_dim(value, which, 0, keepdims=False)

    qkv_received = plane_moved(qkv_grads)
    qkv_hand_on = plane_hand_on(qkv_grads, qkv_received)
    qkv_handed = plane_handed(qkv_hand_on)
    expert_received = after(expert_received, qkv_grads)
    expert_hand_on = plane_hand_on(expert_grads, expert_received)
    out_received = after(out_received, qkv_hand_on)
    out_handed = plane_handed(plane_hand_on(out_grads, out_received))
    if phased:
        moe_far, results_near = after((moe_far, results_near), qkv_hand_on)
        moe = outs[1][:rows].astype(F32) + results_near.astype(F32)
        moe = moe + jnp.concatenate(moe_far, axis=0).astype(F32)
    grad_normed_other = after(grad_normed_other, qkv_hand_on)
    grad_normed = grad_normed + core_swap(grad_normed_other).astype(F32)
    grad_hidden_norm, _ = norm_back(hidden, gain_one, grad_normed)
    grad_input = grad_middle + grad_hidden_norm
    output = middle + moe
    expert_handed = plane_handed(after(expert_hand_on, out_handed))
    qkv_sum, qkv_pairs = line_sum(*plane_sum(qkv_grads, qkv_received, qkv_handed))
    out_handed = after(out_handed, qkv_handed)
    out_sum, out_pairs = line_sum(*plane_sum(out_grads, out_received, out_handed))
    expert_handed = after(expert_handed, qkv_pairs, out_pairs)
    out_other = core_swap(of_core(out_sum, other_core).astype(BF16)).astype(F32)
    out_sum = in_core_order(of_core(out_sum, core), out_other)
    grad_out_proj = out_sum.swapaxes(0, 1).reshape(shard, query_width).T

    blocks = [
        [half[0][0], *(came[0] for came in received), *handed]
        for half, received, handed in zip(expert_grads, expert_received, expert_handed)
    ]
    mine, to_other = expert_sums(core, blocks, gu_shard, down_shard)
    grad_gate_up, grad_down = expert_shards(
        core, mine, core_swap(to_other), gu_shard, down_shard
    )
    qkv_other = core_swap(of_core(qkv_sum, other_core).astype(BF16))
    grad_qkv, extra_sum = projection_shards(
        core, qkv_sum, qkv_other, (own_query, qkv_weight.shape[1])
    )
    return (
        output[None],
        grad_input[None],
        extra_sum[:, 0],
        grad_qkv,
        grad_out_proj,
        extra_sum[:, 1],
        extra_sum[:, 2 : 2 + n_experts],
        grad_gate_up,
        grad_down,
    )


def solution(mesh):
    return jax.shard_map(
        on_device,
        mesh=mesh,
        in_specs=(
            P(("dp", "exp"), "ctx", None),
            P(("dp", "exp"), None),
            P(("dp", "exp"), None),
            P(("dp", "exp"), "ctx", None),
            P(("dp", "exp"), "ctx", None),
            P(("dp", "ctx", "exp")),
            P(("dp", "ctx", "exp"), None),
            P(None, ("dp", "ctx", "exp")),
            P(("dp", "ctx", "exp")),
            P(("dp", "ctx", "exp"), None),
            P("exp", ("dp", "ctx"), None),
            P("exp", ("dp", "ctx"), None),
        ),
        out_specs=(
            P(("dp", "exp"), "ctx", None),
            P(("dp", "exp"), "ctx", None),
            P(("dp", "ctx", "exp")),
            P(("dp", "ctx", "exp"), None),
            P(None, ("dp", "ctx", "exp")),
            P(("dp", "ctx", "exp")),
            P(("dp", "ctx", "exp"), None),
            P("exp", ("dp", "ctx"), None),
            P("exp", ("dp", "ctx"), None),
        ),
        check_vma=False,
    )
```

```python
import math

import jax
import jax.numpy as jnp
from jax import lax
from jax.experimental import pallas as pl
from jax.experimental.pallas import tpu as pltpu
from jax.sharding import PartitionSpec as P

QUERY_HEADS = 12
KEY_VALUE_HEADS = 2
HEAD_SIZE = 128
TOP = 4
CORES = 2
LANES = 128
ROUTER_LANE = 2


EPS = 1e-06
BASE = 1000000.0
BF16 = jnp.bfloat16
F32 = jnp.float32


def norm_rows(v, gain):
    return v * lax.rsqrt(jnp.mean(v * v, axis=-1, keepdims=True) + EPS) * gain


def norm_back(v, gain, grad):
    root = lax.rsqrt(jnp.mean(v * v, axis=-1, keepdims=True) + EPS)
    unit = v * root
    scaled = grad * gain
    along = jnp.mean(scaled * unit, axis=-1, keepdims=True)
    return root * (scaled - unit * along), (grad * unit).astype(BF16)


def rotation_tables(slot_position):
    half = HEAD_SIZE // 2
    freq = jnp.exp(jnp.arange(half, dtype=F32) * (-2.0 * math.log(BASE) / HEAD_SIZE))
    angle = slot_position.astype(F32)[:, None] * freq[None, :]
    cosine, sine = jnp.cos(angle), jnp.sin(angle)
    return jnp.concatenate([cosine, cosine], axis=1), jnp.concatenate([-sine, sine], axis=1)


def rotate(t, cosine, sine):
    half = HEAD_SIZE // 2
    return t * cosine + jnp.concatenate([t[:, half:], t[:, :half]], axis=1) * sine


def doc_starts(packed, lengths):
    ends = jnp.cumsum(lengths)
    return jnp.max(jnp.where(packed[:, None] >= ends[None, :], ends[None, :], 0), axis=1)


def dot(a, b):
    return jnp.dot(a, b, preferred_element_type=F32)


def dot_turned(a, b):
    return lax.dot_general(a, b, (((1,), (1,)), ((), ())), preferred_element_type=F32)


def dot_rows(a, b):
    return lax.dot_general(a, b, (((0,), (0,)), ((), ())), preferred_element_type=F32)


def after(value, *others):
    values, tree = jax.tree.flatten(value)
    others = jax.tree.leaves(others)

    def kernel(*refs):
        pass

    anywhere = pl.BlockSpec(memory_space=pl.ANY)
    tied = pl.pallas_call(
        kernel,
        out_shape=[jax.ShapeDtypeStruct(v.shape, v.dtype) for v in values],
        in_specs=[anywhere] * (len(values) + len(others)),
        out_specs=[anywhere] * len(values),
        input_output_aliases={i: i for i in range(len(values))},
        cost_estimate=pl.CostEstimate(flops=1, bytes_accessed=1, transcendentals=0),
        name="after",
    )(*values, *others)
    return jax.tree.unflatten(tree, tied)


def axis_len(axis):
    if axis == "y":
        return lax.axis_size("ctx") // CORES
    return lax.axis_size(axis)


def axis_place(axis):
    if axis == "y":
        return lax.axis_index("ctx") // CORES
    return lax.axis_index(axis)


def shifted(value, axis, step):
    name, stride = ("ctx", CORES) if axis == "y" else (axis, 1)
    n = lax.axis_size(name)
    return lax.ppermute(value, name, [(i, (i + step * stride) % n) for i in range(n)])


def core_swap(value):
    n = lax.axis_size("ctx")
    return lax.ppermute(value, "ctx", [(i, i ^ 1) for i in range(n)])


def both_cores(value):
    return jnp.concatenate([value, core_swap(value)], axis=0)


def core_sum(value):
    half = value.shape[0] // 2
    other = core_swap(value[half:].astype(BF16))
    return value[:half].astype(F32) + other.astype(F32)


def in_core_order(mine, other):
    core = lax.axis_index("ctx") % CORES
    return jnp.where(core == 0, jnp.stack([mine, other]), jnp.stack([other, mine]))


def plane_first(first, second):
    nx, ny = axis_len("dp"), axis_len("y")
    return (
        {(s, 0): shifted(first, "dp", s) for s in range(1, nx)},
        {(0, t): shifted(second, "y", t) for t in range(1, ny)},
    )


def plane_second(first, second):
    nx, ny = axis_len("dp"), axis_len("y")
    return (
        {(0, t): shifted(first, "y", t) for t in range(1, ny)},
        {(s, 0): shifted(second, "dp", s) for s in range(1, nx)},
    )


def plane_third(came):
    nx, ny = axis_len("dp"), axis_len("y")
    return (
        {(s, t): shifted(came[0][s, 0], "y", t) for s in range(1, nx) for t in range(1, ny)},
        {(s, t): shifted(came[1][0, t], "dp", s) for s in range(1, nx) for t in range(1, ny)},
    )


def place_blocks(halves, came, parts):
    nx, ny = axis_len("dp"), axis_len("y")
    steps = [(s, t) for s in range(nx) for t in range(ny)]
    blocks = []
    for k, half in enumerate(halves):
        known = {(0, 0): half}
        for pair in came:
            known.update(pair[k])
        blocks.append([known[step] for step in steps])

    def kernel(place_ref, *refs):
        first_refs, second_refs = refs[: len(steps)], refs[len(steps) : 2 * len(steps)]
        outs = refs[2 * len(steps) :]
        at = pl.program_id(0)
        x_step = lax.rem(place_ref[0] - at // ny + nx, nx)
        y_step = lax.rem(place_ref[1] - at % ny + ny, ny)
        left = first_refs[0].shape[1]
        for step, first, second in zip(steps, first_refs, second_refs):

            @pl.when((x_step == step[0]) & (y_step == step[1]))
            def _(first=first, second=second):
                for (row, n_rows, column, columns), out in zip(parts, outs):
                    for block, low, high in (
                        (first, 0, left),
                        (second, left, left + second.shape[1]),
                    ):
                        begin, end = max(column, low), min(column + columns, high)
                        if begin < end:
                            out[:, begin - column : end - column] = block[
                                row : row + n_rows, begin - low : end - low
                            ]

    whole = [pl.BlockSpec(v.shape, lambda i, place_ref: (0, 0)) for v in (*blocks[0], *blocks[1])]
    return pl.pallas_call(
        kernel,
        grid_spec=pltpu.PrefetchScalarGridSpec(
            num_scalar_prefetch=1,
            grid=(nx * ny,),
            in_specs=whole,
            out_specs=[
                pl.BlockSpec((n_rows, columns), lambda i, place_ref: (i, 0))
                for _, n_rows, _, columns in parts
            ],
        ),
        out_shape=[
            jax.ShapeDtypeStruct((nx * ny * n_rows, columns), BF16)
            for _, n_rows, _, columns in parts
        ],
        compiler_params=pltpu.CompilerParams(vmem_limit_bytes=48 * 1024 * 1024),
        cost_estimate=pl.CostEstimate(flops=1, bytes_accessed=1, transcendentals=0),
        name="place_blocks",
    )(jnp.stack([axis_place("dp"), axis_place("y")]).astype(jnp.int32), *blocks[0], *blocks[1])


def xor_shift(value, step):
    n = lax.axis_size("exp")
    return lax.ppermute(value, "exp", [(i, i ^ step) for i in range(n)])


def line_gather(value, n, *waits):
    blocks = [value]
    for step in range(1, n):
        if step % 2 == 1:
            handed = blocks[step - 1]
            if waits and step > 1:
                handed = blocks[step - 1] = after(handed, *waits)
            blocks.append(xor_shift(handed, 1))
        else:
            blocks.append(xor_shift(value, step))
    return blocks


def line_pairs(blocks, handed):
    return [
        (blocks[step].astype(F32) + other.astype(F32)).astype(BF16)
        for step, other in zip(range(2, len(blocks), 2), handed)
    ]


def line_far(blocks, near, pairs):
    total = blocks[0].astype(F32) + near.astype(F32)
    for step, pair in zip(range(2, len(blocks), 2), pairs):
        total = total + xor_shift(pair, step).astype(F32)
    return total


def line_scatter(blocks):
    odd = xor_shift(jnp.stack(blocks[1::2]), 1)
    pairs = line_pairs(blocks, odd[1:])
    return line_far(blocks, odd[0], pairs), pairs


PLANE_AXES = (("dp", "y"), ("y", "dp"))


def plane_places():
    return jnp.stack([axis_place("dp"), axis_place("y")]).astype(jnp.int32)


def plane_blocks(parts, axes):
    half = []
    for near in range(axis_len(axes[0])):
        blocks = []
        for far in range(axis_len(axes[1])):
            s, t = (near, far) if axes[0] == "dp" else (far, near)
            x = lax.rem(axis_place("dp") + s, axis_len("dp"))
            y = lax.rem(axis_place("y") + t, axis_len("y"))
            taken = [
                lax.dynamic_slice(part, (x, y, 0, 0), (1, 1, *part.shape[2:])).reshape(
                    part.shape[2:]
                )
                for part in parts
            ]
            blocks.append(jnp.concatenate(taken, axis=0))
        half.append(blocks)
    return half


def plane_moved(halves):
    return [
        [shifted(blocks, axes[0], near) for near, blocks in enumerate(half) if near > 0]
        for half, axes in zip(halves, PLANE_AXES)
    ]


def plane_moved_part(halves, handed_on):
    return [
        [
            [shifted(block, axes[0], near) for block in (blocks[1:] if handed_on else blocks[:1])]
            for near, blocks in enumerate(half)
            if near > 0
        ]
        for half, axes in zip(halves, PLANE_AXES)
    ]


def plane_joined(stay, handed_on):
    return [[a + b for a, b in zip(*half)] for half in zip(stay, handed_on)]


def half_sum(half, received, far):
    total = half[0][far].astype(F32)
    for blocks in received:
        total = total + blocks[far].astype(F32)
    return total


def plane_hand_on(halves, received):
    return [
        [half_sum(half, came, far).astype(BF16) for far in range(1, len(half[0]))]
        for half, came in zip(halves, received)
    ]


def plane_handed(handed):
    return [
        [shifted(block, axes[1], far) for far, block in enumerate(blocks, 1)]
        for blocks, axes in zip(handed, PLANE_AXES)
    ]


def plane_sum(halves, received, handed):
    sums = []
    for half, came, last in zip(halves, received, handed):
        total = half_sum(half, came, 0)
        for block in last:
            total = total + block.astype(F32)
        sums.append(total)
    return sums


def half_shapes(shapes):
    counts = [(axis_len(axes[0]), axis_len(axes[1])) for axes in PLANE_AXES]
    return [(far, *shape) for (near, far), shape in zip(counts, shapes) for _ in range(near)]


def two_halves(arrays):
    n = axis_len("dp")
    return [list(arrays[:n]), list(arrays[n:])]


def store_blocks(place_ref, at, outs, first, second):
    nx, ny = axis_len("dp"), axis_len("y")
    x_step, y_step = step_to(place_ref, at)
    for s in range(nx):

        @pl.when(x_step == s)
        def _(s=s):
            first(outs[s].at[y_step])

    for t in range(ny):

        @pl.when(y_step == t)
        def _(t=t):
            second(outs[nx + t].at[x_step])


def blocks_a_step(block_rows):
    n = 1
    while n * block_rows % LANES != 0:
        n += 1
    return n


def step_to(place_ref, at):
    nx, ny = axis_len("dp"), axis_len("y")
    return lax.rem(at // ny - place_ref[0] + nx, nx), lax.rem(at % ny - place_ref[1] + ny, ny)


SMALL = pl.CostEstimate(flops=1, bytes_accessed=1, transcendentals=0)
LOG2_E = 1.4426950408889634
GELU_ROOT = math.sqrt(2.0 / math.pi)
GELU_CUBE = 0.044715
ROW_TILE = 512


def kernel_params(n_axes=1):
    return pltpu.CompilerParams(
        dimension_semantics=("arbitrary",) * n_axes, vmem_limit_bytes=56 * 1024 * 1024
    )


def contract(a, b, a_dim, b_dim):
    return lax.dot_general(a, b, (((a_dim,), (b_dim,)), ((), ())), preferred_element_type=F32)


def turned(t, cosine, sine):
    return t * cosine + pltpu.roll(t, HEAD_SIZE // 2, 1) * sine


def fill_keys(parts, keys_ref, values_ref):
    for i, part in enumerate(parts):
        n = part.shape[0]
        keys_ref[i * n : (i + 1) * n, :] = part[:, :HEAD_SIZE]
        values_ref[i * n : (i + 1) * n, :] = part[:, HEAD_SIZE:]


def fill_bias(key_place_ref, bounds_ref, bias_ref):
    place = key_place_ref[...]
    allowed = (place >= bounds_ref[0:1, :]) & (place <= bounds_ref[1:2, :])
    bias_ref[...] = jnp.where(allowed, 0.0, -1e30)


def unit_rows(rows, *waits):
    def kernel(rows_ref, *refs):
        value = rows_ref[...]
        root = lax.rsqrt(jnp.mean(value * value, axis=-1, keepdims=True) + EPS)
        refs[-1][...] = (value * root).astype(BF16)

    return pl.pallas_call(
        kernel,
        in_specs=[pl.BlockSpec(memory_space=pltpu.VMEM)]
        + [pl.BlockSpec(memory_space=pl.ANY)] * len(waits),
        out_specs=pl.BlockSpec(memory_space=pltpu.VMEM),
        out_shape=jax.ShapeDtypeStruct(rows.shape, BF16),
        compiler_params=pltpu.CompilerParams(vmem_limit_bytes=32 * 1024 * 1024),
        cost_estimate=SMALL,
        name="unit_rows",
    )(rows, *waits)


def attention_forward(projected, key_value, cosine, sine, key_place, bounds, heads, *waits):
    rows = projected.shape[0]
    n_keys = key_place.shape[0]
    n_parts = len(key_value)
    factor = HEAD_SIZE ** (-0.5) * LOG2_E

    def kernel(projected_ref, cos_ref, sin_ref, place_ref, bounds_ref, *refs):
        parts = refs[:n_parts]
        query_ref, mixed_ref, lse_ref, keys_ref, values_ref, bias_ref = refs[n_parts + len(waits) :]
        head = pl.program_id(0)

        @pl.when(head == 0)
        def _():
            fill_keys(parts, keys_ref, values_ref)
            fill_bias(place_ref, bounds_ref, bias_ref)

        for start in range(0, rows, ROW_TILE):
            tile = slice(start, start + ROW_TILE)
            query = turned(projected_ref[tile, :], cos_ref[tile, :], sin_ref[tile, :]).astype(BF16)
            query_ref[tile, :] = query
            scores = contract(keys_ref[...], query, 1, 1) * factor + bias_ref[:, tile]
            top = jnp.max(scores, axis=0, keepdims=True)
            weights = jnp.exp2(scores - top)
            total = jnp.sum(weights, axis=0, keepdims=True)
            probs = (weights * (1.0 / total)).astype(BF16)
            mixed_ref[tile, :] = contract(probs, values_ref[...], 0, 0).astype(BF16)
            lse_ref[pl.ds(head, 1), tile] = top + jnp.log2(total)

    def fixed(shape):
        return pl.BlockSpec(shape, lambda h: (0,) * len(shape))

    by_head = pl.BlockSpec((rows, HEAD_SIZE), lambda h: (0, h))
    return pl.pallas_call(
        kernel,
        grid=(heads,),
        in_specs=[
            by_head,
            fixed(cosine.shape),
            fixed(sine.shape),
            fixed(key_place.shape),
            fixed(bounds.shape),
        ]
        + [fixed(p.shape) for p in key_value]
        + [pl.BlockSpec(memory_space=pl.ANY)] * len(waits),
        out_specs=[by_head, by_head, fixed((8, rows))],
        out_shape=[
            jax.ShapeDtypeStruct((rows, heads * HEAD_SIZE), BF16),
            jax.ShapeDtypeStruct((rows, heads * HEAD_SIZE), BF16),
            jax.ShapeDtypeStruct((8, rows), F32),
        ],
        scratch_shapes=[
            pltpu.VMEM((n_keys, HEAD_SIZE), BF16),
            pltpu.VMEM((n_keys, HEAD_SIZE), BF16),
            pltpu.VMEM((n_keys, rows), F32),
        ],
        compiler_params=kernel_params(),
        cost_estimate=SMALL,
        name="attention_forward",
    )(projected, cosine, sine, key_place, bounds, *key_value, *waits)


def attention_backward(
    query, head_gradient, lse, key_value, cosine, sine, key_place, bounds, heads
):
    rows = query.shape[0]
    n_keys = key_place.shape[0]
    n_parts = len(key_value)
    scale = HEAD_SIZE ** (-0.5)
    factor = scale * LOG2_E

    def kernel(query_ref, grad_ref, lse_ref, cos_ref, sin_ref, place_ref, bounds_ref, *refs):
        parts = refs[:n_parts]
        out_ref = refs[n_parts]
        part_outs = refs[n_parts + 1 : 2 * n_parts + 1]
        keys_ref, values_ref, bias_ref, grad_keys_ref, grad_values_ref = refs[2 * n_parts + 1 :]
        head = pl.program_id(0)

        @pl.when(head == 0)
        def _():
            fill_keys(parts, keys_ref, values_ref)
            fill_bias(place_ref, bounds_ref, bias_ref)
            grad_keys_ref[...] = jnp.zeros_like(grad_keys_ref)
            grad_values_ref[...] = jnp.zeros_like(grad_values_ref)

        for start in range(0, rows, ROW_TILE):
            tile = slice(start, start + ROW_TILE)
            query, grad = query_ref[tile, :], grad_ref[tile, :]
            scores = contract(keys_ref[...], query, 1, 1) * factor + bias_ref[:, tile]
            probs = jnp.exp2(scores - lse_ref[pl.ds(head, 1), tile])
            weighted = probs * contract(values_ref[...], grad, 1, 1)
            offset = jnp.sum(weighted, axis=0, keepdims=True)
            grad_scores = (weighted - probs * offset).astype(BF16)
            grad_keys_ref[...] += contract(grad_scores, query, 1, 0)
            grad_values_ref[...] += contract(probs.astype(BF16), grad, 1, 0)
            grad_query = contract(grad_scores, keys_ref[...], 0, 0) * scale
            out_ref[tile, :] = turned(grad_query, cos_ref[tile, :], -sin_ref[tile, :]).astype(BF16)

        @pl.when(head == heads - 1)
        def _():
            for i, out in enumerate(part_outs):
                n = out.shape[0]
                out[:, :HEAD_SIZE] = (grad_keys_ref[i * n : (i + 1) * n, :] * scale).astype(out.dtype)
                out[:, HEAD_SIZE:] = grad_values_ref[i * n : (i + 1) * n, :].astype(out.dtype)

    def fixed(shape):
        return pl.BlockSpec(shape, lambda h: (0,) * len(shape))

    by_head = pl.BlockSpec((rows, HEAD_SIZE), lambda h: (0, h))
    return pl.pallas_call(
        kernel,
        grid=(heads,),
        in_specs=[
            by_head,
            by_head,
            fixed(lse.shape),
            fixed(cosine.shape),
            fixed(sine.shape),
            fixed(key_place.shape),
            fixed(bounds.shape),
        ]
        + [fixed(p.shape) for p in key_value],
        out_specs=[by_head] + [fixed(p.shape) for p in key_value],
        out_shape=[jax.ShapeDtypeStruct((rows, heads * HEAD_SIZE), BF16)]
        + [
            jax.ShapeDtypeStruct(p.shape, F32 if i == 0 else BF16)
            for i, p in enumerate(key_value)
        ],
        scratch_shapes=[
            pltpu.VMEM((n_keys, HEAD_SIZE), BF16),
            pltpu.VMEM((n_keys, HEAD_SIZE), BF16),
            pltpu.VMEM((n_keys, rows), F32),
            pltpu.VMEM((n_keys, HEAD_SIZE), F32),
            pltpu.VMEM((n_keys, HEAD_SIZE), F32),
        ],
        compiler_params=kernel_params(),
        cost_estimate=SMALL,
        name="attention_backward",
    )(query, head_gradient, lse, cosine, sine, key_place, bounds, *key_value)


def expert_step(scalars, chunk, cot, gate_up, down, router, index, n_steps, buffers):
    rows, width = chunk[0].shape
    units = down.shape[0]
    n_chunk = len(chunk)
    n_rows = n_chunk * rows
    half_lanes = LANES // 2
    places = [slice(i * rows, (i + 1) * rows) for i in range(n_chunk)]

    def kernel(scalar_ref, router_ref, *refs):
        chunk_refs, cot_refs = refs[:n_chunk], refs[n_chunk : 2 * n_chunk]
        gate_up_ref, down_ref = refs[2 * n_chunk : 2 * n_chunk + 2]
        refs = refs[2 * n_chunk + 2 + len(buffers) :]
        part_outs, buffer_outs = refs[:n_chunk], refs[n_chunk : n_chunk + 5]
        row, cots, gate_w, up_w, down_w, part, gated, grad_gates, grad_ups, in_sems, out_sems = refs[
            n_chunk + 5 :
        ]
        loads, stores = [], []

        def load(source, target):
            copy = pltpu.make_async_copy(source, target, in_sems.at[len(loads)])
            copy.start()
            loads.append(copy)

        def store(source, target):
            copy = pltpu.make_async_copy(source, target, out_sems.at[len(stores)])
            copy.start()
            stores.append(copy)

        for ref, at in zip(chunk_refs, places):
            load(ref, row.at[at])
        load(gate_up_ref.at[:, :units], gate_w)
        load(gate_up_ref.at[:, units:], up_w)
        for ref, at in zip(cot_refs, places):
            load(ref.at[scalar_ref[1]], cots.at[at])
        load(down_ref, down_w)
        in_buffer = [slice(index * n_rows + at.start, index * n_rows + at.stop) for at in places]

        for copy in loads[: n_chunk + 1]:
            copy.wait()
        store(row, buffer_outs[0].at[index * n_rows : (index + 1) * n_rows])
        gates = [jnp.dot(row[at, :], gate_w[...], preferred_element_type=F32) for at in places]
        loads[n_chunk + 1].wait()
        ups = [jnp.dot(row[at, :], up_w[...], preferred_element_type=F32) for at in places]
        for copy in loads[n_chunk + 2 :]:
            copy.wait()
        store(cots.at[:, :width], buffer_outs[1].at[index * n_rows : (index + 1) * n_rows])

        lane = lax.broadcasted_iota(jnp.int32, (rows, LANES), 1)
        for at, gate, up, out, buffer_at in zip(places, gates, ups, part_outs, in_buffer):
            logits = jnp.dot(row[at, :], router_ref[...], preferred_element_type=F32)
            logits = jnp.where(cots[at, width:].astype(F32) > 0, logits, -jnp.inf)
            top = jnp.max(logits, axis=1, keepdims=True)
            weights = jnp.exp(logits - top)
            total = jnp.sum(weights, axis=1, keepdims=True)
            own = jnp.where(lane == scalar_ref[0] + ROUTER_LANE, weights, 0.0)
            weight = jnp.sum(own, axis=1, keepdims=True) / total

            grad_act = contract(cots[at, :width], down_w[...], 1, 1)
            square = gate * gate
            curve = jnp.tanh(GELU_ROOT * gate * (1.0 + GELU_CUBE * square))
            lifted = 0.5 + 0.5 * curve
            gelu = gate * lifted
            slope = lifted + (0.5 * GELU_ROOT) * gate * (1.0 - curve * curve) * (
                1.0 + (3.0 * GELU_CUBE) * square
            )
            act = gelu * up
            share = jnp.sum(act * grad_act, axis=1, keepdims=True)
            gated[at, :] = (act * weight).astype(BF16)
            grad_act = grad_act * weight
            grad_up = (grad_act * gelu).astype(BF16)
            grad_gate = (grad_act * up * slope).astype(BF16)
            grad_gates[at, :] = grad_gate
            grad_ups[at, :] = grad_up
            for source, target in zip((gated, grad_gates, grad_ups), buffer_outs[2:]):
                store(source.at[at], target.at[buffer_at])
            grad_row = contract(grad_gate, gate_w[...], 1, 1) + contract(grad_up, up_w[...], 1, 1)
            part[at, :width] = grad_row.astype(BF16)
            high = share.astype(BF16).astype(F32)
            part[at, width:] = jnp.where(
                lane == scalar_ref[0],
                high,
                jnp.where(lane == scalar_ref[0] + half_lanes, share - high, 0.0),
            ).astype(BF16)
            store(part.at[at], out)
        for copy in stores:
            copy.wait()

    anywhere = pl.BlockSpec(memory_space=pl.ANY)
    first_buffer = 2 + 2 * n_chunk + 2
    outs = pl.pallas_call(
        kernel,
        in_specs=[pl.BlockSpec(memory_space=pltpu.SMEM), pl.BlockSpec(memory_space=pltpu.VMEM)]
        + [anywhere] * (2 * n_chunk + 2 + len(buffers)),
        out_specs=[anywhere] * (n_chunk + 5),
        out_shape=[jax.ShapeDtypeStruct((rows, width + LANES), BF16)] * n_chunk
        + [jax.ShapeDtypeStruct((n_steps * n_rows, width), BF16)] * 2
        + [jax.ShapeDtypeStruct((n_steps * n_rows, units), BF16)] * 3,
        input_output_aliases={first_buffer + i: n_chunk + i for i in range(len(buffers))},
        scratch_shapes=[
            pltpu.VMEM((n_rows, width), BF16),
            pltpu.VMEM((n_rows, width + LANES), BF16),
            pltpu.VMEM((width, units), BF16),
            pltpu.VMEM((width, units), BF16),
            pltpu.VMEM((units, width), BF16),
            pltpu.VMEM((n_rows, width + LANES), BF16),
        ]
        + [pltpu.VMEM((n_rows, units), BF16)] * 3
        + [
            pltpu.SemaphoreType.DMA((2 * n_chunk + 3,)),
            pltpu.SemaphoreType.DMA((4 * n_chunk + 2,)),
        ],
        compiler_params=pltpu.CompilerParams(vmem_limit_bytes=56 * 1024 * 1024),
        cost_estimate=SMALL,
        name="expert_step",
    )(scalars, router, *chunk, *cot, gate_up, down, *buffers)
    return outs[:n_chunk], outs[n_chunk:]


def gate_up_grads(rows, grad_gate, grad_up):
    n_rows, width = rows.shape
    units = grad_gate.shape[1]
    tile = 256

    def kernel(rows_ref, gate_ref, up_ref, gate_out, up_out):
        for right, out in ((gate_ref, gate_out), (up_ref, up_out)):
            out[...] = contract(rows_ref[...], right[...], 0, 0).astype(BF16)

    whole = pl.BlockSpec((n_rows, units), lambda j: (0, 0))
    out = pl.BlockSpec((tile, units), lambda j: (j, 0))
    return pl.pallas_call(
        kernel,
        grid=(width // tile,),
        in_specs=[pl.BlockSpec((n_rows, tile), lambda j: (0, j)), whole, whole],
        out_specs=[out, out],
        out_shape=[jax.ShapeDtypeStruct((width, units), BF16)] * 2,
        compiler_params=kernel_params(),
        cost_estimate=SMALL,
        name="gate_up_grads",
    )(rows, grad_gate, grad_up)


def expert_weight_grads(gate_grad, up_grad, cot, gated):
    n_rows, width = cot.shape
    units = gated.shape[1]
    half = width // 2
    nx, ny = axis_len("dp"), axis_len("y")
    n_blocks = nx * ny
    gu_rows, down_rows = width // n_blocks, units // n_blocks
    n_out = 2 * n_blocks
    block_shape = (gu_rows + down_rows, half)
    chunk, tile = n_rows // 4, 256

    def kernel(place_ref, gate_ref, up_ref, cot_ref, gated_ref, *refs):
        outs, down_sum = refs[:n_out], refs[n_out]
        step = pl.program_id(0)

        @pl.when(step == 0)
        def _():
            down_sum[...] = jnp.zeros_like(down_sum)

        for at in range(0, width, tile):
            down_sum[:, at : at + tile] += contract(gated_ref[...], cot_ref[:, at : at + tile], 0, 0)

        def store(out, grad_ref, at, columns):
            out[:gu_rows, :] = grad_ref[at * gu_rows : (at + 1) * gu_rows, :]
            down = down_sum[at * down_rows : (at + 1) * down_rows, columns]
            out[gu_rows:, :] = down.astype(BF16)

        @pl.when(step == 3)
        def _():
            for at in range(n_blocks):
                x_step, y_step = step_to(place_ref, at)
                for s in range(nx):
                    for t in range(ny):

                        @pl.when((x_step == s) & (y_step == t))
                        def _(at=at, s=s, t=t):
                            store(outs[s * ny + t], gate_ref, at, slice(0, half))
                            store(outs[n_blocks + t * nx + s], up_ref, at, slice(half, width))

    def by_chunk(columns):
        return pl.BlockSpec((chunk, columns), lambda j, place: (j, 0))

    whole = pl.BlockSpec((width, units), lambda j, place: (0, 0))
    outs = pl.pallas_call(
        kernel,
        grid_spec=pltpu.PrefetchScalarGridSpec(
            num_scalar_prefetch=1,
            grid=(4,),
            in_specs=[whole, whole, by_chunk(width), by_chunk(units)],
            out_specs=[pl.BlockSpec(block_shape, lambda j, place: (0, 0))] * n_out,
            scratch_shapes=[pltpu.VMEM((units, width), F32)],
        ),
        out_shape=[jax.ShapeDtypeStruct(block_shape, BF16)] * n_out,
        compiler_params=kernel_params(),
        cost_estimate=SMALL,
        name="expert_weight_grads",
    )(plane_places(), gate_grad, up_grad, cot, gated)
    return [
        [outs[s * ny : (s + 1) * ny] for s in range(nx)],
        [outs[n_blocks + t * nx : n_blocks + (t + 1) * nx] for t in range(ny)],
    ]


def expert_results(gated, down):
    n_rows, units = gated.shape
    width = down.shape[1]
    half = n_rows // 8

    def kernel(gated_ref, down_ref, own_ref, other_ref):
        for i, out in enumerate((own_ref, other_ref)):
            rows = gated_ref[i * half : (i + 1) * half, :]
            out[...] = jnp.dot(rows, down_ref[...], preferred_element_type=F32).astype(BF16)

    out = pl.BlockSpec((half, width), lambda j: (2 * (1 - j % 2) + j // 2, 0))
    return pl.pallas_call(
        kernel,
        grid=(4,),
        in_specs=[
            pl.BlockSpec((2 * half, units), lambda j: (j, 0)),
            pl.BlockSpec(down.shape, lambda j: (0, 0)),
        ],
        out_specs=[out, out],
        out_shape=[jax.ShapeDtypeStruct((4 * half, width), BF16)] * 2,
        compiler_params=kernel_params(),
        cost_estimate=SMALL,
        name="expert_results",
    )(gated, down)


def branch_backward(grads, mixed, weight):
    rows, columns = mixed.shape
    width = weight.shape[0]
    half, chip_half = columns // 2, rows // 2
    block_rows = width // (axis_len("dp") * axis_len("y"))
    shapes = half_shapes([(block_rows, half)] * 2)
    n_out = len(shapes)
    together = width // block_rows
    tile = together * block_rows
    n_tiles = width // tile

    def kernel(place_ref, own_ref, other_ref, mixed_ref, weight_ref, *refs):
        out_ref, outs, total_ref = refs[0], refs[1 : 1 + n_out], refs[1 + n_out]
        at = pl.program_id(0)
        both = jnp.concatenate([own_ref[...], other_ref[...]], axis=0)
        part = jnp.dot(both, weight_ref[...], preferred_element_type=F32)

        @pl.when(at == 0)
        def _():
            total_ref[...] = part

        @pl.when(at > 0)
        def _():
            total_ref[...] += part

        product = contract(both, mixed_ref[...], 0, 0).astype(BF16)
        for i in range(together):
            block = product[i * block_rows : (i + 1) * block_rows]

            def first(out, block=block):
                out[...] = block[:, :half]

            def second(out, block=block):
                out[...] = block[:, half:]

            store_blocks(place_ref, at * together + i, outs, first, second)

        @pl.when(at == n_tiles - 1)
        def _():
            out_ref[...] = total_ref[...].astype(BF16)

    def fixed(shape):
        return pl.BlockSpec(shape, lambda j, place: (0,) * len(shape))

    by_columns = pl.BlockSpec((chip_half, tile), lambda j, place: (0, j))
    outs = pl.pallas_call(
        kernel,
        grid_spec=pltpu.PrefetchScalarGridSpec(
            num_scalar_prefetch=1,
            grid=(n_tiles,),
            in_specs=[
                by_columns,
                by_columns,
                fixed(mixed.shape),
                pl.BlockSpec((tile, columns), lambda j, place: (j, 0)),
            ],
            out_specs=[fixed(mixed.shape)] + [fixed(shape) for shape in shapes],
            scratch_shapes=[pltpu.VMEM((rows, columns), F32)],
        ),
        out_shape=[jax.ShapeDtypeStruct((rows, columns), BF16)]
        + [jax.ShapeDtypeStruct(shape, BF16) for shape in shapes],
        compiler_params=kernel_params(),
        cost_estimate=SMALL,
        name="branch_backward",
    )(plane_places(), *grads, mixed, weight)
    return outs[0], two_halves(outs[1:])


def projection_backward(
    normed, units, weight, grad_query, grad_key_value, split, extra_rows, extra_columns
):
    rows, width = normed.shape
    own_query = grad_query.shape[1]
    columns = own_query + grad_key_value.shape[1]
    half = rows // 2
    block_rows = width // (axis_len("dp") * axis_len("y"))
    shapes = half_shapes([(block_rows, split), (block_rows, columns - split + LANES)])
    together = blocks_a_step(block_rows)
    tile = together * block_rows

    def kernel(
        place_ref, normed_ref, unit_ref, other_unit_ref, weight_ref, query_ref, key_value_ref, *refs
    ):
        extra_refs, column_ref = refs[: len(extra_rows)], refs[len(extra_rows)]
        own_ref, other_ref = refs[len(extra_rows) + 1 : len(extra_rows) + 3]
        outs = refs[len(extra_rows) + 3 :]
        at = pl.program_id(0)
        part = contract(query_ref[...], weight_ref[:, :own_query], 1, 1) + contract(
            key_value_ref[...], weight_ref[:, own_query:], 1, 1
        )
        own_ref[...] = part[:half]
        other_ref[...] = part[half:].astype(BF16)
        both_units = jnp.concatenate([unit_ref[...], other_unit_ref[...]], axis=0)
        terms = (part * both_units.astype(F32)).astype(BF16)
        first = (lax.broadcasted_iota(jnp.int32, (rows, LANES), 1) == 0).astype(F32).astype(BF16)
        extra = contract(terms, first, 0, 0)
        row = 0
        for extra_ref in extra_refs:
            n = extra_ref.shape[0]
            extra += contract(extra_ref[...], column_ref[row : row + n, :], 0, 0)
            row += n
        by_query = contract(normed_ref[...], query_ref[...], 0, 0).astype(BF16)
        by_key_value = contract(normed_ref[...], key_value_ref[...], 0, 0).astype(BF16)
        extra = extra.astype(BF16)
        for i in range(together):
            these = slice(i * block_rows, (i + 1) * block_rows)

            def first(out, these=these):
                out[...] = by_query[these, :split]

            def second(out, these=these):
                out[:, : own_query - split] = by_query[these, split:]
                out[:, own_query - split : columns - split] = by_key_value[these]
                out[:, columns - split :] = extra[these]

            store_blocks(place_ref, at * together + i, outs, first, second)

    def fixed(shape):
        return pl.BlockSpec(shape, lambda j, place: (0,) * len(shape))

    def by_columns(n):
        return pl.BlockSpec((n, tile), lambda j, place: (0, j))

    outs = pl.pallas_call(
        kernel,
        grid_spec=pltpu.PrefetchScalarGridSpec(
            num_scalar_prefetch=1,
            grid=(width // tile,),
            in_specs=[
                by_columns(rows),
                by_columns(half),
                by_columns(half),
                pl.BlockSpec((tile, columns), lambda j, place: (j, 0)),
                fixed(grad_query.shape),
                fixed(grad_key_value.shape),
            ]
            + [by_columns(r.shape[0]) for r in extra_rows]
            + [fixed(extra_columns.shape)],
            out_specs=[by_columns(half), by_columns(half)] + [fixed(shape) for shape in shapes],
        ),
        out_shape=[
            jax.ShapeDtypeStruct((half, width), F32),
            jax.ShapeDtypeStruct((half, width), BF16),
        ]
        + [jax.ShapeDtypeStruct(shape, BF16) for shape in shapes],
        compiler_params=kernel_params(),
        cost_estimate=SMALL,
        name="projection_backward",
    )(
        plane_places(),
        normed,
        *units,
        weight,
        grad_query,
        grad_key_value,
        *extra_rows,
        extra_columns,
    )
    return (
        outs[0],
        outs[1],
        two_halves(outs[2:]),
    )


def middle_backward(backs, gates, middle, gain, router, grad_out):
    rows, width = middle.shape
    half_lanes = LANES // 2
    arrays = jax.tree.leaves(backs)
    n_backs = len(arrays)
    sizes = [len(jax.tree.leaves(back)) for back in backs]

    def kernel(*refs):
        gate_ref, middle_ref, gain_ref, router_ref, out_ref = refs[n_backs : n_backs + 5]
        grad_ref, rounded_ref, terms_ref, logits_ref = refs[n_backs + 5 :]
        came, at = 0.0, 0
        for n in sizes:
            pieces = [r[...].astype(F32) for r in refs[at : at + n]]
            came = came + (jnp.concatenate(pieces, axis=0) if n > 1 else pieces[0])
            at += n
        shares = came[:, width:]
        lane = lax.broadcasted_iota(jnp.int32, (rows, LANES), 1)
        shares = shares + pltpu.roll(shares, half_lanes, 1)
        shares = jnp.where(lane < half_lanes, shares, 0.0)
        shares = pltpu.roll(shares, ROUTER_LANE, 1)
        gate = gate_ref[...]
        mean = jnp.sum(gate * shares, axis=1, keepdims=True)
        logits = (gate * (shares - mean)).astype(BF16)
        logits_ref[...] = logits
        grad = came[:, :width] + contract(logits, router_ref[...], 1, 1)
        value = middle_ref[...]
        root = lax.rsqrt(jnp.mean(value * value, axis=-1, keepdims=True) + EPS)
        unit = value * root
        scaled = grad * gain_ref[...]
        along_unit = jnp.mean(scaled * unit, axis=-1, keepdims=True)
        total = out_ref[...] + root * (scaled - unit * along_unit)
        grad_ref[...] = total
        rounded_ref[...] = total.astype(BF16)
        terms_ref[...] = (grad * unit).astype(BF16)

    vmem = pl.BlockSpec(memory_space=pltpu.VMEM)
    return pl.pallas_call(
        kernel,
        in_specs=[vmem] * (n_backs + 5),
        out_specs=[vmem] * 4,
        out_shape=[
            jax.ShapeDtypeStruct((rows, width), F32),
            jax.ShapeDtypeStruct((rows, width), BF16),
            jax.ShapeDtypeStruct((rows, width), BF16),
            jax.ShapeDtypeStruct((rows, LANES), BF16),
        ],
        compiler_params=pltpu.CompilerParams(vmem_limit_bytes=48 * 1024 * 1024),
        cost_estimate=SMALL,
        name="middle_backward",
    )(*arrays, gates, middle, gain, router, grad_out)


def middle_forward(hidden, own, other, gain):
    rows, width = hidden.shape

    def kernel(hidden_ref, own_ref, other_ref, gain_ref, middle_ref, inner_ref):
        middle = hidden_ref[...] + own_ref[...] + other_ref[...].astype(F32)
        middle_ref[...] = middle
        root = lax.rsqrt(jnp.mean(middle * middle, axis=-1, keepdims=True) + EPS)
        inner_ref[...] = (middle * root * gain_ref[...]).astype(BF16)

    block = pl.BlockSpec((rows, width), lambda j: (0, 0))
    return pl.pallas_call(
        kernel,
        grid=(1,),
        in_specs=[block, block, block, pl.BlockSpec((1, width), lambda j: (0, 0))],
        out_specs=[block, block],
        out_shape=[
            jax.ShapeDtypeStruct((rows, width), F32),
            jax.ShapeDtypeStruct((rows, width), BF16),
        ],
        compiler_params=kernel_params(),
        cost_estimate=SMALL,
        name="middle_forward",
    )(hidden, own, other, gain)


def expert_sums(core, halves, gu_shard, down_shard):
    block_rows, half = halves[0][0].shape
    counts = [len(blocks) for blocks in halves]
    kept = gu_shard + down_shard

    def kernel(core_ref, *refs):
        mine_ref, other_ref, total = refs[sum(counts) :]
        at = 0
        for i, n in enumerate(counts):
            columns = slice(i * half, (i + 1) * half)
            total[:, columns] = sum(r[...].astype(F32) for r in refs[at : at + n])
            at += n
        core = core_ref[0]
        for which, out in ((core, mine_ref), (1 - core, other_ref)):
            gu = pl.ds(pl.multiple_of(which * gu_shard, 8), gu_shard)
            down = pl.ds(pl.multiple_of(CORES * gu_shard + which * down_shard, 8), down_shard)
            out[:gu_shard, :] = total[gu, :].astype(out.dtype)
            out[gu_shard:, :] = total[down, :].astype(out.dtype)

    vmem = pl.BlockSpec(memory_space=pltpu.VMEM)
    return pl.pallas_call(
        kernel,
        in_specs=[pl.BlockSpec(memory_space=pltpu.SMEM)] + [vmem] * sum(counts),
        out_specs=[vmem, vmem],
        out_shape=[
            jax.ShapeDtypeStruct((kept, 2 * half), F32),
            jax.ShapeDtypeStruct((kept, 2 * half), BF16),
        ],
        scratch_shapes=[pltpu.VMEM((block_rows, 2 * half), F32)],
        compiler_params=pltpu.CompilerParams(vmem_limit_bytes=48 * 1024 * 1024),
        cost_estimate=SMALL,
        name="expert_sums",
    )(core.astype(jnp.int32).reshape(1), *halves[0], *halves[1])


def expert_shards(core, mine, received, gu_shard, down_shard):
    width = mine.shape[1]

    def kernel(core_ref, mine_ref, received_ref, gu_ref, down_ref):
        core = core_ref[0]
        for which, rows in ((core, mine_ref), (1 - core, received_ref)):
            gu_ref[which] = rows[:gu_shard, :].astype(F32)
            down_ref[which] = rows[gu_shard:, :].astype(F32)

    vmem = pl.BlockSpec(memory_space=pltpu.VMEM)
    return pl.pallas_call(
        kernel,
        in_specs=[pl.BlockSpec(memory_space=pltpu.SMEM), vmem, vmem],
        out_specs=[vmem, vmem],
        out_shape=[
            jax.ShapeDtypeStruct((CORES, gu_shard, width), F32),
            jax.ShapeDtypeStruct((CORES, down_shard, width), F32),
        ],
        compiler_params=pltpu.CompilerParams(vmem_limit_bytes=48 * 1024 * 1024),
        cost_estimate=SMALL,
        name="expert_shards",
    )(core.astype(jnp.int32).reshape(1), mine, received)


def projection_shards(core, summed, received, columns):
    own_query, whole = columns
    rows = summed.shape[1]
    own_width = own_query + 2 * HEAD_SIZE
    key_at = KEY_VALUE_HEADS * own_query
    value_at = key_at + KEY_VALUE_HEADS * HEAD_SIZE

    def kernel(core_ref, summed_ref, received_ref, out_ref, extra_ref):
        core = core_ref[0]
        mine, other = summed_ref[core], received_ref[...].astype(F32)
        for which, part in ((core, mine), (1 - core, other)):
            for start, size, at in (
                (0, own_query, 0),
                (key_at, HEAD_SIZE, own_query),
                (value_at, HEAD_SIZE, own_query + HEAD_SIZE),
            ):
                target = pl.ds(pl.multiple_of(start + which * size, LANES), size)
                out_ref[:, target] = part[:, at : at + size]
        extra_ref[...] = mine[:, own_width:] + other[:, own_width:]

    vmem = pl.BlockSpec(memory_space=pltpu.VMEM)
    return pl.pallas_call(
        kernel,
        in_specs=[pl.BlockSpec(memory_space=pltpu.SMEM), vmem, vmem],
        out_specs=[vmem, vmem],
        out_shape=[
            jax.ShapeDtypeStruct((rows, whole), F32),
            jax.ShapeDtypeStruct((rows, LANES), F32),
        ],
        cost_estimate=SMALL,
        name="projection_shards",
    )(core.astype(jnp.int32).reshape(1), summed, received)


def on_device(
    hidden_in,
    lengths,
    order,
    routes,
    cotangent,
    attn_gain,
    qkv_weight,
    out_weight,
    ffn_gain,
    router_weight,
    gate_up_weight,
    down_weight,
):
    hidden = hidden_in[0]
    grad_out = cotangent[0]
    rows, width = hidden.shape
    n_experts = router_weight.shape[1]
    nx, ny, nz = axis_len("dp"), axis_len("y"), axis_len("exp")
    core = lax.axis_index("ctx") % CORES
    other_core = 1 - core
    shard = qkv_weight.shape[0]
    chip_rows = CORES * rows
    query_width = QUERY_HEADS * HEAD_SIZE
    heads = QUERY_HEADS // KEY_VALUE_HEADS
    own_query = heads * HEAD_SIZE
    own_width = own_query + 2 * HEAD_SIZE
    hidden_units = gate_up_weight.shape[2] // 2
    scale = HEAD_SIZE ** (-0.5)

    extra = jnp.concatenate([attn_gain[:, None], ffn_gain[:, None], router_weight], axis=1)
    extra = jnp.pad(extra, ((0, 0), (0, LANES - extra.shape[1])))
    split = 5 * HEAD_SIZE

    def gather_z(pair, *waits):
        blocks = line_gather(pair.reshape(CORES * shard, -1), nz, *waits)
        place = lax.axis_index("exp")
        whole = jnp.zeros((CORES, nz, shard, pair.shape[2]), BF16)
        for step, block in enumerate(blocks):
            at = jnp.bitwise_xor(place, step)
            whole = lax.dynamic_update_slice_in_dim(
                whole, block.reshape(CORES, 1, shard, -1), at, 1
            )
        return whole.reshape(CORES * nz * shard, -1)

    weights = jnp.concatenate([qkv_weight, extra, out_weight.T], axis=1)
    weights = in_core_order(weights, core_swap(weights))
    key_at = query_width + core * HEAD_SIZE
    value_at = key_at + KEY_VALUE_HEADS * HEAD_SIZE
    extra_at = qkv_weight.shape[1]
    out_at = extra_at + LANES + core * own_query
    weights = jnp.concatenate(
        [
            lax.dynamic_slice_in_dim(weights, core * own_query, own_query, 2),
            lax.dynamic_slice_in_dim(weights, key_at, HEAD_SIZE, 2),
            lax.dynamic_slice_in_dim(weights, value_at, HEAD_SIZE, 2),
            weights[:, :, extra_at : extra_at + LANES],
            lax.dynamic_slice_in_dim(weights, out_at, own_query, 2),
        ],
        axis=2,
    )
    def expert_rows(which):
        return (
            lax.dynamic_index_in_dim(gate_up_weight, which, 0, keepdims=False),
            lax.dynamic_index_in_dim(down_weight, which, 0, keepdims=False),
        )

    gu_mine, down_mine = expert_rows(core)
    gu_shard, down_shard = gu_mine.shape[0], down_mine.shape[0]
    received = core_swap(after(jnp.concatenate(expert_rows(other_core), axis=0), weights))
    gu_pair = in_core_order(gu_mine, received[:gu_shard]).reshape(CORES * gu_shard, -1)
    down_pair = in_core_order(down_mine, received[gu_shard:]).reshape(CORES * down_shard, -1)
    half_width = width // 2
    expert_halves = (
        jnp.concatenate([gu_pair[:, :hidden_units], down_pair[:, :half_width]], axis=0),
        jnp.concatenate([gu_pair[:, hidden_units:], down_pair[:, half_width:]], axis=0),
    )
    expert_first = plane_first(*expert_halves)

    weights_z = after(gather_z(weights), expert_first)
    block_rows = CORES * nz * shard
    half_query = own_query // 2
    group = 4 if nz % 4 == 0 else nz
    phased = group == nz
    qkv_z, out_z = weights_z[:, : own_width + LANES], weights_z[:, own_width + LANES :]
    qkv_halves = (qkv_z[:, :split], qkv_z[:, split:])
    out_halves = (out_z[:, :half_query], out_z[:, half_query:])

    expert_ids = jnp.arange(n_experts, dtype=jnp.int32)
    used = jnp.any(routes[0][:, :, None] == expert_ids[None, None, :], axis=1)
    marks = jnp.pad(
        used.astype(BF16), ((0, 0), (ROUTER_LANE, LANES - ROUTER_LANE - n_experts))
    )
    cot_rows = jnp.concatenate([grad_out.astype(BF16), marks], axis=1)
    cot_all = lax.all_gather(after(cot_rows, weights_z), "exp", axis=0, tiled=False)

    units = unit_rows(hidden, weights_z)
    units_other = core_swap(units)
    qkv_first, qkv_second = plane_first(*qkv_halves), plane_second(*qkv_halves)
    qkv_first, qkv_second, out_halves = after((qkv_first, qkv_second, out_halves), units_other)
    qkv_third = plane_third(qkv_first)
    w_all, extra_all = place_blocks(
        qkv_halves,
        (qkv_first, qkv_second, qkv_third),
        ((0, block_rows, 0, own_width), (0, block_rows, own_width, LANES)),
    )
    out_halves = after(out_halves, w_all)
    out_first, out_second = plane_first(*out_halves), plane_second(*out_halves)
    gain_one = extra_all[:, 0].astype(F32)
    gain_two = extra_all[:, 1].astype(F32)
    lanes = jnp.arange(LANES)
    is_router = (lanes >= ROUTER_LANE) & (lanes < ROUTER_LANE + n_experts)
    router_all = jnp.where(is_router[None, :], extra_all, 0)

    normed = jnp.concatenate([units, units_other], axis=0)
    normed = (normed.astype(F32) * gain_one).astype(BF16)
    packed_all, all_lengths = after((order[0], lengths[0]), weights_z)
    starts_all = doc_starts(packed_all, all_lengths)

    def own_first(values):
        y_place, y_rows = axis_place("y"), chip_rows
        parts = []
        for t in range(ny):
            at = lax.rem(y_place - t + ny, ny) * y_rows
            for which in (core, other_core):
                parts.append(lax.dynamic_slice_in_dim(values, at + which * rows, rows, 0))
        return jnp.concatenate(parts, axis=0)

    packed_keys, starts = own_first(packed_all), own_first(starts_all)[:chip_rows]
    packed = packed_keys[:chip_rows]
    cosine, sine = rotation_tables(packed - starts)
    bounds = jnp.concatenate(
        [starts[None, :], packed[None, :], jnp.zeros((6, chip_rows), jnp.int32)], axis=0
    )
    key_place = packed_keys[:, None]
    projected = dot(normed, w_all)
    key_value = jnp.concatenate(
        [
            rotate(projected[:, own_query : own_query + HEAD_SIZE], cosine, sine),
            projected[:, own_query + HEAD_SIZE : own_width],
        ],
        axis=1,
    ).astype(BF16)
    key_value = [key_value] + [shifted(key_value, "y", t) for t in range(1, ny)]
    out_first, expert_halves, projected, cot_all = after(
        (out_first, expert_halves, projected, cot_all), key_value, out_second
    )
    out_third = plane_third(out_first)
    cot_other = core_swap(cot_all)
    expert_second = plane_second(*expert_halves)
    query_rows, mixed, lse = attention_forward(
        projected, key_value, cosine, sine, key_place, bounds, heads
    )
    mixed, expert_first = after((mixed, expert_first), out_third, cot_other)
    expert_third = plane_third(after(expert_first, expert_second))
    (out_turned,) = place_blocks(
        out_halves, (out_first, out_second, out_third), ((0, block_rows, 0, own_query),)
    )
    branch = dot_turned(mixed, out_turned)
    branch_other = core_swap(branch[rows:].astype(BF16))
    middle, inner = middle_forward(hidden, branch, branch_other, gain_two[None, :])
    gate_up_all, down_all = place_blocks(
        expert_halves,
        (expert_first, expert_second, expert_third),
        (
            (0, CORES * gu_shard, 0, 2 * hidden_units),
            (CORES * gu_shard, CORES * down_shard, 0, width),
        ),
    )

    logits = jnp.where(marks > 0, dot(inner, extra_all), -jnp.inf)
    gates = jax.nn.softmax(logits, axis=-1)
    place_z = lax.axis_index("exp")
    own_expert = place_z * CORES + core

    def expert_group(inner_rows, from_place):
        buffers = []

        def run(index, chunk):
            scalars = jnp.stack([own_expert, jnp.bitwise_xor(from_place, index)])
            (mine, other), filled = expert_step(
                scalars.astype(jnp.int32),
                chunk,
                [cot_all, cot_other],
                gate_up_all,
                down_all,
                extra_all,
                index,
                4,
                buffers,
            )
            buffers[:] = filled
            return mine, other

        def joined(mine, other):
            return (mine.astype(F32) + other.astype(F32)).astype(BF16)

        rows_1, rows_2 = xor_shift(inner_rows, 1), xor_shift(inner_rows, 2)
        mine_0, other_0 = run(0, [inner_rows, core_swap(inner_rows)])

        rows_1, rows_2 = after((rows_1, rows_2), other_0)
        rows_3 = xor_shift(rows_2, 1)
        swapped = [core_swap(rows_1), core_swap(rows_2)]
        rows_1, other_1_rows, other_2_rows = after((rows_1, *swapped))
        other_0 = core_swap(other_0)
        mine_1, other_1 = run(1, [rows_1, other_1_rows])

        rows_2, other_1, mine_1 = after((rows_2, other_1, mine_1), other_0)
        other_1 = core_swap(other_1)
        back_1 = joined(mine_1, other_1)
        rows_2, rows_3 = after((rows_2, rows_3), back_1)
        near = xor_shift(back_1, 1)
        other_3_rows = core_swap(rows_3)
        mine_2, other_2 = run(2, [rows_2, other_2_rows])

        rows_3, other_2 = after((rows_3, other_2), other_3_rows)
        other_2 = core_swap(other_2)
        mine_3, other_3 = run(3, [rows_3, other_3_rows])

        mine_3, other_3 = after((mine_3, other_3), other_2, near)
        back_3 = joined(mine_3, core_swap(other_3))
        handed = xor_shift(back_3, 1)
        all_rows, all_cots, gated_all, grad_gates, grad_ups = after(buffers, back_3)
        if phased:
            grad_gate, grad_up = gate_up_grads(all_rows, grad_gates, grad_ups)
            grad_gate, grad_up, handed = after((grad_gate, grad_up, handed))
        mine_0, mine_2 = after((mine_0, mine_2), back_3)
        back_2 = joined(mine_2, other_2)
        (pair,) = line_pairs([None, None, back_2, None], [handed])
        if phased:
            grad_gate, gated_all, pair = after((grad_gate, gated_all, pair), gates)
        pieces = [pair[: rows // 2], pair[rows // 2 :]]
        moved, received = xor_shift(pieces[0], 2), []
        if phased:
            weight_grads = expert_weight_grads(grad_gate, grad_up, all_cots, gated_all)
            weight_grads, gated_all, moved, pieces = after((weight_grads, gated_all, moved, pieces))
            received = plane_moved_part(weight_grads, True)
        else:
            weight_grads = (
                dot_rows(all_rows, grad_gates),
                dot_rows(all_rows, grad_ups),
                dot_rows(gated_all, all_cots),
            )
        moved_more = xor_shift(pieces[1], 2)
        back_0 = joined(mine_0, other_0)
        outs, outs_other = expert_results(gated_all, down_all)
        outs, outs_other, moved_more, received, weight_grads = after(
            (outs, outs_other, moved_more, received, weight_grads), back_0
        )
        if phased:
            received = plane_joined(plane_moved_part(weight_grads, False), received)
        outs_other = core_swap(outs_other)
        outs = [
            (outs[half].astype(F32) + outs_other[half].astype(F32)).astype(BF16)
            for half in (slice(0, 2 * rows), slice(2 * rows, 4 * rows))
        ]
        return (back_0, near, (moved, moved_more)), outs, weight_grads, received

    if phased:
        backs, outs, expert_grads, expert_received = expert_group(inner, place_z)
    else:

        def visit(turn, state):
            inner_here, back, out, sums = state
            more_back, outs, more, _ = expert_group(
                inner_here, lax.rem(place_z + turn * group, nz)
            )
            back = back + more_back[0].astype(F32) + more_back[1].astype(F32)
            back = back + jnp.concatenate(more_back[2], axis=0).astype(F32)
            odd, even = (o.reshape(2, rows, width) for o in outs)
            out = out + line_scatter([even[0], odd[0], even[1], odd[1]])[0]
            sums = tuple(a + b for a, b in zip(sums, more))
            return (*(shifted(v, "exp", nz - group) for v in (inner_here, back, out)), sums)

        sums = (
            jnp.zeros((width, hidden_units), F32),
            jnp.zeros((width, hidden_units), F32),
            jnp.zeros((hidden_units, width), F32),
        )
        start = (jnp.zeros((rows, width + LANES), F32), jnp.zeros((rows, width), F32), sums)
        _, back, moe, sums = lax.fori_loop(0, nz // group, visit, (inner, *start))
        backs = (back,)
        gate, up, down = (w.astype(BF16) for w in sums)
        gate, up = (w.reshape(nx, ny, CORES * gu_shard, hidden_units) for w in (gate, up))
        down = down.reshape(nx, ny, CORES * down_shard, width)
        expert_grads = [
            plane_blocks([gate, down[..., :half_width]], PLANE_AXES[0]),
            plane_blocks([up, down[..., half_width:]], PLANE_AXES[1]),
        ]
        expert_received = plane_joined(
            plane_moved_part(expert_grads, False), plane_moved_part(expert_grads, True)
        )

    if phased:
        results_handed = xor_shift(outs[0][rows:], 1)

    grad_middle, grad_branch, ffn_terms, grad_logits = middle_backward(
        backs, gates, middle, gain_two[None, :], router_all, grad_out
    )
    grad_branch = [grad_branch, core_swap(grad_branch)]
    blended_gradient, out_grads = branch_backward(grad_branch, mixed, out_turned)
    if phased:
        blended_gradient = after(blended_gradient, outs[0])
    grad_query, grad_kv_own, *grad_kv_parts = attention_backward(
        query_rows, blended_gradient, lse, key_value, cosine, sine, key_place, bounds, heads
    )

    if phased:
        grad_query, grad_kv_own, grad_kv_parts, results_handed = after(
            (grad_query, grad_kv_own, grad_kv_parts, results_handed)
        )
    grad_kv_parts = [shifted(part, "y", ny - t) for t, part in enumerate(grad_kv_parts, 1)]
    out_grads = after(out_grads, grad_kv_parts)
    out_received = plane_moved(out_grads)
    if phased:
        pair = (outs[1][rows:].astype(F32) + results_handed.astype(F32)).astype(BF16)
        cut = rows // 4
        moe_far = [xor_shift(pair[:cut], 2)]
        results_near = xor_shift(after(outs[0][:rows], pair), 1)

    for part in grad_kv_parts:
        grad_kv_own = grad_kv_own + part.astype(F32)
    grad_key_value = jnp.concatenate(
        [rotate(grad_kv_own[:, :HEAD_SIZE], cosine, -sine), grad_kv_own[:, HEAD_SIZE:]], axis=1
    ).astype(BF16)
    if phased:
        grad_key_value = after(grad_key_value, pair)
    is_ffn = (lax.broadcasted_iota(jnp.int32, (rows, LANES), 1) == 1).astype(BF16)
    grad_normed, grad_normed_other, qkv_grads = projection_backward(
        normed,
        [units, units_other],
        w_all,
        grad_query,
        grad_key_value,
        split,
        [ffn_terms, inner],
        jnp.concatenate([is_ffn, grad_logits], axis=0),
    )
    if phased:
        qkv_grads, moe_far, pair = after((qkv_grads, moe_far, pair))
        moe_far.append(xor_shift(pair[cut:], 2))
    qkv_grads, out_received = after((qkv_grads, out_received))

    def line_sum(first, second):
        summed = jnp.concatenate([first, second], axis=1).astype(BF16)
        summed = summed.reshape(CORES, nz, shard, -1)
        place = lax.axis_index("exp")
        return line_scatter(
            [
                lax.dynamic_index_in_dim(summed, jnp.bitwise_xor(place, step), 1, keepdims=False)
                for step in range(nz)
            ]
        )

    def of_core(value, which):
        return lax.dynamic_index_in_dim(value, which, 0, keepdims=False)

    qkv_received = plane_moved(qkv_grads)
    qkv_hand_on = plane_hand_on(qkv_grads, qkv_received)
    qkv_handed = plane_handed(qkv_hand_on)
    expert_received = after(expert_received, qkv_grads)
    expert_hand_on = plane_hand_on(expert_grads, expert_received)
    out_received = after(out_received, qkv_hand_on)
    out_handed = plane_handed(plane_hand_on(out_grads, out_received))
    if phased:
        moe_far, results_near = after((moe_far, results_near), qkv_hand_on)
        moe = outs[1][:rows].astype(F32) + results_near.astype(F32)
        moe = moe + jnp.concatenate(moe_far, axis=0).astype(F32)
    grad_normed_other = after(grad_normed_other, qkv_hand_on)
    grad_normed = grad_normed + core_swap(grad_normed_other).astype(F32)
    grad_hidden_norm, _ = norm_back(hidden, gain_one, grad_normed)
    grad_input = grad_middle + grad_hidden_norm
    output = middle + moe
    expert_handed = plane_handed(after(expert_hand_on, out_handed))
    qkv_sum, qkv_pairs = line_sum(*plane_sum(qkv_grads, qkv_received, qkv_handed))
    out_handed = after(out_handed, qkv_handed)
    out_sum, out_pairs = line_sum(*plane_sum(out_grads, out_received, out_handed))
    expert_handed = after(expert_handed, qkv_pairs, out_pairs)
    out_other = core_swap(of_core(out_sum, other_core).astype(BF16)).astype(F32)
    out_sum = in_core_order(of_core(out_sum, core), out_other)
    grad_out_proj = out_sum.swapaxes(0, 1).reshape(shard, query_width).T

    blocks = [
        [half[0][0], *(came[0] for came in received), *handed]
        for half, received, handed in zip(expert_grads, expert_received, expert_handed)
    ]
    mine, to_other = expert_sums(core, blocks, gu_shard, down_shard)
    grad_gate_up, grad_down = expert_shards(
        core, mine, core_swap(to_other), gu_shard, down_shard
    )
    qkv_other = core_swap(of_core(qkv_sum, other_core).astype(BF16))
    grad_qkv, extra_sum = projection_shards(
        core, qkv_sum, qkv_other, (own_query, qkv_weight.shape[1])
    )
    return (
        output[None],
        grad_input[None],
        extra_sum[:, 0],
        grad_qkv,
        grad_out_proj,
        extra_sum[:, 1],
        extra_sum[:, 2 : 2 + n_experts],
        grad_gate_up,
        grad_down,
    )


def solution(mesh):
    return jax.shard_map(
        on_device,
        mesh=mesh,
        in_specs=(
            P(("dp", "exp"), "ctx", None),
            P(("dp", "exp"), None),
            P(("dp", "exp"), None),
            P(("dp", "exp"), "ctx", None),
            P(("dp", "exp"), "ctx", None),
            P(("dp", "ctx", "exp")),
            P(("dp", "ctx", "exp"), None),
            P(None, ("dp", "ctx", "exp")),
            P(("dp", "ctx", "exp")),
            P(("dp", "ctx", "exp"), None),
            P("exp", ("dp", "ctx"), None),
            P("exp", ("dp", "ctx"), None),
        ),
        out_specs=(
            P(("dp", "exp"), "ctx", None),
            P(("dp", "exp"), "ctx", None),
            P(("dp", "ctx", "exp")),
            P(("dp", "ctx", "exp"), None),
            P(None, ("dp", "ctx", "exp")),
            P(("dp", "ctx", "exp")),
            P(("dp", "ctx", "exp"), None),
            P("exp", ("dp", "ctx"), None),
            P("exp", ("dp", "ctx"), None),
        ),
        check_vma=False,
    )
```
